32 devices in a mesh: patch: 8 (over z, y), rep: 4 (over x, core).
Axes of the slice: x: 2, y: 2, z: 4, core: 2. Of those that a mesh axis runs over, the one named last changes fastest.
Arguments:
- previous_state: float32 [4, 84, 24576], P('rep', None, 'patch'), may hold values from -6 to 6
- target_state: float32 [4, 84, 24576], P('rep', None, 'patch'), may hold values from -6 to 6
- noise_draws: float32 [4, 2, 84, 24576], P('rep', None, None, 'patch'), may hold values from -6 to 6
- noise_level: float32 [4, 2], P('rep'), may hold values from 0.3 to 3
- pixel_owner: int32 [4, 24576], P('rep', 'patch'), may hold values from 0 to 511, as said below
- mesh_to_grid: int32 [4, 3, 24576], P('rep', None, 'patch'), may hold values from 0 to 511, as said below
- neighbours: int32 [4, 4096, 16], P('rep', 'patch'), may hold values from 0 to 639, as said below
- halo_send: int32 [4, 1024], P('rep', 'patch'), may hold values from 0 to 511, as said below
- node_count: int32 [4, 8], P('rep', 'patch'), may hold values from 106 to 512, as said below
- pixel_count: int32 [4, 8], P('rep', 'patch'), may hold values from 640 to 3072, as said below
- w_encode: float32 [168, 512], P(None, ('patch', 'rep')), may hold values from -0.5 to 0.5
- w_project: float32 [512, 1536], P(('patch', 'rep')), may hold values from -0.25 to 0.25
- w_output: float32 [512, 512], P(('patch', 'rep')), may hold values from -0.5 to 0.5
- w_up: float32 [512, 2048], P(('patch', 'rep')), may hold values from -0.25 to 0.25
- w_down: float32 [2048, 512], P(('patch', 'rep')), may hold values from -0.125 to 0.125
- w_noise: float32 [32, 2048], P(None, ('patch', 'rep')), may hold values from -1 to 1
- w_decode: float32 [512, 84], P(('patch', 'rep')), may hold values from -0.25 to 0.25
- m_encode: float32 [168, 512], P(None, ('patch', 'rep')), may hold values from -0.00036621094 to 0.00036621094
- m_project: float32 [512, 1536], P(('patch', 'rep')), may hold values from -0.00036621094 to 0.00036621094
- m_output: float32 [512, 512], P(('patch', 'rep')), may hold values from -0.00036621094 to 0.00036621094
- m_up: float32 [512, 2048], P(('patch', 'rep')), may hold values from -0.00036621094 to 0.00036621094
- m_down: float32 [2048, 512], P(('patch', 'rep')), may hold values from -0.00036621094 to 0.00036621094
- m_noise: float32 [32, 2048], P(None, ('patch', 'rep')), may hold values from -0.00036621094 to 0.00036621094
- m_decode: float32 [512, 84], P(('patch', 'rep')), may hold values from -0.00036621094 to 0.00036621094
- v_encode: float32 [168, 512], P(None, ('patch', 'rep')), may hold values from 1.5747146e-08 to 6.286883e-08
- v_project: float32 [512, 1536], P(('patch', 'rep')), may hold values from 1.5747146e-08 to 6.286883e-08
- v_output: float32 [512, 512], P(('patch', 'rep')), may hold values from 1.5747146e-08 to 6.286883e-08
- v_up: float32 [512, 2048], P(('patch', 'rep')), may hold values from 1.5747146e-08 to 6.286883e-08
- v_down: float32 [2048, 512], P(('patch', 'rep')), may hold values from 1.5747146e-08 to 6.286883e-08
- v_noise: float32 [32, 2048], P(None, ('patch', 'rep')), may hold values from 1.5747146e-08 to 6.286883e-08
- v_decode: float32 [512, 84], P(('patch', 'rep')), may hold values from 1.5747146e-08 to 6.286883e-08
Outputs:
- new_encode: float32 [168, 512], P(None, ('patch', 'rep'))
- new_project: float32 [512, 1536], P(('patch', 'rep'))
- new_output: float32 [512, 512], P(('patch', 'rep'))
- new_up: float32 [512, 2048], P(('patch', 'rep'))
- new_down: float32 [2048, 512], P(('patch', 'rep'))
- new_noise: float32 [32, 2048], P(None, ('patch', 'rep'))
- new_decode: float32 [512, 84], P(('patch', 'rep'))
- moment_encode: float32 [168, 512], P(None, ('patch', 'rep'))
- moment_project: float32 [512, 1536], P(('patch', 'rep'))
- moment_output: float32 [512, 512], P(('patch', 'rep'))
- moment_up: float32 [512, 2048], P(('patch', 'rep'))
- moment_down: float32 [2048, 512], P(('patch', 'rep'))
- moment_noise: float32 [32, 2048], P(None, ('patch', 'rep'))
- moment_decode: float32 [512, 84], P(('patch', 'rep'))
- second_encode: float32 [168, 512], P(None, ('patch', 'rep'))
- second_project: float32 [512, 1536], P(('patch', 'rep'))
- second_output: float32 [512, 512], P(('patch', 'rep'))
- second_up: float32 [512, 2048], P(('patch', 'rep'))
- second_down: float32 [2048, 512], P(('patch', 'rep'))
- second_noise: float32 [32, 2048], P(None, ('patch', 'rep'))
- second_decode: float32 [512, 84], P(('patch', 'rep'))
- loss_sum: float32 [], replicated
- count_total: float32 [], replicated
- grad_norm: float32 [], replicated
The draws below stay inside these ranges and needn't reach their ends.
Inputs may be any that keep to these rules, and one draw needn't show every extreme that they name: `pixel_owner`: names only live nodes of the pixel's patch. `mesh_to_grid`: names only live nodes of the pixel's patch. `neighbours`: entry 0 of each node's list is the node itself; entries of 512 or more name halo rows (lower patch's first). `halo_send`: only live nodes of the sending patch are named. `node_count`: the last patch of every sample is full. `pixel_count`: the last patch of every sample is full.
All inputs are finite; a program needn't handle non-finite values.
Results may differ from the reference program's by a relative error of at most 0.011.
Values may be sent and summed in bfloat16 or wider, within the bound.
A program may use at most 256 MiB of HBM per device.

```python
import math
import jax
import jax.numpy as jnp
from jax import lax

D = 512
HEADS = 4
HD = 128
FF = 2048
CH = 84
FOUR = 32
NEIGH = 16
STEP = 5
NODE_DEV = 512
PIX_DEV = 3072
HALO = 64
SAMPLES = 4
NODES = 4096
PIXELS = 24576
PARAMS = 3340288
N_PATCH = 8


def counts_pair(key):
    first, second = jax.random.split(key)
    place = jnp.arange(N_PATCH)
    last_one = place == N_PATCH - 1
    base_nodes = NODE_DEV // 3 + (NODE_DEV - NODE_DEV // 3) * place // (N_PATCH - 1)
    base_pixels = PIX_DEV // 3 + (PIX_DEV - PIX_DEV // 3) * place // (N_PATCH - 1)
    node_jitter = jax.random.randint(first, (SAMPLES, N_PATCH), 0, NODE_DEV // 8 + 1)
    pixel_jitter = jax.random.randint(second, (SAMPLES, N_PATCH), 0, PIX_DEV // 8 + 1)
    nodes_out = jnp.where(last_one[None, :], NODE_DEV, base_nodes[None, :] - node_jitter)
    pixels_out = jnp.where(last_one[None, :], PIX_DEV, base_pixels[None, :] - pixel_jitter)
    return (nodes_out.astype(jnp.int32), pixels_out.astype(jnp.int32))


def pixel_bounds(key):
    nodes_out = counts_pair(key)[0]
    return jnp.repeat(nodes_out, PIX_DEV, axis=1)


def plant_ends(picks):
    place = jnp.arange(PIXELS)
    picks = jnp.where(place == PIXELS - PIX_DEV, NODE_DEV - 1, picks)
    return jnp.where(place == PIXELS - PIX_DEV + 1, 0, picks)


def draw_node_count(key, part):
    return counts_pair(key)[0]


def draw_pixel_count(key, part):
    return counts_pair(key)[1]


def draw_pixel_owner(key, part):
    bounds = pixel_bounds(key)
    key = jax.random.fold_in(key, 7)
    picks = jax.random.randint(key, (SAMPLES, PIXELS), 0, bounds)
    return plant_ends(picks).astype(jnp.int32)


def draw_mesh_to_grid(key, part):
    bounds = pixel_bounds(key)
    key = jax.random.fold_in(key, 9)
    picks = jax.random.randint(key, (SAMPLES, 3, PIXELS), 0, bounds[:, None, :])
    return plant_ends(picks).astype(jnp.int32)


def draw_halo_send(key, part):
    nodes_out = counts_pair(key)[0]
    key = jax.random.fold_in(key, 5)
    picks = jax.random.randint(key, (SAMPLES, N_PATCH, 2 * HALO), 0, nodes_out[:, :, None])
    return picks.reshape(SAMPLES, N_PATCH * 2 * HALO).astype(jnp.int32)


def draw_neighbours(key, part):
    key = jax.random.fold_in(key, 11)
    others = jax.random.randint(key, (SAMPLES, NODES, NEIGH - 1), 0, NODE_DEV + 2 * HALO)
    selves = jnp.broadcast_to((jnp.arange(NODES) % NODE_DEV)[None, :, None], (SAMPLES, NODES, 1))
    return jnp.concatenate([selves.astype(jnp.int32), others.astype(jnp.int32)], axis=2)


def shard_levels(key, extent, pieces, smallest, top_value):
    gain, own = 1.0, jax.random.fold_in(key, 6)
    for dim, parts in pieces:
        steps = jnp.exp(jax.random.uniform(jax.random.fold_in(own, dim), (parts,), jnp.float32, smallest / len(pieces), top_value / len(pieces)))
        gain = gain * jnp.repeat(steps, extent[dim] // parts).reshape([-1 if axis == dim else 1 for axis in range(len(extent))])
    return gain


def gaussian(key, shape, deviation, limit, cuts=(), kind=jnp.bfloat16):
    gain = shard_levels(key, shape, cuts, -0.22, 0.18) if cuts else 1.0
    entries = jax.random.normal(key, shape, jnp.float32) * deviation * gain
    return jnp.minimum(jnp.maximum(entries, -limit), limit).astype(kind)


def setup_inputs(seed: int = 0) -> dict:
    seeds = jax.random.split(jax.random.key(seed), 32)
    previous_state = gaussian(seeds[0], (SAMPLES, CH, PIXELS), 1.0, 6.0, ((0, 4), (2, 8)), jnp.float32)
    target_state = gaussian(seeds[1], (SAMPLES, CH, PIXELS), 1.0, 6.0, ((0, 4), (2, 8)), jnp.float32)
    noise_draws = gaussian(seeds[2], (SAMPLES, 2, CH, PIXELS), 1.0, 6.0, ((0, 4), (3, 8)), jnp.float32)
    noise_level = jnp.clip(jnp.exp(math.log(3.0) - 2.3025851 * jax.random.uniform(seeds[3], (SAMPLES, 2), jnp.float32) ** shard_levels(seeds[3], (SAMPLES, 2), ((0, 4),), -0.2, 0.2)), 0.3, 3.0)
    pixel_owner = draw_pixel_owner(jax.random.fold_in(seeds[31], 71), 0)
    mesh_to_grid = draw_mesh_to_grid(jax.random.fold_in(seeds[31], 71), 0)
    neighbours = draw_neighbours(jax.random.fold_in(seeds[31], 71), 0)
    halo_send = draw_halo_send(jax.random.fold_in(seeds[31], 71), 0)
    node_count = draw_node_count(jax.random.fold_in(seeds[31], 71), 0)
    pixel_count = draw_pixel_count(jax.random.fold_in(seeds[31], 71), 0)
    w_encode = gaussian(seeds[10], (2 * CH, D), (2 * CH) ** -0.5, 0.5, ((1, 32),), jnp.float32)
    w_project = gaussian(seeds[11], (D, 3 * D), D ** -0.5, 0.25, ((0, 32),), jnp.float32)
    w_output = gaussian(seeds[12], (D, D), (D // 4) ** -0.5, 0.5, ((0, 32),), jnp.float32)
    w_up = gaussian(seeds[13], (D, FF), D ** -0.5, 0.25, ((0, 32),), jnp.float32)
    w_down = gaussian(seeds[14], (FF, D), FF ** -0.5, 0.125, ((0, 32),), jnp.float32)
    w_noise = gaussian(seeds[15], (FOUR, 4 * D), FOUR ** -0.5, 1.0, ((1, 32),), jnp.float32)
    w_decode = gaussian(seeds[16], (D, CH), D ** -0.5, 0.25, ((0, 32),), jnp.float32)
    m_encode = gaussian(seeds[17], (2 * CH, D), (0.11 / PARAMS ** 0.5), 0.00036621094, ((1, 32),), jnp.float32)
    m_project = gaussian(seeds[18], (D, 3 * D), (0.11 / PARAMS ** 0.5), 0.00036621094, ((0, 32),), jnp.float32)
    m_output = gaussian(seeds[19], (D, D), (0.11 / PARAMS ** 0.5), 0.00036621094, ((0, 32),), jnp.float32)
    m_up = gaussian(seeds[20], (D, FF), (0.11 / PARAMS ** 0.5), 0.00036621094, ((0, 32),), jnp.float32)
    m_down = gaussian(seeds[21], (FF, D), (0.11 / PARAMS ** 0.5), 0.00036621094, ((0, 32),), jnp.float32)
    m_noise = gaussian(seeds[22], (FOUR, 4 * D), (0.11 / PARAMS ** 0.5), 0.00036621094, ((1, 32),), jnp.float32)
    m_decode = gaussian(seeds[23], (D, CH), (0.11 / PARAMS ** 0.5), 0.00036621094, ((0, 32),), jnp.float32)
    v_encode = jnp.clip(jnp.exp(math.log(6.286882836548102e-08) - 1.3843913 * jax.random.uniform(seeds[24], (2 * CH, D), jnp.float32) ** shard_levels(seeds[24], (2 * CH, D), ((1, 32),), -0.2, 0.2)), 1.5747145809541507e-08, 6.286882836548102e-08)
    v_project = jnp.clip(jnp.exp(math.log(6.286882836548102e-08) - 1.3843913 * jax.random.uniform(seeds[25], (D, 3 * D), jnp.float32) ** shard_levels(seeds[25], (D, 3 * D), ((0, 32),), -0.2, 0.2)), 1.5747145809541507e-08, 6.286882836548102e-08)
    v_output = jnp.clip(jnp.exp(math.log(6.286882836548102e-08) - 1.3843913 * jax.random.uniform(seeds[26], (D, D), jnp.float32) ** shard_levels(seeds[26], (D, D), ((0, 32),), -0.2, 0.2)), 1.5747145809541507e-08, 6.286882836548102e-08)
    v_up = jnp.clip(jnp.exp(math.log(6.286882836548102e-08) - 1.3843913 * jax.random.uniform(seeds[27], (D, FF), jnp.float32) ** shard_levels(seeds[27], (D, FF), ((0, 32),), -0.2, 0.2)), 1.5747145809541507e-08, 6.286882836548102e-08)
    v_down = jnp.clip(jnp.exp(math.log(6.286882836548102e-08) - 1.3843913 * jax.random.uniform(seeds[28], (FF, D), jnp.float32) ** shard_levels(seeds[28], (FF, D), ((0, 32),), -0.2, 0.2)), 1.5747145809541507e-08, 6.286882836548102e-08)
    v_noise = jnp.clip(jnp.exp(math.log(6.286882836548102e-08) - 1.3843913 * jax.random.uniform(seeds[29], (FOUR, 4 * D), jnp.float32) ** shard_levels(seeds[29], (FOUR, 4 * D), ((1, 32),), -0.2, 0.2)), 1.5747145809541507e-08, 6.286882836548102e-08)
    v_decode = jnp.clip(jnp.exp(math.log(6.286882836548102e-08) - 1.3843913 * jax.random.uniform(seeds[30], (D, CH), jnp.float32) ** shard_levels(seeds[30], (D, CH), ((0, 32),), -0.2, 0.2)), 1.5747145809541507e-08, 6.286882836548102e-08)
    return dict(previous_state=previous_state, target_state=target_state, noise_draws=noise_draws, noise_level=noise_level, pixel_owner=pixel_owner, mesh_to_grid=mesh_to_grid, neighbours=neighbours, halo_send=halo_send, node_count=node_count, pixel_count=pixel_count, w_encode=w_encode, w_project=w_project, w_output=w_output, w_up=w_up, w_down=w_down, w_noise=w_noise, w_decode=w_decode, m_encode=m_encode, m_project=m_project, m_output=m_output, m_up=m_up, m_down=m_down, m_noise=m_noise, m_decode=m_decode, v_encode=v_encode, v_project=v_project, v_output=v_output, v_up=v_up, v_down=v_down, v_noise=v_noise, v_decode=v_decode)


@jax.custom_vjp
def low(v):
    return lax.optimization_barrier(v.astype(jnp.bfloat16)).astype(jnp.float32)

@jax.custom_vjp
def low_back(v):
    return v

def low_keep(v):
    return (low(v), None)

def low_pass(kept, grad):
    return (grad,)

def back_keep(v):
    return (v, None)

def back_low(kept, grad):
    return (low(grad),)
low.defvjp(low_keep, low_pass)
low_back.defvjp(back_keep, back_low)
HIGHEST = lax.Precision.HIGHEST
LEARN_RATE = 0.03
BETA_ONE = 0.9
BETA_TWO = 0.95
EPSILON = 1e-08
DECAY_RATE = 0.1
THRESHOLD = 1.0

def fourier(level):
    frequency = 0.25 * (jnp.arange(FOUR // 2).astype(jnp.float32) + 1.0)
    angles = jnp.log(level) * frequency
    return jnp.concatenate([jnp.sin(angles), jnp.cos(angles)])

def adanorm(hidden, scaling, offset):
    centre = hidden - lax.optimization_barrier(jnp.mean(hidden, axis=-1, keepdims=True))
    spread = lax.optimization_barrier(jnp.mean(centre * centre, axis=-1, keepdims=True))
    return centre * lax.rsqrt(spread + 1e-05) * (1.0 + scaling) + offset

def network(weights, noisy_in, previous, level, owners, decode_idx, near_idx, send_idx, node_live, pixel_live):
    w_encode, w_project, w_output, w_up, w_down, w_noise, w_decode = weights
    patches = near_idx.shape[0]
    halo_rows = send_idx.shape[1] // 2
    c_in = lax.rsqrt(level * level + 1.0)
    c_skip = 1.0 / (level * level + 1.0)
    c_out = level * c_in
    inputs = low(jnp.concatenate([previous, noisy_in * c_in], axis=0))
    encoded = low_back(low(jnp.einsum('cqp,cd->qpd', inputs, w_encode, precision=HIGHEST)))
    summed = low_back(jax.vmap(lambda e, o: jax.ops.segment_sum(e, o, num_segments=NODE_DEV))(encoded * pixel_live[:, :, None], owners))
    counted = jax.vmap(lambda l, o: jax.ops.segment_sum(l, o, num_segments=NODE_DEV))(pixel_live, owners)
    start_rows = summed / jnp.maximum(counted, 1.0)[:, :, None]
    modulate = jnp.dot(fourier(level), w_noise, precision=HIGHEST)
    normed = low(adanorm(start_rows, modulate[:D], modulate[D:2 * D]))
    project = low_back(low(jnp.einsum('qnd,de->qne', normed, w_project, precision=HIGHEST)))
    keyval = project[:, :, D:]
    sent_rows = jax.vmap(lambda e, i: e[i])(keyval, send_idx)
    from_lower = low_back(jnp.roll(sent_rows[:, halo_rows:], 1, axis=0))
    from_upper = low_back(jnp.roll(sent_rows[:, :halo_rows], -1, axis=0))
    extended = jnp.concatenate([keyval, from_lower, from_upper], axis=1)
    near = jax.vmap(lambda e, i: e[i])(extended, near_idx)
    key_rows = near[..., :D].reshape(patches, NODE_DEV, NEIGH, HEADS, HD)
    val_rows = near[..., D:].reshape(patches, NODE_DEV, NEIGH, HEADS, HD)
    queries = project[:, :, :D].reshape(patches, NODE_DEV, HEADS, HD)
    raw_scores = low_back(jnp.einsum('qnhd,qnjhd->qnhj', queries, key_rows, precision=HIGHEST))
    safe_idx = jnp.minimum(near_idx, NODE_DEV - 1).reshape(patches, -1)
    key_live = jnp.take_along_axis(node_live, safe_idx, axis=1).reshape(near_idx.shape)
    valid = (near_idx >= NODE_DEV) | key_live | (jnp.arange(NEIGH) == 0)
    scores = jnp.where(valid[:, :, None, :], raw_scores * HD ** (-0.5), -1e+30)
    attention = low(jax.nn.softmax(scores, axis=-1))
    mixed_out = low_back(low(jnp.einsum('qnhj,qnjhd->qnhd', attention, val_rows, precision=HIGHEST)))
    mixed_out = mixed_out.reshape(patches, NODE_DEV, D)
    middle = start_rows + low_back(jnp.einsum('qnd,de->qne', mixed_out, w_output, precision=HIGHEST))
    second = low(adanorm(middle, modulate[2 * D:3 * D], modulate[3 * D:]))
    upward = low_back(jnp.einsum('qnd,df->qnf', second, w_up, precision=HIGHEST))
    gated_up = low(jax.nn.silu(upward))
    final_rows = middle + low_back(jnp.einsum('qnf,fd->qnd', gated_up, w_down, precision=HIGHEST))
    picked = jax.vmap(lambda h, i: (h[i[0]] + h[i[1]] + h[i[2]]) / 3.0, in_axes=(0, 1))(final_rows, decode_idx)
    output = low_back(jnp.einsum('qpd,dc->cqp', low(picked), w_decode, precision=HIGHEST))
    return c_skip * noisy_in + c_out * output

def sample_loss(weights, previous, target, noise_now, levels, owners, decode_idx, near_idx, send_idx, node_cnt, pixel_cnt):
    previous = previous.reshape(CH, N_PATCH, PIX_DEV)
    target = target.reshape(CH, N_PATCH, PIX_DEV)
    noise_now = noise_now.reshape(2, CH, N_PATCH, PIX_DEV)
    owners = owners.reshape(N_PATCH, PIX_DEV)
    decode_idx = decode_idx.reshape(3, N_PATCH, PIX_DEV)
    near_idx = near_idx.reshape(N_PATCH, NODE_DEV, NEIGH)
    send_idx = send_idx.reshape(N_PATCH, 2 * HALO)
    node_live = jnp.arange(NODE_DEV)[None, :] < node_cnt[:, None]
    pixel_live = (jnp.arange(PIX_DEV)[None, :] < pixel_cnt[:, None]).astype(jnp.float32)
    lowered = [low(w) for w in weights]
    pred_one = network(lowered, target + levels[0] * noise_now[0], previous, levels[0], owners, decode_idx, near_idx, send_idx, node_live, pixel_live)
    pred_two = network(lowered, pred_one + levels[1] * noise_now[1], previous, levels[1], owners, decode_idx, near_idx, send_idx, node_live, pixel_live)
    error = (pred_two - target) * pixel_live[None, :, :]
    return jnp.sum(error * error)

def reference(previous_state, target_state, noise_draws, noise_level, pixel_owner, mesh_to_grid, neighbours, halo_send, node_count, pixel_count, w_encode, w_project, w_output, w_up, w_down, w_noise, w_decode, m_encode, m_project, m_output, m_up, m_down, m_noise, m_decode, v_encode, v_project, v_output, v_up, v_down, v_noise, v_decode):
    weights = [w_encode, w_project, w_output, w_up, w_down, w_noise, w_decode]
    moments = [m_encode, m_project, m_output, m_up, m_down, m_noise, m_decode]
    seconds = [v_encode, v_project, v_output, v_up, v_down, v_noise, v_decode]

    def one_sample(carry, data):
        running, grads = carry
        value, pull = jax.vjp(lambda ws: sample_loss(ws, *data), weights)
        more, = pull(jnp.ones((), jnp.float32))
        return ((running + value, [a + b for a, b in zip(grads, more)]), None)
    zeros = [jnp.zeros_like(w) for w in weights]
    (loss_sum, grads), _ = lax.scan(one_sample, (jnp.zeros((), jnp.float32), zeros), (previous_state, target_state, noise_draws, noise_level, pixel_owner, mesh_to_grid, neighbours, halo_send, node_count, pixel_count))
    count_total = CH * jnp.sum((jnp.arange(PIX_DEV)[None, None, :] < pixel_count[:, :, None]).astype(jnp.float32))
    squares = jnp.zeros((), jnp.float32)
    for g in grads:
        squares = squares + jnp.sum(g * g)
    grad_norm = jnp.sqrt(squares)
    factor = THRESHOLD / jnp.maximum(grad_norm, THRESHOLD)
    new_weights, new_moments, new_seconds = ([], [], [])
    for w, m, v, g in zip(weights, moments, seconds, grads):
        clipped = g * factor
        moment = BETA_ONE * m + (1.0 - BETA_ONE) * clipped
        variance = BETA_TWO * v + (1.0 - BETA_TWO) * clipped * clipped
        stepped = moment / (1.0 - BETA_ONE ** STEP) / (jnp.sqrt(variance / (1.0 - BETA_TWO ** STEP)) + EPSILON)
        new_weights.append(w - LEARN_RATE * (stepped + DECAY_RATE * w))
        new_moments.append(moment)
        new_seconds.append(variance)
    return (new_weights[0], new_weights[1], new_weights[2], new_weights[3], new_weights[4], new_weights[5], new_weights[6], new_moments[0], new_moments[1], new_moments[2], new_moments[3], new_moments[4], new_moments[5], new_moments[6], new_seconds[0], new_seconds[1], new_seconds[2], new_seconds[3], new_seconds[4], new_seconds[5], new_seconds[6], loss_sum, count_total, grad_norm)
```

```python
import jax
import jax.numpy as jnp
from jax import lax
from jax.sharding import PartitionSpec as P

HEADS = 4
HD = 128
FOUR = 32
NEIGH = 16
STEP = 5


LEARN_RATE = 0.03
BETA_ONE = 0.9
BETA_TWO = 0.95
EPSILON = 1e-08
DECAY_RATE = 0.1
THRESHOLD = 1.0

BOTH = ("patch", "rep")
LOW = jnp.bfloat16
WIDE = jnp.float32
SCALE = HD ** (-0.5)


def nn(a, b):
    return lax.dot_general(a, b, (((1,), (0,)), ((), ())), preferred_element_type=WIDE)


def nt(a, b):
    return lax.dot_general(a, b, (((1,), (1,)), ((), ())), preferred_element_type=WIDE)


def tn(a, b):
    return lax.dot_general(a, b, (((0,), (0,)), ((), ())), preferred_element_type=WIDE)


def tt(a, b):
    return lax.dot_general(a, b, (((0,), (1,)), ((), ())), preferred_element_type=WIDE)


def fourier(level):
    frequency = 0.25 * (jnp.arange(FOUR // 2).astype(jnp.float32) + 1.0)
    angles = jnp.log(level) * frequency
    return jnp.concatenate([jnp.sin(angles), jnp.cos(angles)])


def norm_parts(hidden):
    centre = hidden - jnp.mean(hidden, axis=-1, keepdims=True)
    spread = jnp.mean(centre * centre, axis=-1, keepdims=True)
    inverse = lax.rsqrt(spread + 1e-05)
    return centre * inverse, inverse


def norm_back(unit, inverse, scaling, d_out):
    d_scale = jnp.sum(d_out * unit, axis=0)
    d_shift = jnp.sum(d_out, axis=0)
    d_unit = d_out * (1.0 + scaling)
    along = jnp.mean(d_unit * unit, axis=-1, keepdims=True)
    d_hidden = inverse * (d_unit - jnp.mean(d_unit, axis=-1, keepdims=True) - unit * along)
    return d_hidden, d_scale, d_shift


def exchange(rows):
    half = rows.shape[0] // 2
    devices = lax.axis_size("patch")
    up = [(i, (i + 1) % devices) for i in range(devices)]
    down = [(j, i) for i, j in up]
    from_lower = lax.ppermute(rows[half:], "patch", up)
    from_upper = lax.ppermute(rows[:half], "patch", down)
    return jnp.concatenate([from_lower, from_upper], axis=0)


def attend(project, extended, listed, head):
    width = HEADS * HD
    cols = slice(head * HD, (head + 1) * HD)
    queries, keys = project[:, cols], extended[:, cols]
    values = extended[:, width + head * HD : width + (head + 1) * HD]
    scores = jnp.where(listed > 0.0, nt(queries, keys) * SCALE, -1e30)
    top = jnp.max(scores, axis=-1, keepdims=True)
    weight = listed * jnp.exp(scores - top)
    return queries, keys, values, weight / jnp.sum(weight, axis=-1, keepdims=True)


def forward(weights, wave, noisy, level, sums_previous, shared):
    w_encode, w_project, w_output, w_up, w_down, w_decode = weights
    owner_hot, counted, node_hot, listed, send_hot = shared
    width = w_project.shape[0]
    c_in = lax.rsqrt(level * level + 1.0)
    c_skip = 1.0 / (level * level + 1.0)
    c_out = level * c_in
    sums = jnp.concatenate([sums_previous, nt(owner_hot, (noisy * c_in).astype(LOW))], axis=1).astype(LOW)
    start = nt(sums, w_encode) / counted
    unit_one, inv_one = norm_parts(start)
    normed = (unit_one * (1.0 + wave[0]) + wave[1]).astype(LOW)
    project = nn(normed, w_project).astype(LOW)
    keyval = project[:, width:]
    extended = jnp.concatenate([keyval, exchange(nn(send_hot, keyval).astype(LOW))], axis=0)
    mixed, attention = [], []
    for head in range(HEADS):
        _, _, values, probs = attend(project, extended, listed, head)
        attention.append(probs)
        mixed.append(nn(probs.astype(LOW), values))
    mixed = jnp.concatenate(mixed, axis=1).astype(LOW)
    middle = start + nn(mixed, w_output)
    unit_two, inv_two = norm_parts(middle)
    second = (unit_two * (1.0 + wave[2]) + wave[3]).astype(LOW)
    upward = nn(second, w_up)
    gated = (upward * jax.nn.sigmoid(upward)).astype(LOW)
    final = (middle + nn(gated, w_down)).astype(LOW)
    nodes_out = tt(w_decode, final).astype(LOW)
    output = nn(nodes_out, node_hot) * (1.0 / 3.0)
    predicted = c_skip * noisy + c_out * output
    stored = (sums, unit_one, inv_one, normed, project, extended, attention, mixed, unit_two, inv_two, second,
              upward, gated, final, c_in, c_skip, c_out)
    return predicted, stored


def backward(weights, wave, stored, d_pred, shared, need_input):
    w_encode, w_project, w_output, w_up, w_down, w_decode = weights
    owner_hot, counted, node_hot, listed, send_hot = shared
    (sums, unit_one, inv_one, normed, project, extended, attention, mixed, unit_two, inv_two, second,
     upward, gated, final, c_in, c_skip, c_out) = stored
    width = w_project.shape[0]
    nodes = project.shape[0]
    d_output = (c_out * d_pred).astype(LOW)
    gathered = (nt(node_hot, d_output) * (1.0 / 3.0)).astype(LOW)
    g_decode = tn(final, gathered)
    d_final = nt(gathered, w_decode)
    d_branch = d_final.astype(LOW)
    g_down = tn(gated, d_branch)
    d_gated = nt(d_branch, w_down)
    gate = jax.nn.sigmoid(upward)
    d_upward = (d_gated * gate * (1.0 + upward * (1.0 - gate))).astype(LOW)
    g_up = tn(second, d_upward)
    d_second = nt(d_upward, w_up)
    d_norm, d_scale_two, d_shift_two = norm_back(unit_two, inv_two, wave[2], d_second)
    d_middle = d_final + d_norm
    d_attn = d_middle.astype(LOW)
    g_output = tn(mixed, d_attn)
    d_mixed = nt(d_attn, w_output).astype(LOW)
    d_queries, d_keys, d_values = [], [], []
    for head in range(HEADS):
        cols = slice(head * HD, (head + 1) * HD)
        queries, keys = project[:, cols], extended[:, cols]
        values = extended[:, width + head * HD : width + (head + 1) * HD]
        probs = attention[head]
        d_head = d_mixed[:, cols]
        d_probs = nt(d_head, values)
        d_values.append(tn(probs.astype(LOW), d_head))
        d_scores = probs * (d_probs - jnp.sum(probs * d_probs, axis=-1, keepdims=True))
        d_low = (d_scores * SCALE).astype(LOW)
        d_queries.append(nn(d_low, keys))
        d_keys.append(tn(d_low, queries))
    d_extended = jnp.concatenate(d_keys + d_values, axis=1)
    returned = exchange_order(d_extended[nodes:].astype(LOW))
    d_keyval = d_extended[:nodes] + tn(send_hot, returned)
    d_project = jnp.concatenate(d_queries + [d_keyval], axis=1).astype(LOW)
    g_project = tn(normed, d_project)
    d_normed = nt(d_project, w_project)
    d_norm, d_scale_one, d_shift_one = norm_back(unit_one, inv_one, wave[0], d_normed)
    d_start = d_middle + d_norm
    d_summed = (d_start / counted).astype(LOW)
    g_encode = tn(d_summed, sums)
    d_wave = jnp.concatenate([d_scale_one, d_shift_one, d_scale_two, d_shift_two])
    grads = [g_encode, g_project, g_output, g_up, g_down, g_decode]
    if not need_input:
        return grads, d_wave, None
    channels = d_pred.shape[0]
    d_nodes = tt(w_encode[:, channels:], d_summed).astype(LOW)
    return grads, d_wave, c_skip * d_pred + c_in * nn(d_nodes, owner_hot)


def exchange_order(rows):
    half = rows.shape[0] // 2
    devices = lax.axis_size("patch")
    up = [(i, (i + 1) % devices) for i in range(devices)]
    down = [(j, i) for i, j in up]
    from_upper = lax.ppermute(rows[:half], "patch", down)
    from_lower = lax.ppermute(rows[half:], "patch", up)
    return jnp.concatenate([from_lower, from_upper], axis=0)


def fill(array, columns):
    return jnp.pad(array, ((0, 0), (0, columns - array.shape[1])))


def pack(encode, project, output, up, noise, decode):
    rows = project.shape[0]
    return jnp.concatenate(
        [project, output, up, fill(encode.T, 256), fill(decode, 128), noise.reshape(rows, -1)], axis=1
    )


def on_device(
    previous_state, target_state, noise_draws, noise_level, pixel_owner, mesh_to_grid, neighbours, halo_send,
    node_count, pixel_count, w_encode, w_project, w_output, w_up, w_down, w_noise, w_decode,
    m_encode, m_project, m_output, m_up, m_down, m_noise, m_decode,
    v_encode, v_project, v_output, v_up, v_down, v_noise, v_decode,
):
    width = w_project.shape[1] // 3
    hidden = w_up.shape[1]
    channels = previous_state.shape[1]
    rows = w_project.shape[0]
    packed = pack(*(w.astype(LOW) for w in (w_encode, w_project, w_output, w_up, w_noise, w_decode)))
    all_wide = lax.all_gather(packed, BOTH, axis=0, tiled=True)
    all_down = lax.all_gather(w_down.astype(LOW), BOTH, axis=0, tiled=True)
    at = [0, 3 * width, 4 * width, 4 * width + hidden, 4 * width + hidden + 256, 4 * width + hidden + 384]
    w_low = (
        all_wide[:, at[3] : at[3] + 2 * channels],
        all_wide[:, : at[1]],
        all_wide[:, at[1] : at[2]],
        all_wide[:, at[2] : at[3]],
        all_down,
        all_wide[:, at[4] : at[4] + channels],
    )
    devices = width // rows
    low_noise = all_wide[:, at[5] :].reshape(devices, FOUR, -1).transpose(1, 0, 2).reshape(FOUR, -1)

    previous, target = previous_state[0], target_state[0]
    noise_now, levels = noise_draws[0], noise_level[0]
    owners, decode_idx, near_idx, send_idx = pixel_owner[0], mesh_to_grid[0], neighbours[0], halo_send[0]
    nodes = near_idx.shape[0]
    halo = send_idx.shape[0] // 2
    pixels = owners.shape[0]
    pixel_live = (jnp.arange(pixels) < pixel_count[0, 0]).astype(WIDE)
    node_col = jnp.arange(nodes)[:, None]
    owner_hot = ((owners[None, :] == node_col) & (pixel_live[None, :] > 0.0)).astype(LOW)
    counted = jnp.maximum(jnp.sum(owner_hot, axis=1, dtype=WIDE), 1.0)[:, None]
    node_hot = sum((decode_idx[i][None, :] == node_col).astype(WIDE) for i in range(3)).astype(LOW)
    place = jnp.arange(nodes + 2 * halo)[None, :]
    listed = sum((near_idx[:, j : j + 1] == place).astype(WIDE) for j in range(1, NEIGH))
    listed = jnp.where((place >= nodes) | (place < node_count[0, 0]), listed, 0.0)
    listed = listed + (near_idx[:, :1] == place).astype(WIDE)
    send_hot = (send_idx[:, None] == jnp.arange(nodes)[None, :]).astype(LOW)
    shared = (owner_hot, counted, node_hot, listed, send_hot)

    waves = [fourier(levels[i]) for i in range(2)]
    modulate = jnp.dot(jnp.stack(waves), low_noise.astype(WIDE), precision=lax.Precision.HIGHEST)
    modulate = modulate.reshape(2, 4, width)
    sums_previous = nt(owner_hot, previous.astype(LOW))
    noisy_one = target + levels[0] * noise_now[0]
    pred_one, kept_one = forward(w_low, modulate[0], noisy_one, levels[0], sums_previous, shared)
    noisy_two = pred_one + levels[1] * noise_now[1]
    pred_two, kept_two = forward(w_low, modulate[1], noisy_two, levels[1], sums_previous, shared)
    error = (pred_two - target) * pixel_live[None, :]
    loss_local = jnp.sum(error * error)
    count_local = channels * jnp.sum(pixel_live)
    grads_two, wave_two, d_noisy = backward(w_low, modulate[1], kept_two, 2.0 * error, shared, True)
    grads_one, wave_one, _ = backward(w_low, modulate[0], kept_one, d_noisy, shared, False)
    g_encode, g_project, g_output, g_up, g_down, g_decode = [a + b for a, b in zip(grads_one, grads_two)]
    g_noise = waves[0][:, None] * wave_one[None, :] + waves[1][:, None] * wave_two[None, :]
    g_noise = g_noise.reshape(FOUR, devices, -1).transpose(1, 0, 2).reshape(width, -1)
    g_wide = jnp.concatenate(
        [g_project, g_output, g_up, fill(g_encode, 256), fill(g_decode, 128), g_noise], axis=1
    )
    s_wide = lax.psum_scatter(g_wide.astype(LOW), BOTH, scatter_dimension=0, tiled=True).astype(WIDE)
    s_down = lax.psum_scatter(g_down.astype(LOW), BOTH, scatter_dimension=0, tiled=True).astype(WIDE)
    shards = (
        s_wide[:, at[3] : at[3] + 2 * channels].T,
        s_wide[:, : at[1]],
        s_wide[:, at[1] : at[2]],
        s_wide[:, at[2] : at[3]],
        s_down,
        s_wide[:, at[5] :].reshape(FOUR, -1),
        s_wide[:, at[4] : at[4] + channels],
    )
    squares = jnp.sum(s_wide * s_wide) + jnp.sum(s_down * s_down)
    totals = lax.psum((squares, loss_local, count_local), BOTH)
    grad_norm = jnp.sqrt(totals[0])
    factor = THRESHOLD / jnp.maximum(grad_norm, THRESHOLD)
    masters = (w_encode, w_project, w_output, w_up, w_down, w_noise, w_decode)
    moments = (m_encode, m_project, m_output, m_up, m_down, m_noise, m_decode)
    seconds = (v_encode, v_project, v_output, v_up, v_down, v_noise, v_decode)
    new_weights, new_moments, new_seconds = ([], [], [])
    for w, m, v, g in zip(masters, moments, seconds, shards):
        clipped = g * factor
        moment = BETA_ONE * m + (1.0 - BETA_ONE) * clipped
        variance = BETA_TWO * v + (1.0 - BETA_TWO) * clipped * clipped
        stepped = (
            moment
            / (1.0 - BETA_ONE**STEP)
            / (jnp.sqrt(variance / (1.0 - BETA_TWO**STEP)) + EPSILON)
        )
        new_weights.append(w - LEARN_RATE * (stepped + DECAY_RATE * w))
        new_moments.append(moment)
        new_seconds.append(variance)
    return (
        tuple(new_weights)
        + tuple(new_moments)
        + tuple(new_seconds)
        + (totals[1], totals[2], grad_norm)
    )


def solution(mesh):
    in_specs = (
        P("rep", None, "patch"),
        P("rep", None, "patch"),
        P("rep", None, None, "patch"),
        P("rep", None),
        P("rep", "patch"),
        P("rep", None, "patch"),
        P("rep", "patch", None),
        P("rep", "patch"),
        P("rep", "patch"),
        P("rep", "patch"),
        P(None, ("patch", "rep")),
        P(("patch", "rep"), None),
        P(("patch", "rep"), None),
        P(("patch", "rep"), None),
        P(("patch", "rep"), None),
        P(None, ("patch", "rep")),
        P(("patch", "rep"), None),
        P(None, ("patch", "rep")),
        P(("patch", "rep"), None),
        P(("patch", "rep"), None),
        P(("patch", "rep"), None),
        P(("patch", "rep"), None),
        P(None, ("patch", "rep")),
        P(("patch", "rep"), None),
        P(None, ("patch", "rep")),
        P(("patch", "rep"), None),
        P(("patch", "rep"), None),
        P(("patch", "rep"), None),
        P(("patch", "rep"), None),
        P(None, ("patch", "rep")),
        P(("patch", "rep"), None),
    )
    out_specs = (
        P(None, ("patch", "rep")),
        P(("patch", "rep"), None),
        P(("patch", "rep"), None),
        P(("patch", "rep"), None),
        P(("patch", "rep"), None),
        P(None, ("patch", "rep")),
        P(("patch", "rep"), None),
        P(None, ("patch", "rep")),
        P(("patch", "rep"), None),
        P(("patch", "rep"), None),
        P(("patch", "rep"), None),
        P(("patch", "rep"), None),
        P(None, ("patch", "rep")),
        P(("patch", "rep"), None),
        P(None, ("patch", "rep")),
        P(("patch", "rep"), None),
        P(("patch", "rep"), None),
        P(("patch", "rep"), None),
        P(("patch", "rep"), None),
        P(None, ("patch", "rep")),
        P(("patch", "rep"), None),
        P(),
        P(),
        P(),
    )
    return jax.shard_map(
        on_device, mesh=mesh, in_specs=in_specs, out_specs=out_specs, check_vma=False
    )
```

```python
import jax
import jax.numpy as jnp
from jax import lax
from jax.experimental import pallas as pl
from jax.experimental.pallas import tpu as pltpu
from jax.sharding import PartitionSpec as P

HEADS = 4
HD = 128
FOUR = 32
NEIGH = 16
STEP = 5


LEARN_RATE = 0.03
BETA_ONE = 0.9
BETA_TWO = 0.95
EPSILON = 1e-08
DECAY_RATE = 0.1
THRESHOLD = 1.0

BOTH = ("patch", "rep")
LOW = jnp.bfloat16
WIDE = jnp.float32
SCALE = HD ** (-0.5)


MESH = pl.DeviceIdType.MESH
GRID = (4, 2, 2, 2)


def places():
    patch, rep = lax.axis_index("patch"), lax.axis_index("rep")
    z, y, x, c = patch // 2, patch % 2, rep // 2, rep % 2
    sibling = {"patch": patch, "rep": x * 2 + (1 - c)}
    across_x = {"patch": patch, "rep": (1 - x) * 2 + c}
    across_y = {"patch": z * 2 + (1 - y), "rep": rep}
    along_z = [{"patch": ((z + d) % 4) * 2 + y, "rep": rep} for d in range(4)]
    return z, y, x, c, sibling, across_x, across_y, along_z


def greet(others):
    barrier = pltpu.get_barrier_semaphore()
    for other in others:
        pl.semaphore_signal(barrier, inc=1, device_id=other, device_id_type=MESH)
    pl.semaphore_wait(barrier, len(others))


def send(src, dst, sems, index, device):
    copy = pltpu.make_async_remote_copy(
        src_ref=src, dst_ref=dst, send_sem=sems.at[(0,) + index], recv_sem=sems.at[(1,) + index],
        device_id=device, device_id_type=MESH,
    )
    copy.start()
    return copy


def plus(*terms):
    total = terms[0].astype(WIDE)
    for term in terms[1:]:
        total = total + term.astype(WIDE)
    return total


def scatter_scratch(rows, cols):
    h = cols // 2
    return [
        pltpu.VMEM((4, 2, 2, rows, cols), LOW),
        pltpu.VMEM((4, 2, 2, rows, cols), LOW),
        pltpu.VMEM((4, 2, rows, h), LOW),
        pltpu.VMEM((4, 2, rows, h), LOW),
        pltpu.VMEM((4, rows, h), LOW),
        pltpu.VMEM((4, 2, rows, h), LOW),
        pltpu.VMEM((4, 2, rows, h), LOW),
        pltpu.VMEM((4, rows, h), LOW),
        pltpu.VMEM((3, rows, cols), LOW),
        pltpu.VMEM((3, rows, cols), LOW),
    ]


def scatter_kernel(g_one, g_two, extra, out_one, out_two, totals, *scratch):
    z, y, x, c, sibling, across_x, across_y, along_z = places()
    parts = ((g_one, out_one) + scratch[:10], (g_two, out_two) + scratch[10:20])
    board, sems, small = scratch[20:]
    greet([sibling, across_x, across_y] + along_z[1:])
    steps = [(d, (z + d) % 4) for d in (1, 2, 3, 0)]
    sent, first, left, right, left_two, right_two, last = [], {}, {}, {}, {}, {}, {}
    for d, zd in steps:
        for i, (g, out, near, acc, near_l, acc_l, end_l, near_r, acc_r, end_r, going, come) in enumerate(parts):
            first[d, i] = send(g.at[zd, :, :, 1 - c], near.at[zd], sems, (0, d, i), sibling)
    for d, zd in steps:
        for i, (g, out, near, acc, near_l, acc_l, end_l, near_r, acc_r, end_r, going, come) in enumerate(parts):
            h = g.shape[-1] // 2
            first[d, i].wait_recv()
            acc[zd] = plus(g[zd, :, :, c], near[zd]).astype(LOW)
            left[d, i] = send(acc.at[zd, :, 1 - x, :, :h], near_l.at[zd], sems, (1, d, i), across_x)
            right[d, i] = send(acc.at[zd, 1 - y, :, :, h:], near_r.at[zd], sems, (2, d, i), across_y)
    for d, zd in steps:
        for i, (g, out, near, acc, near_l, acc_l, end_l, near_r, acc_r, end_r, going, come) in enumerate(parts):
            h = g.shape[-1] // 2
            left[d, i].wait_recv()
            acc_l[zd] = plus(acc[zd, :, x, :, :h], near_l[zd]).astype(LOW)
            left_two[d, i] = send(acc_l.at[zd, 1 - y], end_l.at[zd], sems, (3, d, i), across_y)
            right[d, i].wait_recv()
            acc_r[zd] = plus(acc[zd, y, :, :, h:], near_r[zd]).astype(LOW)
            right_two[d, i] = send(acc_r.at[zd, 1 - x], end_r.at[zd], sems, (4, d, i), across_x)
    for d, zd in steps:
        for i, (g, out, near, acc, near_l, acc_l, end_l, near_r, acc_r, end_r, going, come) in enumerate(parts):
            h = g.shape[-1] // 2
            left_two[d, i].wait_recv()
            done_l = plus(acc_l[zd, y], end_l[zd])
            right_two[d, i].wait_recv()
            done_r = plus(acc_r[zd, x], end_r[zd])
            if d == 0:
                out[:, :h] = done_l
                out[:, h:] = done_r
            else:
                going[d - 1, :, :h] = done_l.astype(LOW)
                going[d - 1, :, h:] = done_r.astype(LOW)
                last[d, i] = send(going.at[d - 1], come.at[d - 1], sems, (5, d, i), along_z[d])
    squares = jnp.zeros((), WIDE)
    for i, part in enumerate(parts):
        out, come = part[1], part[11]
        for d in (1, 2, 3):
            last[d, i].wait_recv()
        out[...] = plus(out[...], come[0], come[1], come[2])
        squares = squares + jnp.sum(out[...] * out[...])
    row = lax.broadcasted_iota(jnp.int32, extra.shape, 0)
    board[0] = jnp.where(row == 0, squares, extra[...])
    more = []
    for phase, device in enumerate((sibling, across_x, across_y)):
        copy = send(board.at[phase], board.at[4 + phase], small, (phase,), device)
        copy.wait_recv()
        more.append(copy)
        board[phase + 1] = board[phase] + board[4 + phase]
    for d in (1, 2, 3):
        more.append(send(board.at[3], board.at[8 + z], small, (2 + d,), along_z[d]))
    board[8 + z] = board[3]
    for d in (1, 2, 3):
        more[2 + d].wait_recv()
    totals[...] = board[8] + board[9] + board[10] + board[11]
    for group in (first, left, right, left_two, right_two, last):
        for copy in group.values():
            copy.wait_send()
    for copy in more:
        copy.wait_send()


def reduce_scatter(g_one, g_two, extra):
    rows = [g.shape[0] // 32 for g in (g_one, g_two)]
    cols = [g.shape[1] for g in (g_one, g_two)]
    vmem = pl.BlockSpec(memory_space=pltpu.VMEM)
    return pl.pallas_call(
        scatter_kernel,
        out_shape=[jax.ShapeDtypeStruct((r, n), WIDE) for r, n in zip(rows, cols)]
        + [jax.ShapeDtypeStruct(extra.shape, WIDE)],
        in_specs=[vmem] * 3,
        out_specs=[vmem] * 3,
        scratch_shapes=scatter_scratch(rows[0], cols[0]) + scatter_scratch(rows[1], cols[1])
        + [pltpu.VMEM((12,) + extra.shape, WIDE), pltpu.SemaphoreType.DMA((2, 6, 4, 2)),
           pltpu.SemaphoreType.DMA((2, 6))],
        compiler_params=pltpu.CompilerParams(
            collective_id=1, has_side_effects=True, vmem_limit_bytes=48 * 2**20),
    )(g_one.reshape(GRID + (rows[0], cols[0])), g_two.reshape(GRID + (rows[1], cols[1])), extra)


def gather_kernel(a_one, a_two, out_one, out_two, sems, local):
    z, y, x, c, sibling, across_x, across_y, along_z = places()
    greet([sibling, across_x, across_y] + along_z[1:])
    parts = ((a_one, out_one), (a_two, out_two))
    steps = [(d, (z + d) % 4) for d in (0, 1, 2, 3)]
    copies, own, x_one, y_one, x_two, y_two, core = [], [], {}, {}, {}, {}, {}
    planes = {}
    for i, (a, out) in enumerate(parts):
        copy = pltpu.make_async_copy(a, out.at[z, y, x, c], local.at[i])
        copy.start()
        own.append(copy)
        for d in (2, 1, 3):
            planes[d, i] = send(a, out.at[z, y, x, c], sems, (0, d, i), along_z[d])
    for i in range(2):
        own[i].wait()
    for d in range(4):
        zd = (z - d + 4) % 4
        for i, (a, out) in enumerate(parts):
            h = a.shape[-1] // 2
            if d:
                planes[d, i].wait_recv()
            here_l, here_r = out.at[zd, y, x, c, :, :h], out.at[zd, y, x, c, :, h:]
            x_one[d, i] = send(here_l, here_l, sems, (1, d, i), across_x)
            y_one[d, i] = send(here_r, here_r, sems, (2, d, i), across_y)
    for d in range(4):
        zd = (z - d + 4) % 4
        for i, (a, out) in enumerate(parts):
            h = a.shape[-1] // 2
            x_one[d, i].wait_recv()
            both = out.at[zd, y, :, c, :, :h]
            y_two[d, i] = send(both, both, sems, (3, d, i), across_y)
            y_one[d, i].wait_recv()
            both = out.at[zd, :, x, c, :, h:]
            x_two[d, i] = send(both, both, sems, (4, d, i), across_x)
    for d in range(4):
        zd = (z - d + 4) % 4
        for i, (a, out) in enumerate(parts):
            y_two[d, i].wait_recv()
            x_two[d, i].wait_recv()
            plane = out.at[zd, :, :, c]
            core[d, i] = send(plane, plane, sems, (5, d, i), sibling)
    for group in (planes, x_one, y_one, x_two, y_two):
        for copy in group.values():
            copy.wait_send()
    for copy in core.values():
        copy.wait()


def all_gather(a_one, a_two):
    shapes = [a.shape for a in (a_one, a_two)]
    outs = pl.pallas_call(
        gather_kernel,
        out_shape=[jax.ShapeDtypeStruct(GRID + s, LOW) for s in shapes],
        in_specs=[pl.BlockSpec(memory_space=pltpu.VMEM)] * 2,
        out_specs=[pl.BlockSpec(memory_space=pl.ANY)] * 2,
        scratch_shapes=[pltpu.SemaphoreType.DMA((2, 6, 4, 2)), pltpu.SemaphoreType.DMA((2,))],
        compiler_params=pltpu.CompilerParams(
            collective_id=2, has_side_effects=True, vmem_limit_bytes=32 * 2**20),
    )(a_one, a_two)
    return [o.reshape(32 * s[0], s[1]) for o, s in zip(outs, shapes)]


def nn(a, b):
    return lax.dot_general(a, b, (((1,), (0,)), ((), ())), preferred_element_type=WIDE)


def nt(a, b):
    return lax.dot_general(a, b, (((1,), (1,)), ((), ())), preferred_element_type=WIDE)


def tn(a, b):
    return lax.dot_general(a, b, (((0,), (0,)), ((), ())), preferred_element_type=WIDE)


def tt(a, b):
    return lax.dot_general(a, b, (((0,), (1,)), ((), ())), preferred_element_type=WIDE)


def fourier(level):
    frequency = 0.25 * (jnp.arange(FOUR // 2).astype(jnp.float32) + 1.0)
    angles = jnp.log(level) * frequency
    return jnp.concatenate([jnp.sin(angles), jnp.cos(angles)])


def norm_parts(hidden):
    centre = hidden - jnp.mean(hidden, axis=-1, keepdims=True)
    spread = jnp.mean(centre * centre, axis=-1, keepdims=True)
    inverse = lax.rsqrt(spread + 1e-05)
    return centre * inverse, inverse


def norm_back(unit, inverse, scaling, d_out):
    d_scale = jnp.sum(d_out * unit, axis=0)
    d_shift = jnp.sum(d_out, axis=0)
    d_unit = d_out * (1.0 + scaling)
    along = jnp.mean(d_unit * unit, axis=-1, keepdims=True)
    d_hidden = inverse * (d_unit - jnp.mean(d_unit, axis=-1, keepdims=True) - unit * along)
    return d_hidden, d_scale, d_shift


def exchange(rows):
    half = rows.shape[0] // 2
    devices = lax.axis_size("patch")
    up = [(i, (i + 1) % devices) for i in range(devices)]
    down = [(j, i) for i, j in up]
    from_lower = lax.ppermute(rows[half:], "patch", up)
    from_upper = lax.ppermute(rows[:half], "patch", down)
    return jnp.concatenate([from_lower, from_upper], axis=0)


def attend(project, extended, listed, head):
    width = HEADS * HD
    cols = slice(head * HD, (head + 1) * HD)
    queries, keys = project[:, cols], extended[:, cols]
    values = extended[:, width + head * HD : width + (head + 1) * HD]
    scores = jnp.where(listed > 0.0, nt(queries, keys) * SCALE, -1e30)
    top = jnp.max(scores, axis=-1, keepdims=True)
    weight = listed * jnp.exp(scores - top)
    return queries, keys, values, weight / jnp.sum(weight, axis=-1, keepdims=True)


def forward(weights, wave, noisy, level, sums_previous, shared):
    w_encode, w_project, w_output, w_up, w_down, w_decode = weights
    owner_hot, counted, node_hot, listed, send_hot = shared
    width = w_project.shape[0]
    c_in = lax.rsqrt(level * level + 1.0)
    c_skip = 1.0 / (level * level + 1.0)
    c_out = level * c_in
    sums = jnp.concatenate([sums_previous, nt(owner_hot, (noisy * c_in).astype(LOW))], axis=1).astype(LOW)
    start = nt(sums, w_encode) / counted
    unit_one, inv_one = norm_parts(start)
    normed = (unit_one * (1.0 + wave[0]) + wave[1]).astype(LOW)
    project = nn(normed, w_project).astype(LOW)
    keyval = project[:, width:]
    extended = jnp.concatenate([keyval, exchange(nn(send_hot, keyval).astype(LOW))], axis=0)
    mixed, attention = [], []
    for head in range(HEADS):
        _, _, values, probs = attend(project, extended, listed, head)
        attention.append(probs)
        mixed.append(nn(probs.astype(LOW), values))
    mixed = jnp.concatenate(mixed, axis=1).astype(LOW)
    middle = start + nn(mixed, w_output)
    unit_two, inv_two = norm_parts(middle)
    second = (unit_two * (1.0 + wave[2]) + wave[3]).astype(LOW)
    upward = nn(second, w_up)
    gated = (upward * jax.nn.sigmoid(upward)).astype(LOW)
    final = (middle + nn(gated, w_down)).astype(LOW)
    nodes_out = tt(w_decode, final).astype(LOW)
    output = nn(nodes_out, node_hot) * (1.0 / 3.0)
    predicted = c_skip * noisy + c_out * output
    stored = (sums, unit_one, inv_one, normed, project, extended, attention, mixed, unit_two, inv_two, second,
              upward, gated, final, c_in, c_skip, c_out)
    return predicted, stored


def backward(weights, wave, stored, d_pred, shared, need_input):
    w_encode, w_project, w_output, w_up, w_down, w_decode = weights
    owner_hot, counted, node_hot, listed, send_hot = shared
    (sums, unit_one, inv_one, normed, project, extended, attention, mixed, unit_two, inv_two, second,
     upward, gated, final, c_in, c_skip, c_out) = stored
    width = w_project.shape[0]
    nodes = project.shape[0]
    d_output = (c_out * d_pred).astype(LOW)
    gathered = (nt(node_hot, d_output) * (1.0 / 3.0)).astype(LOW)
    g_decode = tn(final, gathered)
    d_final = nt(gathered, w_decode)
    d_branch = d_final.astype(LOW)
    g_down = tn(gated, d_branch)
    d_gated = nt(d_branch, w_down)
    gate = jax.nn.sigmoid(upward)
    d_upward = (d_gated * gate * (1.0 + upward * (1.0 - gate))).astype(LOW)
    g_up = tn(second, d_upward)
    d_second = nt(d_upward, w_up)
    d_norm, d_scale_two, d_shift_two = norm_back(unit_two, inv_two, wave[2], d_second)
    d_middle = d_final + d_norm
    d_attn = d_middle.astype(LOW)
    g_output = tn(mixed, d_attn)
    d_mixed = nt(d_attn, w_output).astype(LOW)
    d_queries, d_keys, d_values = [], [], []
    for head in range(HEADS):
        cols = slice(head * HD, (head + 1) * HD)
        queries, keys = project[:, cols], extended[:, cols]
        values = extended[:, width + head * HD : width + (head + 1) * HD]
        probs = attention[head]
        d_head = d_mixed[:, cols]
        d_probs = nt(d_head, values)
        d_values.append(tn(probs.astype(LOW), d_head))
        d_scores = probs * (d_probs - jnp.sum(probs * d_probs, axis=-1, keepdims=True))
        d_low = (d_scores * SCALE).astype(LOW)
        d_queries.append(nn(d_low, keys))
        d_keys.append(tn(d_low, queries))
    d_extended = jnp.concatenate(d_keys + d_values, axis=1)
    returned = exchange_order(d_extended[nodes:].astype(LOW))
    d_keyval = d_extended[:nodes] + tn(send_hot, returned)
    d_project = jnp.concatenate(d_queries + [d_keyval], axis=1).astype(LOW)
    g_project = tn(normed, d_project)
    d_normed = nt(d_project, w_project)
    d_norm, d_scale_one, d_shift_one = norm_back(unit_one, inv_one, wave[0], d_normed)
    d_start = d_middle + d_norm
    d_summed = (d_start / counted).astype(LOW)
    g_encode = tn(d_summed, sums)
    d_wave = jnp.concatenate([d_scale_one, d_shift_one, d_scale_two, d_shift_two])
    grads = [g_encode, g_project, g_output, g_up, g_down, g_decode]
    if not need_input:
        return grads, d_wave, None
    channels = d_pred.shape[0]
    d_nodes = tt(w_encode[:, channels:], d_summed).astype(LOW)
    return grads, d_wave, c_skip * d_pred + c_in * nn(d_nodes, owner_hot)


def exchange_order(rows):
    half = rows.shape[0] // 2
    devices = lax.axis_size("patch")
    up = [(i, (i + 1) % devices) for i in range(devices)]
    down = [(j, i) for i, j in up]
    from_upper = lax.ppermute(rows[:half], "patch", down)
    from_lower = lax.ppermute(rows[half:], "patch", up)
    return jnp.concatenate([from_lower, from_upper], axis=0)


def fill(array, columns):
    return jnp.pad(array, ((0, 0), (0, columns - array.shape[1])))


def pack(encode, project, output, up, noise, decode):
    rows = project.shape[0]
    return jnp.concatenate(
        [project, output, up, fill(encode.T, 256), fill(decode, 128), noise.reshape(rows, -1)], axis=1
    )


def on_device(
    previous_state, target_state, noise_draws, noise_level, pixel_owner, mesh_to_grid, neighbours, halo_send,
    node_count, pixel_count, w_encode, w_project, w_output, w_up, w_down, w_noise, w_decode,
    m_encode, m_project, m_output, m_up, m_down, m_noise, m_decode,
    v_encode, v_project, v_output, v_up, v_down, v_noise, v_decode,
):
    width = w_project.shape[1] // 3
    hidden = w_up.shape[1]
    channels = previous_state.shape[1]
    rows = w_project.shape[0]
    packed = pack(*(w.astype(LOW) for w in (w_encode, w_project, w_output, w_up, w_noise, w_decode)))
    small_slice = lax.axis_size("patch") == 8 and lax.axis_size("rep") == 4
    if small_slice:
        all_wide, all_down = all_gather(packed, w_down.astype(LOW))
    else:
        all_wide = lax.all_gather(packed, BOTH, axis=0, tiled=True)
        all_down = lax.all_gather(w_down.astype(LOW), BOTH, axis=0, tiled=True)
    at = [0, 3 * width, 4 * width, 4 * width + hidden, 4 * width + hidden + 256, 4 * width + hidden + 384]
    w_low = (
        all_wide[:, at[3] : at[3] + 2 * channels],
        all_wide[:, : at[1]],
        all_wide[:, at[1] : at[2]],
        all_wide[:, at[2] : at[3]],
        all_down,
        all_wide[:, at[4] : at[4] + channels],
    )
    devices = width // rows
    low_noise = all_wide[:, at[5] :].reshape(devices, FOUR, -1).transpose(1, 0, 2).reshape(FOUR, -1)

    previous, target = previous_state[0], target_state[0]
    noise_now, levels = noise_draws[0], noise_level[0]
    owners, decode_idx, near_idx, send_idx = pixel_owner[0], mesh_to_grid[0], neighbours[0], halo_send[0]
    nodes = near_idx.shape[0]
    halo = send_idx.shape[0] // 2
    pixels = owners.shape[0]
    pixel_live = (jnp.arange(pixels) < pixel_count[0, 0]).astype(WIDE)
    node_col = jnp.arange(nodes)[:, None]
    owner_hot = ((owners[None, :] == node_col) & (pixel_live[None, :] > 0.0)).astype(LOW)
    counted = jnp.maximum(jnp.sum(owner_hot, axis=1, dtype=WIDE), 1.0)[:, None]
    node_hot = sum((decode_idx[i][None, :] == node_col).astype(WIDE) for i in range(3)).astype(LOW)
    place = jnp.arange(nodes + 2 * halo)[None, :]
    listed = sum((near_idx[:, j : j + 1] == place).astype(WIDE) for j in range(1, NEIGH))
    listed = jnp.where((place >= nodes) | (place < node_count[0, 0]), listed, 0.0)
    listed = listed + (near_idx[:, :1] == place).astype(WIDE)
    send_hot = (send_idx[:, None] == jnp.arange(nodes)[None, :]).astype(LOW)
    shared = (owner_hot, counted, node_hot, listed, send_hot)

    waves = [fourier(levels[i]) for i in range(2)]
    modulate = jnp.dot(jnp.stack(waves), low_noise.astype(WIDE), precision=lax.Precision.HIGHEST)
    modulate = modulate.reshape(2, 4, width)
    sums_previous = nt(owner_hot, previous.astype(LOW))
    noisy_one = target + levels[0] * noise_now[0]
    pred_one, kept_one = forward(w_low, modulate[0], noisy_one, levels[0], sums_previous, shared)
    noisy_two = pred_one + levels[1] * noise_now[1]
    pred_two, kept_two = forward(w_low, modulate[1], noisy_two, levels[1], sums_previous, shared)
    error = (pred_two - target) * pixel_live[None, :]
    loss_local = jnp.sum(error * error)
    count_local = channels * jnp.sum(pixel_live)
    grads_two, wave_two, d_noisy = backward(w_low, modulate[1], kept_two, 2.0 * error, shared, True)
    grads_one, wave_one, _ = backward(w_low, modulate[0], kept_one, d_noisy, shared, False)
    g_encode, g_project, g_output, g_up, g_down, g_decode = [a + b for a, b in zip(grads_one, grads_two)]
    g_noise = waves[0][:, None] * wave_one[None, :] + waves[1][:, None] * wave_two[None, :]
    g_noise = g_noise.reshape(FOUR, devices, -1).transpose(1, 0, 2).reshape(width, -1)
    g_wide = jnp.concatenate(
        [g_project, g_output, g_up, fill(g_encode, 256), fill(g_decode, 128), g_noise], axis=1
    )
    if small_slice:
        row = lax.broadcasted_iota(jnp.int32, (8, 128), 0)
        extra = jnp.where(row == 1, loss_local, 0.0) + jnp.where(row == 2, count_local, 0.0)
        s_wide, s_down, totals = reduce_scatter(g_wide.astype(LOW), g_down.astype(LOW), extra)
        totals = totals[:3, 0]
    else:
        s_wide = lax.psum_scatter(g_wide.astype(LOW), BOTH, scatter_dimension=0, tiled=True).astype(WIDE)
        s_down = lax.psum_scatter(g_down.astype(LOW), BOTH, scatter_dimension=0, tiled=True).astype(WIDE)
        squares = jnp.sum(s_wide * s_wide) + jnp.sum(s_down * s_down)
        totals = lax.psum((squares, loss_local, count_local), BOTH)
    shards = (
        s_wide[:, at[3] : at[3] + 2 * channels].T,
        s_wide[:, : at[1]],
        s_wide[:, at[1] : at[2]],
        s_wide[:, at[2] : at[3]],
        s_down,
        s_wide[:, at[5] :].reshape(FOUR, -1),
        s_wide[:, at[4] : at[4] + channels],
    )
    grad_norm = jnp.sqrt(totals[0])
    factor = THRESHOLD / jnp.maximum(grad_norm, THRESHOLD)
    masters = (w_encode, w_project, w_output, w_up, w_down, w_noise, w_decode)
    moments = (m_encode, m_project, m_output, m_up, m_down, m_noise, m_decode)
    seconds = (v_encode, v_project, v_output, v_up, v_down, v_noise, v_decode)
    new_weights, new_moments, new_seconds = ([], [], [])
    for w, m, v, g in zip(masters, moments, seconds, shards):
        clipped = g * factor
        moment = BETA_ONE * m + (1.0 - BETA_ONE) * clipped
        variance = BETA_TWO * v + (1.0 - BETA_TWO) * clipped * clipped
        stepped = (
            moment
            / (1.0 - BETA_ONE**STEP)
            / (jnp.sqrt(variance / (1.0 - BETA_TWO**STEP)) + EPSILON)
        )
        new_weights.append(w - LEARN_RATE * (stepped + DECAY_RATE * w))
        new_moments.append(moment)
        new_seconds.append(variance)
    return (
        tuple(new_weights)
        + tuple(new_moments)
        + tuple(new_seconds)
        + (totals[1], totals[2], grad_norm)
    )


def solution(mesh):
    in_specs = (
        P("rep", None, "patch"),
        P("rep", None, "patch"),
        P("rep", None, None, "patch"),
        P("rep", None),
        P("rep", "patch"),
        P("rep", None, "patch"),
        P("rep", "patch", None),
        P("rep", "patch"),
        P("rep", "patch"),
        P("rep", "patch"),
        P(None, ("patch", "rep")),
        P(("patch", "rep"), None),
        P(("patch", "rep"), None),
        P(("patch", "rep"), None),
        P(("patch", "rep"), None),
        P(None, ("patch", "rep")),
        P(("patch", "rep"), None),
        P(None, ("patch", "rep")),
        P(("patch", "rep"), None),
        P(("patch", "rep"), None),
        P(("patch", "rep"), None),
        P(("patch", "rep"), None),
        P(None, ("patch", "rep")),
        P(("patch", "rep"), None),
        P(None, ("patch", "rep")),
        P(("patch", "rep"), None),
        P(("patch", "rep"), None),
        P(("patch", "rep"), None),
        P(("patch", "rep"), None),
        P(None, ("patch", "rep")),
        P(("patch", "rep"), None),
    )
    out_specs = (
        P(None, ("patch", "rep")),
        P(("patch", "rep"), None),
        P(("patch", "rep"), None),
        P(("patch", "rep"), None),
        P(("patch", "rep"), None),
        P(None, ("patch", "rep")),
        P(("patch", "rep"), None),
        P(None, ("patch", "rep")),
        P(("patch", "rep"), None),
        P(("patch", "rep"), None),
        P(("patch", "rep"), None),
        P(("patch", "rep"), None),
        P(None, ("patch", "rep")),
        P(("patch", "rep"), None),
        P(None, ("patch", "rep")),
        P(("patch", "rep"), None),
        P(("patch", "rep"), None),
        P(("patch", "rep"), None),
        P(("patch", "rep"), None),
        P(None, ("patch", "rep")),
        P(("patch", "rep"), None),
        P(),
        P(),
        P(),
    )
    return jax.shard_map(
        on_device, mesh=mesh, in_specs=in_specs, out_specs=out_specs, check_vma=False
    )
```

```python
import functools
import types

import jax
import jax.numpy as jnp
from jax import lax
from jax.experimental import pallas as pl
from jax.experimental.pallas import tpu as pltpu
from jax.sharding import PartitionSpec as P

HEADS = 4
HD = 128
FOUR = 32
NEIGH = 16
STEP = 5


LEARN_RATE = 0.03
BETA_ONE = 0.9
BETA_TWO = 0.95
EPSILON = 1e-08
DECAY_RATE = 0.1
THRESHOLD = 1.0

BOTH = ("patch", "rep")
LOW = jnp.bfloat16
WIDE = jnp.float32
SCALE = HD ** (-0.5)
VMEM_LIMIT = 62 * 2**20


def nn(a, b):
    return lax.dot_general(a, b, (((1,), (0,)), ((), ())), preferred_element_type=WIDE)


def nt(a, b):
    return lax.dot_general(a, b, (((1,), (1,)), ((), ())), preferred_element_type=WIDE)


def tn(a, b):
    return lax.dot_general(a, b, (((0,), (0,)), ((), ())), preferred_element_type=WIDE)


def fourier(level):
    frequency = 0.25 * (jnp.arange(FOUR // 2).astype(jnp.float32) + 1.0)
    angles = jnp.log(level) * frequency
    return jnp.concatenate([jnp.sin(angles), jnp.cos(angles)])


def norm_parts(hidden):
    centre = hidden - jnp.mean(hidden, axis=-1, keepdims=True)
    spread = jnp.mean(centre * centre, axis=-1, keepdims=True)
    inverse = lax.rsqrt(spread + 1e-05)
    return centre * inverse, inverse


MESH = pl.DeviceIdType.MESH
GRID = (4, 2, 2, 2)


def places():
    patch, rep = lax.axis_index("patch"), lax.axis_index("rep")
    z, y, x, c = patch // 2, patch % 2, rep // 2, rep % 2
    sibling = {"patch": patch, "rep": x * 2 + (1 - c)}
    across_x = {"patch": patch, "rep": (1 - x) * 2 + c}
    across_y = {"patch": z * 2 + (1 - y), "rep": rep}
    along_z = [{"patch": ((z + d) % 4) * 2 + y, "rep": rep} for d in range(4)]
    return z, y, x, c, sibling, across_x, across_y, along_z


def greet(others):
    barrier = pltpu.get_barrier_semaphore()
    for other in others:
        pl.semaphore_signal(barrier, inc=1, device_id=other, device_id_type=MESH)
    pl.semaphore_wait(barrier, len(others))


def send(src, dst, sems, index, device):
    copy = pltpu.make_async_remote_copy(
        src_ref=src, dst_ref=dst, send_sem=sems.at[(0,) + index], recv_sem=sems.at[(1,) + index],
        device_id=device, device_id_type=MESH,
    )
    copy.start()
    return copy


def plus(*terms):
    total = terms[0].astype(WIDE)
    for term in terms[1:]:
        total = total + term.astype(WIDE)
    return total


def scatter_scratch(rows, cols):
    h = cols // 2
    return [
        pltpu.VMEM((4, 2, 2, rows, cols), LOW),
        pltpu.VMEM((4, 2, 2, rows, cols), LOW),
        pltpu.VMEM((4, 2, rows, h), LOW),
        pltpu.VMEM((4, 2, rows, h), LOW),
        pltpu.VMEM((4, rows, h), LOW),
        pltpu.VMEM((4, 2, rows, h), LOW),
        pltpu.VMEM((4, 2, rows, h), LOW),
        pltpu.VMEM((4, rows, h), LOW),
        pltpu.VMEM((3, rows, cols), LOW),
        pltpu.VMEM((3, rows, cols), LOW),
    ]


def scatter_kernel(g_one, g_two, extra, out_one, out_two, totals, *scratch):
    z, y, x, c, sibling, across_x, across_y, along_z = places()
    parts = ((g_one, out_one) + scratch[:10], (g_two, out_two) + scratch[10:20])
    board, sems, small = scratch[20:]
    greet([sibling, across_x, across_y] + along_z[1:])
    steps = [(d, (z + d) % 4) for d in (1, 2, 3, 0)]
    sent, first, left, right, left_two, right_two, last = [], {}, {}, {}, {}, {}, {}
    for d, zd in steps:
        for i, (g, out, near, acc, near_l, acc_l, end_l, near_r, acc_r, end_r, going, come) in enumerate(parts):
            first[d, i] = send(g.at[zd, :, :, 1 - c], near.at[zd], sems, (0, d, i), sibling)
    for d, zd in steps:
        for i, (g, out, near, acc, near_l, acc_l, end_l, near_r, acc_r, end_r, going, come) in enumerate(parts):
            h = g.shape[-1] // 2
            first[d, i].wait_recv()
            acc[zd] = plus(g[zd, :, :, c], near[zd]).astype(LOW)
            left[d, i] = send(acc.at[zd, :, 1 - x, :, :h], near_l.at[zd], sems, (1, d, i), across_x)
            right[d, i] = send(acc.at[zd, 1 - y, :, :, h:], near_r.at[zd], sems, (2, d, i), across_y)
    for d, zd in steps:
        for i, (g, out, near, acc, near_l, acc_l, end_l, near_r, acc_r, end_r, going, come) in enumerate(parts):
            h = g.shape[-1] // 2
            left[d, i].wait_recv()
            acc_l[zd] = plus(acc[zd, :, x, :, :h], near_l[zd]).astype(LOW)
            left_two[d, i] = send(acc_l.at[zd, 1 - y], end_l.at[zd], sems, (3, d, i), across_y)
            right[d, i].wait_recv()
            acc_r[zd] = plus(acc[zd, y, :, :, h:], near_r[zd]).astype(LOW)
            right_two[d, i] = send(acc_r.at[zd, 1 - x], end_r.at[zd], sems, (4, d, i), across_x)
    for d, zd in steps:
        for i, (g, out, near, acc, near_l, acc_l, end_l, near_r, acc_r, end_r, going, come) in enumerate(parts):
            h = g.shape[-1] // 2
            left_two[d, i].wait_recv()
            done_l = plus(acc_l[zd, y], end_l[zd])
            right_two[d, i].wait_recv()
            done_r = plus(acc_r[zd, x], end_r[zd])
            if d == 0:
                out[:, :h] = done_l
                out[:, h:] = done_r
            else:
                going[d - 1, :, :h] = done_l.astype(LOW)
                going[d - 1, :, h:] = done_r.astype(LOW)
                last[d, i] = send(going.at[d - 1], come.at[d - 1], sems, (5, d, i), along_z[d])
    squares = jnp.zeros((), WIDE)
    for i, part in enumerate(parts):
        out, come = part[1], part[11]
        for d in (1, 2, 3):
            last[d, i].wait_recv()
        out[...] = plus(out[...], come[0], come[1], come[2])
        squares = squares + jnp.sum(out[...] * out[...])
    row = lax.broadcasted_iota(jnp.int32, extra.shape, 0)
    board[0] = jnp.where(row == 0, squares, extra[...])
    more = []
    for phase, device in enumerate((sibling, across_x, across_y)):
        copy = send(board.at[phase], board.at[4 + phase], small, (phase,), device)
        copy.wait_recv()
        more.append(copy)
        board[phase + 1] = board[phase] + board[4 + phase]
    for d in (1, 2, 3):
        more.append(send(board.at[3], board.at[8 + z], small, (2 + d,), along_z[d]))
    board[8 + z] = board[3]
    for d in (1, 2, 3):
        more[2 + d].wait_recv()
    totals[...] = board[8] + board[9] + board[10] + board[11]
    for group in (first, left, right, left_two, right_two, last):
        for copy in group.values():
            copy.wait_send()
    for copy in more:
        copy.wait_send()


def reduce_scatter(g_one, g_two, extra):
    rows = [g.shape[0] // 32 for g in (g_one, g_two)]
    cols = [g.shape[1] for g in (g_one, g_two)]
    vmem = pl.BlockSpec(memory_space=pltpu.VMEM)
    return pl.pallas_call(
        scatter_kernel,
        out_shape=[jax.ShapeDtypeStruct((r, n), WIDE) for r, n in zip(rows, cols)]
        + [jax.ShapeDtypeStruct(extra.shape, WIDE)],
        in_specs=[vmem] * 3,
        out_specs=[vmem] * 3,
        scratch_shapes=scatter_scratch(rows[0], cols[0]) + scatter_scratch(rows[1], cols[1])
        + [pltpu.VMEM((12,) + extra.shape, WIDE), pltpu.SemaphoreType.DMA((2, 6, 4, 2)),
           pltpu.SemaphoreType.DMA((2, 6))],
        compiler_params=pltpu.CompilerParams(
            collective_id=1, has_side_effects=True, vmem_limit_bytes=48 * 2**20),
    )(g_one.reshape(GRID + (rows[0], cols[0])), g_two.reshape(GRID + (rows[1], cols[1])), extra)


def gather_kernel(a_one, a_two, out_one, out_two, sems, local):
    z, y, x, c, sibling, across_x, across_y, along_z = places()
    greet([sibling, across_x, across_y] + along_z[1:])
    parts = ((a_one, out_one), (a_two, out_two))
    steps = [(d, (z + d) % 4) for d in (0, 1, 2, 3)]
    copies, own, x_one, y_one, x_two, y_two, core = [], [], {}, {}, {}, {}, {}
    planes = {}
    for i, (a, out) in enumerate(parts):
        copy = pltpu.make_async_copy(a, out.at[z, y, x, c], local.at[i])
        copy.start()
        own.append(copy)
        for d in (2, 1, 3):
            planes[d, i] = send(a, out.at[z, y, x, c], sems, (0, d, i), along_z[d])
    for i in range(2):
        own[i].wait()
    for d in range(4):
        zd = (z - d + 4) % 4
        for i, (a, out) in enumerate(parts):
            h = a.shape[-1] // 2
            if d:
                planes[d, i].wait_recv()
            here_l, here_r = out.at[zd, y, x, c, :, :h], out.at[zd, y, x, c, :, h:]
            x_one[d, i] = send(here_l, here_l, sems, (1, d, i), across_x)
            y_one[d, i] = send(here_r, here_r, sems, (2, d, i), across_y)
    for d in range(4):
        zd = (z - d + 4) % 4
        for i, (a, out) in enumerate(parts):
            h = a.shape[-1] // 2
            x_one[d, i].wait_recv()
            both = out.at[zd, y, :, c, :, :h]
            y_two[d, i] = send(both, both, sems, (3, d, i), across_y)
            y_one[d, i].wait_recv()
            both = out.at[zd, :, x, c, :, h:]
            x_two[d, i] = send(both, both, sems, (4, d, i), across_x)
    for d in range(4):
        zd = (z - d + 4) % 4
        for i, (a, out) in enumerate(parts):
            y_two[d, i].wait_recv()
            x_two[d, i].wait_recv()
            plane = out.at[zd, :, :, c]
            core[d, i] = send(plane, plane, sems, (5, d, i), sibling)
    for group in (planes, x_one, y_one, x_two, y_two):
        for copy in group.values():
            copy.wait_send()
    for copy in core.values():
        copy.wait()


def all_gather(a_one, a_two):
    shapes = [a.shape for a in (a_one, a_two)]
    outs = pl.pallas_call(
        gather_kernel,
        out_shape=[jax.ShapeDtypeStruct(GRID + s, LOW) for s in shapes],
        in_specs=[pl.BlockSpec(memory_space=pltpu.VMEM)] * 2,
        out_specs=[pl.BlockSpec(memory_space=pl.ANY)] * 2,
        scratch_shapes=[pltpu.SemaphoreType.DMA((2, 6, 4, 2)), pltpu.SemaphoreType.DMA((2,))],
        compiler_params=pltpu.CompilerParams(
            collective_id=2, has_side_effects=True, vmem_limit_bytes=32 * 2**20),
    )(a_one, a_two)
    return [o.reshape(32 * s[0], s[1]) for o, s in zip(outs, shapes)]


HALF_COLS = 128


def net_scratch(nodes, halo, pixels, width, hidden, kept):
    near = nodes + 2 * halo
    return dict(
        owner_hot=pltpu.VMEM((nodes, pixels), LOW),
        node_hot=pltpu.VMEM((nodes, pixels), LOW),
        bias=pltpu.VMEM((near, nodes), WIDE),
        send_hot=pltpu.VMEM((2 * halo, nodes), LOW),
        inv_count=pltpu.VMEM((nodes, 1), WIDE),
        sums=pltpu.VMEM((2 * nodes, 2 * HALF_COLS), LOW),
        wave=pltpu.VMEM((2, 4, width), WIDE),
        d_wave=pltpu.VMEM((2, 4, width), WIDE),
        start=pltpu.VMEM((nodes, width), WIDE),
        unit_one=pltpu.VMEM((2, nodes, width), LOW),
        inv_one=pltpu.VMEM((2, nodes, 1), WIDE),
        normed=pltpu.VMEM((2 * near, width), LOW),
        queries=pltpu.VMEM((2, nodes, width), LOW),
        extended=pltpu.VMEM((2, near, 2 * width), LOW),
        probs=pltpu.VMEM((2, HEADS, near, nodes), LOW),
        mixed=pltpu.VMEM((2 * nodes, width), LOW),
        unit_two=pltpu.VMEM((2, nodes, width), LOW),
        inv_two=pltpu.VMEM((2, nodes, 1), WIDE),
        second=pltpu.VMEM((2 * nodes, width), LOW),
        gated=pltpu.VMEM((2 * nodes, hidden), LOW),
        slope=pltpu.VMEM((2 * nodes, hidden), LOW),
        final=pltpu.VMEM((2 * nodes, width), LOW),
        taken=pltpu.VMEM((2 * nodes, HALF_COLS), LOW),
        d_branch=pltpu.VMEM((2 * nodes, width), LOW),
        d_attn=pltpu.VMEM((2 * nodes, width), LOW),
        d_queries=pltpu.VMEM((2 * nodes, width), LOW),
        d_keyval=pltpu.VMEM((2 * near, 2 * width), LOW),
        d_summed=pltpu.VMEM((2 * nodes, width), LOW),
        d_mixed=pltpu.VMEM((nodes, width), LOW),
        d_scores=pltpu.VMEM((near, nodes), LOW),
        scores=pltpu.VMEM((near, nodes), WIDE),
        d_normed=pltpu.VMEM((nodes, width), WIDE),
        outgoing=pltpu.VMEM((4, 2 * halo, width), LOW),
        returned=pltpu.VMEM((2, 2 * halo, width), LOW),
        state=pltpu.VMEM((kept, pixels), WIDE),
        aim=pltpu.VMEM((kept, pixels), WIDE),
        extra=pltpu.VMEM((kept, pixels), WIDE),
        low_state=pltpu.VMEM((HALF_COLS, pixels), LOW),
        staged=pltpu.VMEM((2, 256, hidden), LOW),
        loads=pltpu.SemaphoreType.DMA((4,)),
        stores=pltpu.SemaphoreType.DMA((2,)),
        links=pltpu.SemaphoreType.DMA((2, 4, 2)),
    )


def loop(count, body):
    def step(i, carry):
        body(i)
        return carry

    lax.fori_loop(0, count, step, 0)


def block(index, size):
    return pl.ds(pl.multiple_of(index * size, size), size)


def net_kernel(names, chan, numbers, counts, previous, noisy, target, noise, owners, decode_idx, near_idx, send_idx,
               waves, w_wide, w_down, g_wide, g_down, loss, *scratch):
    r = types.SimpleNamespace(**dict(zip(names, scratch)))
    nodes, pixels = near_idx.shape[1], owners.shape[1]
    halo = send_idx.shape[0] // 2
    near = nodes + 2 * halo
    width, hidden = w_down.shape[1], w_down.shape[0]
    at = [0, 3 * width, 4 * width, 4 * width + hidden, 4 * width + hidden + 256, 4 * width + hidden + 384]
    tile = 1024
    tiles = pixels // tile
    patches = lax.axis_size("patch")
    me = lax.axis_index("patch")
    lower, upper = {"patch": (me + patches - 1) % patches}, {"patch": (me + 1) % patches}
    barrier = pltpu.get_barrier_semaphore()
    for other in (lower, upper):
        pl.semaphore_signal(barrier, inc=1, device_id=other, device_id_type=MESH)

    def load(src, dst, slot):
        copy = pltpu.make_async_copy(src, dst, r.loads.at[slot])
        copy.start()
        return copy

    pairs = ((previous, r.low_state), (noisy, r.state), (target, r.aim), (noise, r.extra))
    loads = [load(src, dst, slot) for slot, (src, dst) in enumerate(pairs)]
    rows_used = r.state.shape[0]

    level = [numbers[4 * s] for s in range(2)]
    c_in = [numbers[4 * s + 1] for s in range(2)]
    c_skip = [numbers[4 * s + 2] for s in range(2)]
    c_out = [numbers[4 * s + 3] for s in range(2)]

    noise_block = w_wide[:, at[5] : at[5] + 128].astype(WIDE).reshape(32, 16, 128)
    lane = lax.broadcasted_iota(jnp.int32, (1, 128), 1)
    for s in range(2):
        parts = jnp.sum(noise_block * waves[s][None], axis=1)
        both = parts + pltpu.roll(parts, 64, 1)
        for k in range(16):
            piece = jnp.where(lane < 64, both[2 * k : 2 * k + 1], both[2 * k + 1 : 2 * k + 2])
            r.wave[s, k // 4 : k // 4 + 1, (k % 4) * 128 : (k % 4 + 1) * 128] = piece

    def build_hot(t):
        cols = block(t, tile)
        place = lax.broadcasted_iota(jnp.int32, (1, tile), 1) + t * tile
        own = jnp.where(place < counts[1], owners[:, cols], -1)
        three = [decode_idx[i : i + 1, cols] for i in range(3)]

        def rows(b):
            row = lax.broadcasted_iota(jnp.int32, (16, tile), 0) + b * 16
            r.owner_hot[block(b, 16), cols] = (row == own).astype(WIDE).astype(LOW)
            total = sum((row == idx).astype(WIDE) for idx in three)
            r.node_hot[block(b, 16), cols] = total.astype(LOW)

        loop(nodes // 16, rows)

    loop(tiles, build_hot)

    def build_bias(b):
        rows = block(b, 32)
        place = lax.broadcasted_iota(jnp.int32, (32, nodes), 0) + b * 32
        listed = jnp.zeros((32, nodes), WIDE)
        for j in range(1, NEIGH):
            listed = listed + (near_idx[j : j + 1] == place).astype(WIDE)
        listed = jnp.where((place >= nodes) | (place < counts[0]), listed, 0.0)
        listed = listed + (near_idx[0:1] == place).astype(WIDE)
        r.bias[rows] = jnp.where(listed > 0.0, jnp.log(jnp.maximum(listed, 1.0)), -1e30)

    loop(near // 32, build_bias)
    r.send_hot[...] = (
        lax.broadcasted_iota(jnp.int32, (2 * halo, nodes), 1) == send_idx[...]
    ).astype(WIDE).astype(LOW)

    loads[0].wait()
    summed = nt(r.owner_hot[...], r.low_state[...])
    channel = lax.broadcasted_iota(jnp.int32, (nodes, HALF_COLS), 1)
    total = jnp.sum(jnp.where(channel == chan, summed, 0.0), axis=1, keepdims=True)
    r.inv_count[...] = 1.0 / jnp.maximum(total, 1.0)
    summed = jnp.where(channel < chan, summed, 0.0).astype(LOW)
    r.sums[:nodes, :HALF_COLS] = summed
    r.sums[nodes:, :HALF_COLS] = summed
    for copy in loads[1:]:
        copy.wait()
    pl.semaphore_wait(barrier, 2)

    def pass_on(number, first, second):
        copies = []
        for i, (dst, device) in enumerate(((first, lower), (second, upper))):
            copy = pltpu.make_async_remote_copy(
                src_ref=r.outgoing.at[number, i * halo : (i + 1) * halo], dst_ref=dst,
                send_sem=r.links.at[0, number, i], recv_sem=r.links.at[1, number, i],
                device_id=device, device_id_type=MESH,
            )
            copy.start()
            copies.append(copy)
        return copies

    def encode(s):
        rows = slice(s * nodes, (s + 1) * nodes)
        r.low_state[:rows_used] = (r.state[...] * c_in[s]).astype(LOW)
        r.sums[rows, HALF_COLS:] = nt(r.owner_hot[...], r.low_state[...]).astype(LOW)
        r.start[...] = nt(r.sums[rows], w_wide[:, at[3] : at[4]]) * r.inv_count[...]

        def norm(b):
            part = block(b, 64)
            unit, inverse = norm_parts(r.start[part])
            r.unit_one[s, part] = unit.astype(LOW)
            r.inv_one[s, part] = inverse
            scaled = unit * (1.0 + r.wave[s, 0:1]) + r.wave[s, 1:2]
            r.normed[pl.ds(pl.multiple_of(s * nodes + b * 64, 64), 64)] = scaled.astype(LOW)

        loop(nodes // 64, norm)
        normed = r.normed[rows]
        r.outgoing[s] = nn(r.send_hot[...], normed).astype(LOW)
        first = 2 * nodes + 2 * halo * s
        copies = pass_on(s, r.normed.at[first + halo : first + 2 * halo], r.normed.at[first : first + halo])
        r.queries[s] = nn(normed, w_wide[:, :width]).astype(LOW)
        r.extended[s, :nodes] = nn(normed, w_wide[:, width : 3 * width]).astype(LOW)
        return copies

    def attend(s, copies):
        rows = slice(s * nodes, (s + 1) * nodes)
        for copy in copies:
            copy.wait()
        first = 2 * nodes + 2 * halo * s
        r.extended[s, nodes:] = nn(r.normed[first : first + 2 * halo], w_wide[:, width : 3 * width]).astype(LOW)
        for head in range(HEADS):
            cols = slice(head * HD, (head + 1) * HD)
            r.scores[...] = nt(r.extended[s, :, cols], r.queries[s, :, cols])

            def soft(b):
                part = block(b, 128)
                top = jnp.full((8, 128), -1e30, WIDE)
                for k in range(near // 64):
                    rows = slice(k * 64, (k + 1) * 64)
                    score = r.scores[rows, part] * SCALE + r.bias[rows, part]
                    r.scores[rows, part] = score
                    top = jnp.maximum(top, jnp.max(score.reshape(8, 8, 128), axis=0))
                top = jnp.max(top, axis=0, keepdims=True)
                total = jnp.zeros((8, 128), WIDE)
                for k in range(near // 64):
                    rows = slice(k * 64, (k + 1) * 64)
                    weight = jnp.exp(r.scores[rows, part] - top)
                    r.scores[rows, part] = weight
                    total = total + jnp.sum(weight.reshape(8, 8, 128), axis=0)
                total = 1.0 / jnp.sum(total, axis=0, keepdims=True)
                for k in range(near // 64):
                    rows = slice(k * 64, (k + 1) * 64)
                    r.probs[s, head, rows, part] = (r.scores[rows, part] * total).astype(LOW)

            loop(nodes // 128, soft)
            values = r.extended[s, :, width + head * HD : width + (head + 1) * HD]
            r.mixed[rows, cols] = tn(values, r.probs[s, head]).T.astype(LOW)
        r.start[...] += nn(r.mixed[rows], w_wide[:, at[1] : at[2]])

        def norm(b):
            part = block(b, 64)
            unit, inverse = norm_parts(r.start[part])
            r.unit_two[s, part] = unit.astype(LOW)
            r.inv_two[s, part] = inverse
            scaled = unit * (1.0 + r.wave[s, 2:3]) + r.wave[s, 3:4]
            r.second[pl.ds(pl.multiple_of(s * nodes + b * 64, 64), 64)] = scaled.astype(LOW)

        loop(nodes // 64, norm)

        def feed(j):
            cols = block(j, 256)
            upward = nn(r.second[rows], w_wide[:, pl.ds(pl.multiple_of(at[2] + j * 256, 256), 256)])
            gate = 1.0 / (1.0 + jnp.exp(-upward))
            r.gated[rows, cols] = (upward * gate).astype(LOW)
            r.slope[rows, cols] = (gate * (1.0 + upward * (1.0 - gate))).astype(LOW)

        loop(hidden // 256, feed)
        r.final[rows] = (r.start[...] + nn(r.gated[rows], w_down[...])).astype(LOW)
        out = nn(r.final[rows], w_wide[:, at[4] : at[5]]) * (1.0 / 3.0)
        return out.T.astype(LOW)[:rows_used]

    def gradient(s):
        rows = slice(s * nodes, (s + 1) * nodes)
        taken = (nt(r.node_hot[...], r.low_state[...]) * (1.0 / 3.0)).astype(LOW)
        r.taken[rows] = taken
        d_final = nt(taken, w_wide[:, at[4] : at[5]])
        r.start[...] = d_final
        r.d_branch[rows] = d_final.astype(LOW)

        def feed(j):
            cols = block(j, 256)
            d_gated = nt(r.d_branch[rows], w_down[cols])
            r.slope[rows, cols] = (d_gated * r.slope[rows, cols].astype(WIDE)).astype(LOW)

        loop(hidden // 256, feed)
        r.d_normed[...] = nt(r.slope[rows], w_wide[:, at[2] : at[3]])
        norm_gradient(s, r.unit_two, r.inv_two, 2)
        r.d_attn[rows] = r.start[...].astype(LOW)
        r.d_mixed[...] = nt(r.d_attn[rows], w_wide[:, at[1] : at[2]]).astype(LOW)
        first = 2 * nodes + 2 * halo * s
        far = slice(first, first + 2 * halo)
        for head in range(HEADS):
            cols = slice(head * HD, (head + 1) * HD)
            after = slice(width + head * HD, width + (head + 1) * HD)
            r.scores[...] = nt(r.extended[s, :, after], r.d_mixed[:, cols])

            def soft(b):
                part = block(b, 128)
                total = jnp.zeros((8, 128), WIDE)
                for k in range(near // 64):
                    rows = slice(k * 64, (k + 1) * 64)
                    slope = r.probs[s, head, rows, part].astype(WIDE) * r.scores[rows, part]
                    total = total + jnp.sum(slope.reshape(8, 8, 128), axis=0)
                total = jnp.sum(total, axis=0, keepdims=True)
                for k in range(near // 64):
                    rows = slice(k * 64, (k + 1) * 64)
                    slope = r.probs[s, head, rows, part].astype(WIDE) * (r.scores[rows, part] - total)
                    r.d_scores[rows, part] = (slope * SCALE).astype(LOW)

            loop(nodes // 128, soft)
            d_values = nn(r.probs[s, head], r.d_mixed[:, cols]).astype(LOW)
            d_keys = nn(r.d_scores[...], r.queries[s, :, cols]).astype(LOW)
            r.d_keyval[rows, after] = d_values[:nodes]
            r.d_keyval[far, after] = d_values[nodes:]
            r.d_keyval[rows, cols] = d_keys[:nodes]
            r.d_keyval[far, cols] = d_keys[nodes:]
            r.d_queries[rows, cols] = tn(r.extended[s, :, cols], r.d_scores[...]).T.astype(LOW)
        r.outgoing[2 + s] = nt(r.d_keyval[far], w_wide[:, width : 3 * width]).astype(LOW)
        copies = pass_on(2 + s, r.returned.at[s, halo:], r.returned.at[s, :halo])
        r.d_normed[...] = nt(r.d_queries[rows], w_wide[:, :width]) + nt(r.d_keyval[rows], w_wide[:, width : 3 * width])
        return copies

    def norm_gradient(s, units, inverses, which):
        r.d_wave[s, which : which + 2] = jnp.zeros((2, width), WIDE)

        def norm(b):
            part = block(b, 64)
            unit = units[s, part].astype(WIDE)
            d_out = r.d_normed[part]
            d_scale = jnp.sum(d_out * unit, axis=0, keepdims=True)
            d_shift = jnp.sum(d_out, axis=0, keepdims=True)
            r.d_wave[s, which : which + 1] += d_scale
            r.d_wave[s, which + 1 : which + 2] += d_shift
            d_unit = d_out * (1.0 + r.wave[s, which : which + 1])
            along = jnp.mean(d_unit * unit, axis=-1, keepdims=True)
            d_hidden = d_unit - jnp.mean(d_unit, axis=-1, keepdims=True) - unit * along
            r.start[part] += inverses[s, part] * d_hidden

        loop(nodes // 64, norm)

    def absorb(s, copies):
        rows = slice(s * nodes, (s + 1) * nodes)
        for copy in copies:
            copy.wait()
        r.d_normed[...] += tn(r.send_hot[...], r.returned[s])
        norm_gradient(s, r.unit_one, r.inv_one, 0)
        r.d_summed[rows] = (r.start[...] * r.inv_count[...]).astype(LOW)

    copies = encode(0)
    nodes_out = attend(0, copies)

    def decode_one(t):
        cols = block(t, tile)
        out = nn(nodes_out, r.node_hot[:, cols])
        r.state[:, cols] = c_skip[0] * r.state[:, cols] + c_out[0] * out + level[1] * r.extra[:, cols]

    loop(tiles, decode_one)
    copies = encode(1)
    nodes_out_two = attend(1, copies)
    loss[...] = jnp.zeros(loss.shape, WIDE)

    def decode_two(t):
        cols = block(t, tile)
        out = nn(nodes_out_two, r.node_hot[:, cols])
        place = lax.broadcasted_iota(jnp.int32, (1, tile), 1) + t * tile
        error = c_skip[1] * r.state[:, cols] + c_out[1] * out - r.aim[:, cols]
        error = jnp.where(place < counts[1], error, 0.0)
        loss[...] += jnp.sum(error * error)
        r.extra[:, cols] = 2.0 * error
        r.low_state[:rows_used, cols] = (c_out[1] * 2.0 * error).astype(LOW)

    loop(tiles, decode_two)
    copies = gradient(1)
    absorb(1, copies)
    d_nodes = nn(r.d_summed[nodes:], w_wide[:, at[3] + HALF_COLS : at[4]])
    d_nodes = d_nodes.T.astype(LOW)[:rows_used]

    def into_one(t):
        cols = block(t, tile)
        d_noisy = c_skip[1] * r.extra[:, cols] + c_in[1] * nn(d_nodes, r.owner_hot[:, cols])
        r.low_state[:rows_used, cols] = (c_out[0] * d_noisy).astype(LOW)

    loop(tiles, into_one)
    copies = gradient(0)

    stores = [None, None]

    def store(slot, dst, cols):
        copy = pltpu.make_async_copy(r.staged.at[slot, :, :cols], dst, r.stores.at[slot])
        copy.start()
        stores[slot] = copy

    done = [0]

    def product(left, i, right, out, first):
        slot, cols = done[0] % 2, right.shape[1]
        done[0] += 1
        if stores[slot] is not None:
            stores[slot].wait()
        r.staged[slot, :, :cols] = tn(left[:, i * 256 : (i + 1) * 256], right[...]).astype(LOW)
        store(slot, out.at[i * 256 : (i + 1) * 256, first : first + cols], cols)

    for i in range(hidden // 256):
        product(r.gated, i, r.d_branch, g_down, 0)
    for i in range(width // 256):
        product(r.second, i, r.slope, g_wide, at[2])
        product(r.mixed, i, r.d_attn, g_wide, at[1])
        product(r.final, i, r.taken, g_wide, at[4])
        product(r.normed, i, r.d_keyval, g_wide, width)
        product(r.normed.at[: 2 * nodes], i, r.d_queries, g_wide, 0)
    absorb(0, copies)
    for i in range(width // 256):
        product(r.d_summed, i, r.sums, g_wide, at[3])
    for i in range(2):
        slot = (done[0] + i) % 2
        stores[slot].wait()
        total = jnp.zeros((16, 16, 128), WIDE)
        for s in range(2):
            pieces = []
            for k in range(8 * i, 8 * i + 8):
                piece = r.d_wave[s, k // 4 : k // 4 + 1, (k % 4) * 128 : (k % 4 + 1) * 128]
                turned = pltpu.roll(piece, 64, 1)
                pieces.append(jnp.where(lane < 64, piece, turned))
                pieces.append(jnp.where(lane < 64, turned, piece))
            rows = jnp.concatenate(pieces, axis=0)
            total = total + rows[:, None, :] * waves[s][None]
        r.staged[slot, :, :128] = total.reshape(256, 128).astype(LOW)
        store(slot, g_wide.at[i * 256 : (i + 1) * 256, at[5] : at[5] + 128], 128)
    for copy in stores:
        copy.wait()


def run_net(chan, numbers, counts, previous, noisy, target, noise, owners, decode_idx, near_idx, send_idx, waves, w_wide, w_down):
    nodes, pixels = near_idx.shape[1], owners.shape[1]
    hidden, width = w_down.shape
    scratch = net_scratch(nodes, send_idx.shape[0] // 2, pixels, width, hidden, noisy.shape[0])
    vmem, smem = pl.BlockSpec(memory_space=pltpu.VMEM), pl.BlockSpec(memory_space=pltpu.SMEM)
    hbm = pl.BlockSpec(memory_space=pl.ANY)
    return pl.pallas_call(
        functools.partial(net_kernel, tuple(scratch), chan),
        out_shape=[jax.ShapeDtypeStruct(w_wide.shape, LOW), jax.ShapeDtypeStruct(w_down.shape, LOW),
                   jax.ShapeDtypeStruct((8, 128), WIDE)],
        in_specs=[smem] * 2 + [hbm] * 4 + [vmem] * 7,
        out_specs=[hbm, hbm, vmem],
        scratch_shapes=list(scratch.values()),
        compiler_params=pltpu.CompilerParams(
            collective_id=3, has_side_effects=True, vmem_limit_bytes=VMEM_LIMIT),
    )(numbers, counts, previous, noisy, target, noise, owners, decode_idx, near_idx, send_idx, waves, w_wide, w_down)


def fill(array, columns):
    return jnp.pad(array, ((0, 0), (0, columns - array.shape[1])))


def pack(encode, project, output, up, decode):
    half = encode.shape[0] // 2
    return [project, output, up, fill(encode[:half].T, HALF_COLS), fill(encode[half:].T, HALF_COLS),
            fill(decode, HALF_COLS)]


def on_device(
    previous_state, target_state, noise_draws, noise_level, pixel_owner, mesh_to_grid, neighbours, halo_send,
    node_count, pixel_count, w_encode, w_project, w_output, w_up, w_down, w_noise, w_decode,
    m_encode, m_project, m_output, m_up, m_down, m_noise, m_decode,
    v_encode, v_project, v_output, v_up, v_down, v_noise, v_decode,
):
    width = w_project.shape[1] // 3
    hidden = w_up.shape[1]
    channels = previous_state.shape[1]
    rows = w_project.shape[0]
    small_slice = lax.axis_size("patch") == 8 and lax.axis_size("rep") == 4
    packed = pack(*(w.astype(LOW) for w in (w_encode, w_project, w_output, w_up, w_decode)))
    low_noise = w_noise.astype(LOW)
    if small_slice:
        packed = jnp.concatenate(packed + [low_noise.reshape(rows, HALF_COLS)], axis=1)
        all_wide, all_down = all_gather(packed, w_down.astype(LOW))
    else:
        all_wide = lax.all_gather(jnp.concatenate(packed, axis=1), BOTH, axis=0, tiled=True)
        all_down = lax.all_gather(w_down.astype(LOW), BOTH, axis=0, tiled=True)
        noise = lax.all_gather(low_noise, BOTH, axis=1, tiled=True).reshape(FOUR, -1, 64)
        all_wide = jnp.concatenate([all_wide, noise.transpose(1, 0, 2).reshape(width, HALF_COLS)], axis=1)
    at = [0, 3 * width, 4 * width, 4 * width + hidden, 4 * width + hidden + 256, 4 * width + hidden + 384]

    levels = noise_level[0]
    pixels = pixel_owner.shape[1]
    padding = ((0, -channels % 16), (0, 0))
    previous = jnp.concatenate([previous_state[0], jnp.ones((1, pixels), WIDE)], axis=0).astype(LOW)
    previous = jnp.pad(previous, ((0, HALF_COLS - channels - 1), (0, 0)))
    target = jnp.pad(target_state[0], padding)
    noisy = jnp.pad(target_state[0] + levels[0] * noise_draws[0, 0], padding)
    noise_two = jnp.pad(noise_draws[0, 1], padding)
    c_in = lax.rsqrt(levels * levels + 1.0)
    numbers = jnp.stack([levels, c_in, 1.0 / (levels * levels + 1.0), levels * c_in], axis=1).reshape(8)
    counts = jnp.concatenate([node_count[0], pixel_count[0]])
    waves = jnp.stack([fourier(levels[i]).reshape(FOUR // 2, 2) for i in range(2)])
    waves = jnp.repeat(waves, 64, axis=2)
    g_wide, g_down, loss_local = run_net(
        channels, numbers, counts, previous, noisy, target, noise_two, pixel_owner, mesh_to_grid[0], neighbours[0].T,
        halo_send.reshape(-1, 1), waves, all_wide, all_down,
    )
    count_local = (channels * jnp.minimum(pixel_count[0, 0], pixels)).astype(WIDE)
    if small_slice:
        row = lax.broadcasted_iota(jnp.int32, (8, 128), 0)
        extra = jnp.where(row == 1, loss_local, 0.0) + jnp.where(row == 2, count_local, 0.0)
        s_wide, s_down, totals = reduce_scatter(g_wide, g_down, extra)
        totals = totals[:3, 0]
        s_noise = s_wide[:, at[5] :].reshape(FOUR, -1)
    else:
        g_noise = g_wide[:, at[5] :].reshape(-1, FOUR, 64).transpose(1, 0, 2).reshape(FOUR, -1)
        s_wide = lax.psum_scatter(g_wide[:, : at[5]].astype(WIDE), BOTH, scatter_dimension=0, tiled=True)
        s_down = lax.psum_scatter(g_down.astype(WIDE), BOTH, scatter_dimension=0, tiled=True)
        s_noise = lax.psum_scatter(g_noise.astype(WIDE), BOTH, scatter_dimension=1, tiled=True)
        squares = jnp.sum(s_wide * s_wide) + jnp.sum(s_down * s_down) + jnp.sum(s_noise * s_noise)
        totals = lax.psum((squares, loss_local[0, 0], count_local), BOTH)
    second = at[3] + HALF_COLS
    shards = (
        jnp.concatenate([s_wide[:, at[3] : at[3] + channels], s_wide[:, second : second + channels]], axis=1).T,
        s_wide[:, : at[1]],
        s_wide[:, at[1] : at[2]],
        s_wide[:, at[2] : at[3]],
        s_down,
        s_noise,
        s_wide[:, at[4] : at[4] + channels],
    )
    grad_norm = jnp.sqrt(totals[0])
    factor = THRESHOLD / jnp.maximum(grad_norm, THRESHOLD)
    masters = (w_encode, w_project, w_output, w_up, w_down, w_noise, w_decode)
    moments = (m_encode, m_project, m_output, m_up, m_down, m_noise, m_decode)
    seconds = (v_encode, v_project, v_output, v_up, v_down, v_noise, v_decode)
    new_weights, new_moments, new_seconds = ([], [], [])
    for w, m, v, g in zip(masters, moments, seconds, shards):
        clipped = g * factor
        moment = BETA_ONE * m + (1.0 - BETA_ONE) * clipped
        variance = BETA_TWO * v + (1.0 - BETA_TWO) * clipped * clipped
        stepped = (
            moment
            / (1.0 - BETA_ONE**STEP)
            / (jnp.sqrt(variance / (1.0 - BETA_TWO**STEP)) + EPSILON)
        )
        new_weights.append(w - LEARN_RATE * (stepped + DECAY_RATE * w))
        new_moments.append(moment)
        new_seconds.append(variance)
    return (
        tuple(new_weights)
        + tuple(new_moments)
        + tuple(new_seconds)
        + (totals[1], totals[2], grad_norm)
    )


def solution(mesh):
    in_specs = (
        P("rep", None, "patch"),
        P("rep", None, "patch"),
        P("rep", None, None, "patch"),
        P("rep", None),
        P("rep", "patch"),
        P("rep", None, "patch"),
        P("rep", "patch", None),
        P("rep", "patch"),
        P("rep", "patch"),
        P("rep", "patch"),
        P(None, ("patch", "rep")),
        P(("patch", "rep"), None),
        P(("patch", "rep"), None),
        P(("patch", "rep"), None),
        P(("patch", "rep"), None),
        P(None, ("patch", "rep")),
        P(("patch", "rep"), None),
        P(None, ("patch", "rep")),
        P(("patch", "rep"), None),
        P(("patch", "rep"), None),
        P(("patch", "rep"), None),
        P(("patch", "rep"), None),
        P(None, ("patch", "rep")),
        P(("patch", "rep"), None),
        P(None, ("patch", "rep")),
        P(("patch", "rep"), None),
        P(("patch", "rep"), None),
        P(("patch", "rep"), None),
        P(("patch", "rep"), None),
        P(None, ("patch", "rep")),
        P(("patch", "rep"), None),
    )
    out_specs = (
        P(None, ("patch", "rep")),
        P(("patch", "rep"), None),
        P(("patch", "rep"), None),
        P(("patch", "rep"), None),
        P(("patch", "rep"), None),
        P(None, ("patch", "rep")),
        P(("patch", "rep"), None),
        P(None, ("patch", "rep")),
        P(("patch", "rep"), None),
        P(("patch", "rep"), None),
        P(("patch", "rep"), None),
        P(("patch", "rep"), None),
        P(None, ("patch", "rep")),
        P(("patch", "rep"), None),
        P(None, ("patch", "rep")),
        P(("patch", "rep"), None),
        P(("patch", "rep"), None),
        P(("patch", "rep"), None),
        P(("patch", "rep"), None),
        P(None, ("patch", "rep")),
        P(("patch", "rep"), None),
        P(),
        P(),
        P(),
    )
    return jax.shard_map(
        on_device, mesh=mesh, in_specs=in_specs, out_specs=out_specs, check_vma=False
    )
```

```python
import functools
import types

import jax
import jax.numpy as jnp
from jax import lax
from jax.experimental import pallas as pl
from jax.experimental.pallas import tpu as pltpu
from jax.sharding import PartitionSpec as P

HEADS = 4
HD = 128
FOUR = 32
NEIGH = 16
STEP = 5


LEARN_RATE = 0.03
BETA_ONE = 0.9
BETA_TWO = 0.95
EPSILON = 1e-08
DECAY_RATE = 0.1
THRESHOLD = 1.0

BOTH = ("patch", "rep")
LOW = jnp.bfloat16
WIDE = jnp.float32
SCALE = HD ** (-0.5)
VMEM_LIMIT = 62 * 2**20


def nn(a, b):
    return lax.dot_general(a, b, (((1,), (0,)), ((), ())), preferred_element_type=WIDE)


def nt(a, b):
    return lax.dot_general(a, b, (((1,), (1,)), ((), ())), preferred_element_type=WIDE)


def tn(a, b):
    return lax.dot_general(a, b, (((0,), (0,)), ((), ())), preferred_element_type=WIDE)


def fourier(level):
    frequency = 0.25 * (jnp.arange(FOUR // 2).astype(jnp.float32) + 1.0)
    angles = jnp.log(level) * frequency
    return jnp.concatenate([jnp.sin(angles), jnp.cos(angles)])


def norm_parts(hidden):
    centre = hidden - jnp.mean(hidden, axis=-1, keepdims=True)
    spread = jnp.mean(centre * centre, axis=-1, keepdims=True)
    inverse = lax.rsqrt(spread + 1e-05)
    return centre * inverse, inverse


MESH = pl.DeviceIdType.MESH
GRID = (4, 2, 2, 2)


def places():
    patch, rep = lax.axis_index("patch"), lax.axis_index("rep")
    z, y, x, c = patch // 2, patch % 2, rep // 2, rep % 2
    sibling = {"patch": patch, "rep": x * 2 + (1 - c)}
    across_x = {"patch": patch, "rep": (1 - x) * 2 + c}
    across_y = {"patch": z * 2 + (1 - y), "rep": rep}
    along_z = [{"patch": ((z + d) % 4) * 2 + y, "rep": rep} for d in range(4)]
    return z, y, x, c, sibling, across_x, across_y, along_z


def greet(others):
    barrier = pltpu.get_barrier_semaphore()
    for other in others:
        pl.semaphore_signal(barrier, inc=1, device_id=other, device_id_type=MESH)
    pl.semaphore_wait(barrier, len(others))


def send(src, dst, sems, index, device):
    copy = pltpu.make_async_remote_copy(
        src_ref=src, dst_ref=dst, send_sem=sems.at[(0,) + index], recv_sem=sems.at[(1,) + index],
        device_id=device, device_id_type=MESH,
    )
    copy.start()
    return copy


def plus(*terms):
    total = terms[0].astype(WIDE)
    for term in terms[1:]:
        total = total + term.astype(WIDE)
    return total


def scatter_scratch(rows, cols):
    h = cols // 2
    return [
        pltpu.VMEM((4, 2, 2, rows, cols), LOW),
        pltpu.VMEM((4, 2, 2, rows, cols), LOW),
        pltpu.VMEM((4, 2, rows, h), LOW),
        pltpu.VMEM((4, 2, rows, h), LOW),
        pltpu.VMEM((4, rows, h), LOW),
        pltpu.VMEM((4, 2, rows, h), LOW),
        pltpu.VMEM((4, 2, rows, h), LOW),
        pltpu.VMEM((4, rows, h), LOW),
        pltpu.VMEM((3, rows, cols), LOW),
        pltpu.VMEM((3, rows, cols), LOW),
    ]


def scatter_kernel(g_one, g_two, extra, out_one, out_two, totals, *scratch):
    z, y, x, c, sibling, across_x, across_y, along_z = places()
    parts = ((g_one, out_one) + scratch[:10], (g_two, out_two) + scratch[10:20])
    board, sems, small = scratch[20:]
    greet([sibling, across_x, across_y] + along_z[1:])
    steps = [(d, (z + d) % 4) for d in (1, 2, 3, 0)]
    sent, first, left, right, left_two, right_two, last = [], {}, {}, {}, {}, {}, {}
    for d, zd in steps:
        for i, (g, out, near, acc, near_l, acc_l, end_l, near_r, acc_r, end_r, going, come) in enumerate(parts):
            first[d, i] = send(g.at[zd, :, :, 1 - c], near.at[zd], sems, (0, d, i), sibling)
    for d, zd in steps:
        for i, (g, out, near, acc, near_l, acc_l, end_l, near_r, acc_r, end_r, going, come) in enumerate(parts):
            h = g.shape[-1] // 2
            first[d, i].wait_recv()
            acc[zd] = plus(g[zd, :, :, c], near[zd]).astype(LOW)
            left[d, i] = send(acc.at[zd, :, 1 - x, :, :h], near_l.at[zd], sems, (1, d, i), across_x)
            right[d, i] = send(acc.at[zd, 1 - y, :, :, h:], near_r.at[zd], sems, (2, d, i), across_y)
    for d, zd in steps:
        for i, (g, out, near, acc, near_l, acc_l, end_l, near_r, acc_r, end_r, going, come) in enumerate(parts):
            h = g.shape[-1] // 2
            left[d, i].wait_recv()
            acc_l[zd] = plus(acc[zd, :, x, :, :h], near_l[zd]).astype(LOW)
            left_two[d, i] = send(acc_l.at[zd, 1 - y], end_l.at[zd], sems, (3, d, i), across_y)
            right[d, i].wait_recv()
            acc_r[zd] = plus(acc[zd, y, :, :, h:], near_r[zd]).astype(LOW)
            right_two[d, i] = send(acc_r.at[zd, 1 - x], end_r.at[zd], sems, (4, d, i), across_x)
    for d, zd in steps:
        for i, (g, out, near, acc, near_l, acc_l, end_l, near_r, acc_r, end_r, going, come) in enumerate(parts):
            h = g.shape[-1] // 2
            left_two[d, i].wait_recv()
            done_l = plus(acc_l[zd, y], end_l[zd])
            right_two[d, i].wait_recv()
            done_r = plus(acc_r[zd, x], end_r[zd])
            if d == 0:
                out[:, :h] = done_l
                out[:, h:] = done_r
            else:
                going[d - 1, :, :h] = done_l.astype(LOW)
                going[d - 1, :, h:] = done_r.astype(LOW)
                last[d, i] = send(going.at[d - 1], come.at[d - 1], sems, (5, d, i), along_z[d])
    squares = jnp.zeros((), WIDE)
    for i, part in enumerate(parts):
        out, come = part[1], part[11]
        for d in (1, 2, 3):
            last[d, i].wait_recv()
        out[...] = plus(out[...], come[0], come[1], come[2])
        squares = squares + jnp.sum(out[...] * out[...])
    row = lax.broadcasted_iota(jnp.int32, extra.shape, 0)
    board[0] = jnp.where(row == 0, squares, extra[...])
    more = []
    for phase, device in enumerate((sibling, across_x, across_y)):
        copy = send(board.at[phase], board.at[4 + phase], small, (phase,), device)
        copy.wait_recv()
        more.append(copy)
        board[phase + 1] = board[phase] + board[4 + phase]
    for d in (1, 2, 3):
        more.append(send(board.at[3], board.at[8 + z], small, (2 + d,), along_z[d]))
    board[8 + z] = board[3]
    for d in (1, 2, 3):
        more[2 + d].wait_recv()
    totals[...] = board[8] + board[9] + board[10] + board[11]
    for group in (first, left, right, left_two, right_two, last):
        for copy in group.values():
            copy.wait_send()
    for copy in more:
        copy.wait_send()


def reduce_scatter(g_one, g_two, extra):
    rows = [g.shape[0] // 32 for g in (g_one, g_two)]
    cols = [g.shape[1] for g in (g_one, g_two)]
    vmem = pl.BlockSpec(memory_space=pltpu.VMEM)
    return pl.pallas_call(
        scatter_kernel,
        out_shape=[jax.ShapeDtypeStruct((r, n), WIDE) for r, n in zip(rows, cols)]
        + [jax.ShapeDtypeStruct(extra.shape, WIDE)],
        in_specs=[vmem] * 3,
        out_specs=[vmem] * 3,
        scratch_shapes=scatter_scratch(rows[0], cols[0]) + scatter_scratch(rows[1], cols[1])
        + [pltpu.VMEM((12,) + extra.shape, WIDE), pltpu.SemaphoreType.DMA((2, 6, 4, 2)),
           pltpu.SemaphoreType.DMA((2, 6))],
        compiler_params=pltpu.CompilerParams(
            collective_id=1, has_side_effects=True, vmem_limit_bytes=48 * 2**20),
    )(g_one.reshape(GRID + (rows[0], cols[0])), g_two.reshape(GRID + (rows[1], cols[1])), extra)


HALF_COLS = 128


def net_scratch(nodes, halo, pixels, width, hidden, kept):
    near = nodes + 2 * halo
    return dict(
        owner_hot=pltpu.VMEM((nodes, pixels), LOW),
        node_hot=pltpu.VMEM((nodes, pixels), LOW),
        bias=pltpu.VMEM((near, nodes), WIDE),
        send_hot=pltpu.VMEM((2 * halo, nodes), LOW),
        inv_count=pltpu.VMEM((nodes, 1), WIDE),
        sums=pltpu.VMEM((2 * nodes, 2 * HALF_COLS), LOW),
        wave=pltpu.VMEM((2, 4, width), WIDE),
        d_wave=pltpu.VMEM((2, 4, width), WIDE),
        start=pltpu.VMEM((nodes, width), WIDE),
        unit_one=pltpu.VMEM((2, nodes, width), LOW),
        inv_one=pltpu.VMEM((2, nodes, 1), WIDE),
        normed=pltpu.VMEM((2 * near, width), LOW),
        queries=pltpu.VMEM((2, nodes, width), LOW),
        extended=pltpu.VMEM((2, near, 2 * width), LOW),
        probs=pltpu.VMEM((2, HEADS, near, nodes), LOW),
        mixed=pltpu.VMEM((2 * nodes, width), LOW),
        unit_two=pltpu.VMEM((2, nodes, width), LOW),
        inv_two=pltpu.VMEM((2, nodes, 1), WIDE),
        second=pltpu.VMEM((2 * nodes, width), LOW),
        gated=pltpu.VMEM((2 * nodes, hidden), LOW),
        slope=pltpu.VMEM((2 * nodes, hidden), LOW),
        final=pltpu.VMEM((2 * nodes, width), LOW),
        taken=pltpu.VMEM((2 * nodes, HALF_COLS), LOW),
        d_branch=pltpu.VMEM((2 * nodes, width), LOW),
        d_attn=pltpu.VMEM((2 * nodes, width), LOW),
        d_queries=pltpu.VMEM((2 * nodes, width), LOW),
        d_keyval=pltpu.VMEM((2 * near, 2 * width), LOW),
        d_summed=pltpu.VMEM((2 * nodes, width), LOW),
        d_mixed=pltpu.VMEM((nodes, width), LOW),
        d_scores=pltpu.VMEM((near, nodes), LOW),
        scores=pltpu.VMEM((near, nodes), WIDE),
        d_normed=pltpu.VMEM((nodes, width), WIDE),
        outgoing=pltpu.VMEM((4, 2 * halo, width), LOW),
        returned=pltpu.VMEM((2, 2 * halo, width), LOW),
        state=pltpu.VMEM((kept, pixels), WIDE),
        aim=pltpu.VMEM((kept, pixels), WIDE),
        extra=pltpu.VMEM((kept, pixels), WIDE),
        low_state=pltpu.VMEM((HALF_COLS, pixels), LOW),
        staged=pltpu.VMEM((2, 256, hidden), LOW),
        w_early=pltpu.VMEM(GRID + (width // 32, 5 * width), LOW),
        w_up=pltpu.VMEM(GRID + (width // 32, hidden), LOW),
        w_down=pltpu.VMEM(GRID + (hidden // 32, width), LOW),
        loads=pltpu.SemaphoreType.DMA((7,)),
        stores=pltpu.SemaphoreType.DMA((2,)),
        links=pltpu.SemaphoreType.DMA((2, 4, 2)),
        spread=pltpu.SemaphoreType.DMA((2, 6, 4, 3)),
    )


def loop(count, body):
    def step(i, carry):
        body(i)
        return carry

    lax.fori_loop(0, count, step, 0)


def block(index, size):
    return pl.ds(pl.multiple_of(index * size, size), size)


def spread_steps(arrays, sems, first, where):
    z, y, x, c, sibling, across_x, across_y, along_z = where
    planes, x_one, y_one, x_two, y_two, core = {}, {}, {}, {}, {}, {}

    def plane_of(d):
        return (z - d + 4) % 4

    def cross(d):
        for i, out in enumerate(arrays):
            h = out.shape[-1] // 2
            here_l, here_r = out.at[plane_of(d), y, x, c, :, :h], out.at[plane_of(d), y, x, c, :, h:]
            x_one[d, i] = send(here_l, here_l, sems, (1, d, first + i), across_x)
            y_one[d, i] = send(here_r, here_r, sems, (2, d, first + i), across_y)

    def begin():
        for i, out in enumerate(arrays):
            mine = out.at[z, y, x, c]
            for d in (1, 3, 2):
                planes[d, i] = send(mine, mine, sems, (0, d, first + i), along_z[d])
        cross(0)

    def arrive(d):
        for i in range(len(arrays)):
            planes[d, i].wait_recv()
        cross(d)

    def turn(d):
        for i, out in enumerate(arrays):
            h = out.shape[-1] // 2
            x_one[d, i].wait_recv()
            both = out.at[plane_of(d), y, :, c, :, :h]
            y_two[d, i] = send(both, both, sems, (3, d, first + i), across_y)
            y_one[d, i].wait_recv()
            both = out.at[plane_of(d), :, x, c, :, h:]
            x_two[d, i] = send(both, both, sems, (4, d, first + i), across_x)

    def share(d):
        for i, out in enumerate(arrays):
            y_two[d, i].wait_recv()
            x_two[d, i].wait_recv()
            plane = out.at[plane_of(d), :, :, c]
            core[d, i] = send(plane, plane, sems, (5, d, first + i), sibling)

    def end():
        for group in (planes, x_one, y_one, x_two, y_two):
            for copy in group.values():
                copy.wait_send()
        for copy in core.values():
            copy.wait()

    do = functools.partial
    return [begin, do(arrive, 1), do(arrive, 3), do(turn, 0), do(arrive, 2), do(turn, 1), do(turn, 3), do(share, 0),
            do(turn, 2), do(share, 1), do(share, 3), do(share, 2), end]


def net_kernel(names, chan, gathered, numbers, counts, previous, noisy, target, noise, owners, decode_idx, near_idx,
               send_idx, waves, *rest):
    weights, (g_wide, g_down, loss), scratch = rest[: len(rest) - 3 - len(names)], rest[-3 - len(names) : -len(names)], rest[-len(names) :]
    r = types.SimpleNamespace(**dict(zip(names, scratch)))
    nodes, pixels = near_idx.shape[1], owners.shape[1]
    halo = send_idx.shape[0] // 2
    near = nodes + 2 * halo
    width, hidden = r.start.shape[1], r.gated.shape[1]
    at = [0, 3 * width, 4 * width, 4 * width + hidden, 4 * width + hidden + 256, 4 * width + hidden + 384]
    tile = 1024
    tiles = pixels // tile
    patches = lax.axis_size("patch")
    me = lax.axis_index("patch")
    lower, upper = {"patch": (me + patches - 1) % patches}, {"patch": (me + 1) % patches}
    barrier = pltpu.get_barrier_semaphore()
    others = [lower, upper]
    if not gathered:
        where = places()
        z, y, x, c, sibling, across_x, across_y, along_z = where
        others += [sibling, across_x, across_y] + along_z[1:]
    for other in others:
        pl.semaphore_signal(barrier, inc=1, device_id=other, device_id_type=MESH)

    def load(src, dst, slot):
        copy = pltpu.make_async_copy(src, dst, r.loads.at[slot])
        copy.start()
        return copy

    pairs = ((previous, r.low_state), (noisy, r.state), (target, r.aim), (noise, r.extra))
    loads = [load(src, dst, slot) for slot, (src, dst) in enumerate(pairs)]
    rows_used = r.state.shape[0]
    w_at = [0, width, 3 * width, 4 * width, 4 * width + HALF_COLS, 4 * width + 2 * HALF_COLS, 4 * width + 3 * HALF_COLS]
    w_targets = (r.w_early, r.w_up, r.w_down)
    early_steps, late_steps = [], []
    if gathered:
        pl.semaphore_wait(barrier, len(others))
        for i, (src, dst) in enumerate(zip(weights, w_targets)):
            load(src, dst, 4 + i).wait()
    else:
        project, output, encode_prev, encode_noisy, decode, noise_rows, up, down = weights
        r.w_early[z, y, x, c, :, 4 * width :] = jnp.zeros((width // 32, width), LOW)
        for i, piece in ((0, project), (2, output), (3, encode_prev), (4, encode_noisy), (5, decode), (6, noise_rows)):
            r.w_early[z, y, x, c, :, w_at[i] : w_at[i] + piece.shape[1]] = piece[...].astype(LOW)
        r.w_up[z, y, x, c] = up[...].astype(LOW)
        r.w_down[z, y, x, c] = down[...].astype(LOW)
        early_steps = spread_steps(w_targets[:1], r.spread, 0, where)
        late_steps = spread_steps(w_targets[1:], r.spread, 1, where)
        pl.semaphore_wait(barrier, len(others))

    def advance(steps, count):
        for _ in range(min(count, len(steps))):
            steps.pop(0)()

    def early(first, last):
        return r.w_early[:, :, :, :, :, w_at[first] : (w_at + [5 * width])[last]].reshape(width, -1)

    def all_up():
        return r.w_up[...].reshape(width, hidden)

    advance(early_steps, 1)

    level = [numbers[4 * s] for s in range(2)]
    c_in = [numbers[4 * s + 1] for s in range(2)]
    c_skip = [numbers[4 * s + 2] for s in range(2)]
    c_out = [numbers[4 * s + 3] for s in range(2)]

    def build_hot(t):
        cols = block(t, tile)
        place = lax.broadcasted_iota(jnp.int32, (1, tile), 1) + t * tile
        own = jnp.where(place < counts[1], owners[:, cols], -1)
        three = [decode_idx[i : i + 1, cols] for i in range(3)]

        def rows(b):
            row = lax.broadcasted_iota(jnp.int32, (16, tile), 0) + b * 16
            r.owner_hot[block(b, 16), cols] = (row == own).astype(WIDE).astype(LOW)
            total = sum((row == idx).astype(WIDE) for idx in three)
            r.node_hot[block(b, 16), cols] = total.astype(LOW)

        loop(nodes // 16, rows)


    def build_bias(b):
        rows = block(b, 32)
        place = lax.broadcasted_iota(jnp.int32, (32, nodes), 0) + b * 32
        listed = jnp.zeros((32, nodes), WIDE)
        for j in range(1, NEIGH):
            listed = listed + (near_idx[j : j + 1] == place).astype(WIDE)
        listed = jnp.where((place >= nodes) | (place < counts[0]), listed, 0.0)
        listed = listed + (near_idx[0:1] == place).astype(WIDE)
        r.bias[rows] = jnp.where(listed > 0.0, jnp.log(jnp.maximum(listed, 1.0)), -1e30)

    loop(near // 32, build_bias)
    advance(early_steps, 4)
    advance(late_steps, 1)
    for t in range(tiles):
        build_hot(t)
        advance(early_steps, 2)
    r.send_hot[...] = (
        lax.broadcasted_iota(jnp.int32, (2 * halo, nodes), 1) == send_idx[...]
    ).astype(WIDE).astype(LOW)

    loads[0].wait()
    summed = nt(r.owner_hot[...], r.low_state[...])
    channel = lax.broadcasted_iota(jnp.int32, (nodes, HALF_COLS), 1)
    total = jnp.sum(jnp.where(channel == chan, summed, 0.0), axis=1, keepdims=True)
    r.inv_count[...] = 1.0 / jnp.maximum(total, 1.0)
    summed = jnp.where(channel < chan, summed, 0.0).astype(LOW)
    r.sums[:nodes, :HALF_COLS] = summed
    r.sums[nodes:, :HALF_COLS] = summed
    for copy in loads[1:]:
        copy.wait()
    r.low_state[:rows_used] = (r.state[...] * c_in[0]).astype(LOW)
    r.sums[:nodes, HALF_COLS:] = nt(r.owner_hot[...], r.low_state[...]).astype(LOW)
    advance(early_steps, len(early_steps))
    advance(late_steps, 3)

    noise_block = early(6, 7).astype(WIDE).reshape(32, 16, 128)
    lane = lax.broadcasted_iota(jnp.int32, (1, 128), 1)
    for s in range(2):
        parts = jnp.sum(noise_block * waves[s][None], axis=1)
        both = parts + pltpu.roll(parts, 64, 1)
        for k in range(16):
            piece = jnp.where(lane < 64, both[2 * k : 2 * k + 1], both[2 * k + 1 : 2 * k + 2])
            r.wave[s, k // 4 : k // 4 + 1, (k % 4) * 128 : (k % 4 + 1) * 128] = piece


    def pass_on(number, first, second):
        copies = []
        for i, (dst, device) in enumerate(((first, lower), (second, upper))):
            copy = pltpu.make_async_remote_copy(
                src_ref=r.outgoing.at[number, i * halo : (i + 1) * halo], dst_ref=dst,
                send_sem=r.links.at[0, number, i], recv_sem=r.links.at[1, number, i],
                device_id=device, device_id_type=MESH,
            )
            copy.start()
            copies.append(copy)
        return copies

    def encode(s):
        rows = slice(s * nodes, (s + 1) * nodes)
        if s:
            r.low_state[:rows_used] = (r.state[...] * c_in[s]).astype(LOW)
            r.sums[rows, HALF_COLS:] = nt(r.owner_hot[...], r.low_state[...]).astype(LOW)
        r.start[...] = nt(r.sums[rows], early(3, 5)) * r.inv_count[...]

        def norm(b):
            part = block(b, 64)
            unit, inverse = norm_parts(r.start[part])
            r.unit_one[s, part] = unit.astype(LOW)
            r.inv_one[s, part] = inverse
            scaled = unit * (1.0 + r.wave[s, 0:1]) + r.wave[s, 1:2]
            r.normed[pl.ds(pl.multiple_of(s * nodes + b * 64, 64), 64)] = scaled.astype(LOW)

        loop(nodes // 64, norm)
        normed = r.normed[rows]
        r.outgoing[s] = nn(r.send_hot[...], normed).astype(LOW)
        first = 2 * nodes + 2 * halo * s
        copies = pass_on(s, r.normed.at[first + halo : first + 2 * halo], r.normed.at[first : first + halo])
        r.queries[s] = nn(normed, early(0, 1)).astype(LOW)
        advance(late_steps, 1)
        r.extended[s, :nodes] = nn(normed, early(1, 2)).astype(LOW)
        advance(late_steps, 1)
        return copies

    def attend(s, copies):
        rows = slice(s * nodes, (s + 1) * nodes)
        for copy in copies:
            copy.wait()
        first = 2 * nodes + 2 * halo * s
        r.extended[s, nodes:] = nn(r.normed[first : first + 2 * halo], early(1, 2)).astype(LOW)
        for head in range(HEADS):
            cols = slice(head * HD, (head + 1) * HD)
            r.scores[...] = nt(r.extended[s, :, cols], r.queries[s, :, cols])

            def soft(b):
                part = block(b, 128)
                top = jnp.full((8, 128), -1e30, WIDE)
                for k in range(near // 64):
                    rows = slice(k * 64, (k + 1) * 64)
                    score = r.scores[rows, part] * SCALE + r.bias[rows, part]
                    r.scores[rows, part] = score
                    top = jnp.maximum(top, jnp.max(score.reshape(8, 8, 128), axis=0))
                top = jnp.max(top, axis=0, keepdims=True)
                total = jnp.zeros((8, 128), WIDE)
                for k in range(near // 64):
                    rows = slice(k * 64, (k + 1) * 64)
                    weight = jnp.exp(r.scores[rows, part] - top)
                    r.scores[rows, part] = weight
                    total = total + jnp.sum(weight.reshape(8, 8, 128), axis=0)
                total = 1.0 / jnp.sum(total, axis=0, keepdims=True)
                for k in range(near // 64):
                    rows = slice(k * 64, (k + 1) * 64)
                    r.probs[s, head, rows, part] = (r.scores[rows, part] * total).astype(LOW)

            loop(nodes // 128, soft)
            values = r.extended[s, :, width + head * HD : width + (head + 1) * HD]
            r.mixed[rows, cols] = tn(values, r.probs[s, head]).T.astype(LOW)
            advance(late_steps, 2)
        advance(late_steps, len(late_steps))
        r.start[...] += nn(r.mixed[rows], early(2, 3))

        def norm(b):
            part = block(b, 64)
            unit, inverse = norm_parts(r.start[part])
            r.unit_two[s, part] = unit.astype(LOW)
            r.inv_two[s, part] = inverse
            scaled = unit * (1.0 + r.wave[s, 2:3]) + r.wave[s, 3:4]
            r.second[pl.ds(pl.multiple_of(s * nodes + b * 64, 64), 64)] = scaled.astype(LOW)

        loop(nodes // 64, norm)

        def feed(j):
            cols = block(j, 256)
            upward = nn(r.second[rows], r.w_up[:, :, :, :, :, cols].reshape(width, 256))
            gate = 1.0 / (1.0 + jnp.exp(-upward))
            r.gated[rows, cols] = (upward * gate).astype(LOW)
            r.slope[rows, cols] = (gate * (1.0 + upward * (1.0 - gate))).astype(LOW)

        loop(hidden // 256, feed)
        r.final[rows] = (r.start[...] + nn(r.gated[rows], r.w_down[...].reshape(hidden, width))).astype(LOW)
        out = nn(r.final[rows], early(5, 6)) * (1.0 / 3.0)
        return out.T.astype(LOW)[:rows_used]

    def gradient(s):
        rows = slice(s * nodes, (s + 1) * nodes)
        taken = (nt(r.node_hot[...], r.low_state[...]) * (1.0 / 3.0)).astype(LOW)
        r.taken[rows] = taken
        d_final = nt(taken, early(5, 6))
        r.start[...] = d_final
        r.d_branch[rows] = d_final.astype(LOW)

        def feed(j):
            cols = block(j, 256)
            d_gated = nt(r.d_branch[rows], r.w_down[j // 2, j % 2].reshape(256, width))
            r.slope[rows, cols] = (d_gated * r.slope[rows, cols].astype(WIDE)).astype(LOW)

        loop(hidden // 256, feed)
        r.d_normed[...] = nt(r.slope[rows], all_up())
        norm_gradient(s, r.unit_two, r.inv_two, 2)
        r.d_attn[rows] = r.start[...].astype(LOW)
        r.d_mixed[...] = nt(r.d_attn[rows], early(2, 3)).astype(LOW)
        first = 2 * nodes + 2 * halo * s
        far = slice(first, first + 2 * halo)
        for head in range(HEADS):
            cols = slice(head * HD, (head + 1) * HD)
            after = slice(width + head * HD, width + (head + 1) * HD)
            r.scores[...] = nt(r.extended[s, :, after], r.d_mixed[:, cols])

            def soft(b):
                part = block(b, 128)
                total = jnp.zeros((8, 128), WIDE)
                for k in range(near // 64):
                    rows = slice(k * 64, (k + 1) * 64)
                    slope = r.probs[s, head, rows, part].astype(WIDE) * r.scores[rows, part]
                    total = total + jnp.sum(slope.reshape(8, 8, 128), axis=0)
                total = jnp.sum(total, axis=0, keepdims=True)
                for k in range(near // 64):
                    rows = slice(k * 64, (k + 1) * 64)
                    slope = r.probs[s, head, rows, part].astype(WIDE) * (r.scores[rows, part] - total)
                    r.d_scores[rows, part] = (slope * SCALE).astype(LOW)

            loop(nodes // 128, soft)
            d_values = nn(r.probs[s, head], r.d_mixed[:, cols]).astype(LOW)
            d_keys = nn(r.d_scores[...], r.queries[s, :, cols]).astype(LOW)
            r.d_keyval[rows, after] = d_values[:nodes]
            r.d_keyval[far, after] = d_values[nodes:]
            r.d_keyval[rows, cols] = d_keys[:nodes]
            r.d_keyval[far, cols] = d_keys[nodes:]
            r.d_queries[rows, cols] = tn(r.extended[s, :, cols], r.d_scores[...]).T.astype(LOW)
        r.outgoing[2 + s] = nt(r.d_keyval[far], early(1, 2)).astype(LOW)
        copies = pass_on(2 + s, r.returned.at[s, halo:], r.returned.at[s, :halo])
        r.d_normed[...] = nt(r.d_queries[rows], early(0, 1)) + nt(r.d_keyval[rows], early(1, 2))
        return copies

    def norm_gradient(s, units, inverses, which):
        r.d_wave[s, which : which + 2] = jnp.zeros((2, width), WIDE)

        def norm(b):
            part = block(b, 64)
            unit = units[s, part].astype(WIDE)
            d_out = r.d_normed[part]
            d_scale = jnp.sum(d_out * unit, axis=0, keepdims=True)
            d_shift = jnp.sum(d_out, axis=0, keepdims=True)
            r.d_wave[s, which : which + 1] += d_scale
            r.d_wave[s, which + 1 : which + 2] += d_shift
            d_unit = d_out * (1.0 + r.wave[s, which : which + 1])
            along = jnp.mean(d_unit * unit, axis=-1, keepdims=True)
            d_hidden = d_unit - jnp.mean(d_unit, axis=-1, keepdims=True) - unit * along
            r.start[part] += inverses[s, part] * d_hidden

        loop(nodes // 64, norm)

    def absorb(s, copies):
        rows = slice(s * nodes, (s + 1) * nodes)
        for copy in copies:
            copy.wait()
        r.d_normed[...] += tn(r.send_hot[...], r.returned[s])
        norm_gradient(s, r.unit_one, r.inv_one, 0)
        r.d_summed[rows] = (r.start[...] * r.inv_count[...]).astype(LOW)

    copies = encode(0)
    nodes_out = attend(0, copies)

    def decode_one(t):
        cols = block(t, tile)
        out = nn(nodes_out, r.node_hot[:, cols])
        r.state[:, cols] = c_skip[0] * r.state[:, cols] + c_out[0] * out + level[1] * r.extra[:, cols]

    loop(tiles, decode_one)
    copies = encode(1)
    nodes_out_two = attend(1, copies)
    loss[...] = jnp.zeros(loss.shape, WIDE)

    def decode_two(t):
        cols = block(t, tile)
        out = nn(nodes_out_two, r.node_hot[:, cols])
        place = lax.broadcasted_iota(jnp.int32, (1, tile), 1) + t * tile
        error = c_skip[1] * r.state[:, cols] + c_out[1] * out - r.aim[:, cols]
        error = jnp.where(place < counts[1], error, 0.0)
        loss[...] += jnp.sum(error * error)
        r.extra[:, cols] = 2.0 * error
        r.low_state[:rows_used, cols] = (c_out[1] * 2.0 * error).astype(LOW)

    loop(tiles, decode_two)
    copies = gradient(1)
    absorb(1, copies)
    d_nodes = nn(r.d_summed[nodes:], early(4, 5))
    d_nodes = d_nodes.T.astype(LOW)[:rows_used]

    def into_one(t):
        cols = block(t, tile)
        d_noisy = c_skip[1] * r.extra[:, cols] + c_in[1] * nn(d_nodes, r.owner_hot[:, cols])
        r.low_state[:rows_used, cols] = (c_out[0] * d_noisy).astype(LOW)

    loop(tiles, into_one)
    copies = gradient(0)

    stores = [None, None]

    def store(slot, dst, cols):
        copy = pltpu.make_async_copy(r.staged.at[slot, :, :cols], dst, r.stores.at[slot])
        copy.start()
        stores[slot] = copy

    done = [0]

    def product(left, i, right, out, first):
        slot, cols = done[0] % 2, right.shape[1]
        done[0] += 1
        if stores[slot] is not None:
            stores[slot].wait()
        r.staged[slot, :, :cols] = tn(left[:, i * 256 : (i + 1) * 256], right[...]).astype(LOW)
        store(slot, out.at[i * 256 : (i + 1) * 256, first : first + cols], cols)

    for i in range(hidden // 256):
        product(r.gated, i, r.d_branch, g_down, 0)
    for i in range(width // 256):
        product(r.second, i, r.slope, g_wide, at[2])
        product(r.mixed, i, r.d_attn, g_wide, at[1])
        product(r.final, i, r.taken, g_wide, at[4])
        product(r.normed, i, r.d_keyval, g_wide, width)
        product(r.normed.at[: 2 * nodes], i, r.d_queries, g_wide, 0)
    absorb(0, copies)
    for i in range(width // 256):
        product(r.d_summed, i, r.sums, g_wide, at[3])
    for i in range(2):
        slot = (done[0] + i) % 2
        stores[slot].wait()
        total = jnp.zeros((16, 16, 128), WIDE)
        for s in range(2):
            pieces = []
            for k in range(8 * i, 8 * i + 8):
                piece = r.d_wave[s, k // 4 : k // 4 + 1, (k % 4) * 128 : (k % 4 + 1) * 128]
                turned = pltpu.roll(piece, 64, 1)
                pieces.append(jnp.where(lane < 64, piece, turned))
                pieces.append(jnp.where(lane < 64, turned, piece))
            rows = jnp.concatenate(pieces, axis=0)
            total = total + rows[:, None, :] * waves[s][None]
        r.staged[slot, :, :128] = total.reshape(256, 128).astype(LOW)
        store(slot, g_wide.at[i * 256 : (i + 1) * 256, at[5] : at[5] + 128], 128)
    for copy in stores:
        copy.wait()


def run_net(chan, gathered, numbers, counts, previous, noisy, target, noise, owners, decode_idx, near_idx, send_idx,
            waves, width, hidden, weights):
    nodes, pixels = near_idx.shape[1], owners.shape[1]
    scratch = net_scratch(nodes, send_idx.shape[0] // 2, pixels, width, hidden, noisy.shape[0])
    vmem, smem = pl.BlockSpec(memory_space=pltpu.VMEM), pl.BlockSpec(memory_space=pltpu.SMEM)
    hbm = pl.BlockSpec(memory_space=pl.ANY)
    wide = 4 * width + hidden + 4 * HALF_COLS
    return pl.pallas_call(
        functools.partial(net_kernel, tuple(scratch), chan, gathered),
        out_shape=[jax.ShapeDtypeStruct((width, wide), LOW), jax.ShapeDtypeStruct((hidden, width), LOW),
                   jax.ShapeDtypeStruct((8, 128), WIDE)],
        in_specs=[smem] * 2 + [hbm] * 4 + [vmem] * 5 + [hbm if gathered else vmem] * len(weights),
        out_specs=[hbm, hbm, vmem],
        scratch_shapes=list(scratch.values()),
        compiler_params=pltpu.CompilerParams(
            collective_id=3, has_side_effects=True, vmem_limit_bytes=VMEM_LIMIT),
    )(numbers, counts, previous, noisy, target, noise, owners, decode_idx, near_idx, send_idx, waves, *weights)


def fill(array, columns):
    return jnp.pad(array, ((0, 0), (0, columns - array.shape[1])))


def on_device(
    previous_state, target_state, noise_draws, noise_level, pixel_owner, mesh_to_grid, neighbours, halo_send,
    node_count, pixel_count, w_encode, w_project, w_output, w_up, w_down, w_noise, w_decode,
    m_encode, m_project, m_output, m_up, m_down, m_noise, m_decode,
    v_encode, v_project, v_output, v_up, v_down, v_noise, v_decode,
):
    width = w_project.shape[1] // 3
    hidden = w_up.shape[1]
    channels = previous_state.shape[1]
    rows = w_project.shape[0]
    small_slice = lax.axis_size("patch") == 8 and lax.axis_size("rep") == 4
    flipped = w_encode.T
    halves = (flipped[:, :channels], flipped[:, channels:])
    if small_slice:
        weights = (w_project, w_output) + halves + (w_decode, w_noise.reshape(rows, HALF_COLS), w_up, w_down)
    else:
        pieces = [w_project, w_output] + [fill(half, HALF_COLS) for half in halves] + [fill(w_decode, HALF_COLS)]
        early = lax.all_gather(jnp.concatenate(pieces, axis=1).astype(LOW), BOTH, axis=0, tiled=True)
        noise = lax.all_gather(w_noise.astype(LOW), BOTH, axis=1, tiled=True).reshape(FOUR, -1, 64)
        early = jnp.concatenate([early, noise.transpose(1, 0, 2).reshape(width, HALF_COLS)], axis=1)
        all_up = lax.all_gather(w_up.astype(LOW), BOTH, axis=0, tiled=True)
        all_down = lax.all_gather(w_down.astype(LOW), BOTH, axis=0, tiled=True)
        weights = [w.reshape(GRID + (-1, w.shape[1])) for w in (early, all_up, all_down)]
    at = [0, 3 * width, 4 * width, 4 * width + hidden, 4 * width + hidden + 256, 4 * width + hidden + 384]

    levels = noise_level[0]
    pixels = pixel_owner.shape[1]
    padding = ((0, -channels % 16), (0, 0))
    previous = jnp.concatenate([previous_state[0], jnp.ones((1, pixels), WIDE)], axis=0).astype(LOW)
    previous = jnp.pad(previous, ((0, HALF_COLS - channels - 1), (0, 0)))
    target = jnp.pad(target_state[0], padding)
    noisy = jnp.pad(target_state[0] + levels[0] * noise_draws[0, 0], padding)
    noise_two = jnp.pad(noise_draws[0, 1], padding)
    c_in = lax.rsqrt(levels * levels + 1.0)
    numbers = jnp.stack([levels, c_in, 1.0 / (levels * levels + 1.0), levels * c_in], axis=1).reshape(8)
    counts = jnp.concatenate([node_count[0], pixel_count[0]])
    waves = jnp.stack([fourier(levels[i]).reshape(FOUR // 2, 2) for i in range(2)])
    waves = jnp.repeat(waves, 64, axis=2)
    g_wide, g_down, loss_local = run_net(
        channels, not small_slice, numbers, counts, previous, noisy, target, noise_two, pixel_owner, mesh_to_grid[0],
        neighbours[0].T, halo_send.reshape(-1, 1), waves, width, hidden, weights,
    )
    count_local = (channels * jnp.minimum(pixel_count[0, 0], pixels)).astype(WIDE)
    if small_slice:
        row = lax.broadcasted_iota(jnp.int32, (8, 128), 0)
        extra = jnp.where(row == 1, loss_local, 0.0) + jnp.where(row == 2, count_local, 0.0)
        s_wide, s_down, totals = reduce_scatter(g_wide, g_down, extra)
        totals = totals[:3, 0]
        s_noise = s_wide[:, at[5] :].reshape(FOUR, -1)
    else:
        g_noise = g_wide[:, at[5] :].reshape(-1, FOUR, 64).transpose(1, 0, 2).reshape(FOUR, -1)
        s_wide = lax.psum_scatter(g_wide[:, : at[5]].astype(WIDE), BOTH, scatter_dimension=0, tiled=True)
        s_down = lax.psum_scatter(g_down.astype(WIDE), BOTH, scatter_dimension=0, tiled=True)
        s_noise = lax.psum_scatter(g_noise.astype(WIDE), BOTH, scatter_dimension=1, tiled=True)
        squares = jnp.sum(s_wide * s_wide) + jnp.sum(s_down * s_down) + jnp.sum(s_noise * s_noise)
        totals = lax.psum((squares, loss_local[0, 0], count_local), BOTH)
    second = at[3] + HALF_COLS
    shards = (
        jnp.concatenate([s_wide[:, at[3] : at[3] + channels], s_wide[:, second : second + channels]], axis=1).T,
        s_wide[:, : at[1]],
        s_wide[:, at[1] : at[2]],
        s_wide[:, at[2] : at[3]],
        s_down,
        s_noise,
        s_wide[:, at[4] : at[4] + channels],
    )
    grad_norm = jnp.sqrt(totals[0])
    factor = THRESHOLD / jnp.maximum(grad_norm, THRESHOLD)
    masters = (w_encode, w_project, w_output, w_up, w_down, w_noise, w_decode)
    moments = (m_encode, m_project, m_output, m_up, m_down, m_noise, m_decode)
    seconds = (v_encode, v_project, v_output, v_up, v_down, v_noise, v_decode)
    new_weights, new_moments, new_seconds = ([], [], [])
    for w, m, v, g in zip(masters, moments, seconds, shards):
        clipped = g * factor
        moment = BETA_ONE * m + (1.0 - BETA_ONE) * clipped
        variance = BETA_TWO * v + (1.0 - BETA_TWO) * clipped * clipped
        stepped = (
            moment
            / (1.0 - BETA_ONE**STEP)
            / (jnp.sqrt(variance / (1.0 - BETA_TWO**STEP)) + EPSILON)
        )
        new_weights.append(w - LEARN_RATE * (stepped + DECAY_RATE * w))
        new_moments.append(moment)
        new_seconds.append(variance)
    return (
        tuple(new_weights)
        + tuple(new_moments)
        + tuple(new_seconds)
        + (totals[1], totals[2], grad_norm)
    )


def solution(mesh):
    in_specs = (
        P("rep", None, "patch"),
        P("rep", None, "patch"),
        P("rep", None, None, "patch"),
        P("rep", None),
        P("rep", "patch"),
        P("rep", None, "patch"),
        P("rep", "patch", None),
        P("rep", "patch"),
        P("rep", "patch"),
        P("rep", "patch"),
        P(None, ("patch", "rep")),
        P(("patch", "rep"), None),
        P(("patch", "rep"), None),
        P(("patch", "rep"), None),
        P(("patch", "rep"), None),
        P(None, ("patch", "rep")),
        P(("patch", "rep"), None),
        P(None, ("patch", "rep")),
        P(("patch", "rep"), None),
        P(("patch", "rep"), None),
        P(("patch", "rep"), None),
        P(("patch", "rep"), None),
        P(None, ("patch", "rep")),
        P(("patch", "rep"), None),
        P(None, ("patch", "rep")),
        P(("patch", "rep"), None),
        P(("patch", "rep"), None),
        P(("patch", "rep"), None),
        P(("patch", "rep"), None),
        P(None, ("patch", "rep")),
        P(("patch", "rep"), None),
    )
    out_specs = (
        P(None, ("patch", "rep")),
        P(("patch", "rep"), None),
        P(("patch", "rep"), None),
        P(("patch", "rep"), None),
        P(("patch", "rep"), None),
        P(None, ("patch", "rep")),
        P(("patch", "rep"), None),
        P(None, ("patch", "rep")),
        P(("patch", "rep"), None),
        P(("patch", "rep"), None),
        P(("patch", "rep"), None),
        P(("patch", "rep"), None),
        P(None, ("patch", "rep")),
        P(("patch", "rep"), None),
        P(None, ("patch", "rep")),
        P(("patch", "rep"), None),
        P(("patch", "rep"), None),
        P(("patch", "rep"), None),
        P(("patch", "rep"), None),
        P(None, ("patch", "rep")),
        P(("patch", "rep"), None),
        P(),
        P(),
        P(),
    )
    return jax.shard_map(
        on_device, mesh=mesh, in_specs=in_specs, out_specs=out_specs, check_vma=False
    )
```

```python
import functools
import types

import jax
import jax.numpy as jnp
from jax import lax
from jax.experimental import pallas as pl
from jax.experimental.pallas import tpu as pltpu
from jax.sharding import PartitionSpec as P

HEADS = 4
HD = 128
FOUR = 32
NEIGH = 16
STEP = 5


LEARN_RATE = 0.03
BETA_ONE = 0.9
BETA_TWO = 0.95
EPSILON = 1e-08
DECAY_RATE = 0.1
THRESHOLD = 1.0

BOTH = ("patch", "rep")
LOW = jnp.bfloat16
WIDE = jnp.float32
SCALE = HD ** (-0.5)
VMEM_LIMIT = 64 * 2**20


def nn(a, b):
    return lax.dot_general(a, b, (((1,), (0,)), ((), ())), preferred_element_type=WIDE)


def nt(a, b):
    return lax.dot_general(a, b, (((1,), (1,)), ((), ())), preferred_element_type=WIDE)


def tn(a, b):
    return lax.dot_general(a, b, (((0,), (0,)), ((), ())), preferred_element_type=WIDE)


def fourier(level):
    frequency = 0.25 * (jnp.arange(FOUR // 2).astype(jnp.float32) + 1.0)
    angles = jnp.log(level) * frequency
    return jnp.concatenate([jnp.sin(angles), jnp.cos(angles)])


def norm_parts(hidden):
    centre = hidden - jnp.mean(hidden, axis=-1, keepdims=True)
    spread = jnp.mean(centre * centre, axis=-1, keepdims=True)
    inverse = lax.rsqrt(spread + 1e-05)
    return centre * inverse, inverse


MESH = pl.DeviceIdType.MESH
GRID = (4, 2, 2, 2)


def places():
    patch, rep = lax.axis_index("patch"), lax.axis_index("rep")
    z, y, x, c = patch // 2, patch % 2, rep // 2, rep % 2
    sibling = {"patch": patch, "rep": x * 2 + (1 - c)}
    across_x = {"patch": patch, "rep": (1 - x) * 2 + c}
    across_y = {"patch": z * 2 + (1 - y), "rep": rep}
    along_z = [{"patch": ((z + d) % 4) * 2 + y, "rep": rep} for d in range(4)]
    return z, y, x, c, sibling, across_x, across_y, along_z


def send(src, dst, sems, index, device):
    copy = pltpu.make_async_remote_copy(
        src_ref=src, dst_ref=dst, send_sem=sems.at[(0,) + index], recv_sem=sems.at[(1,) + index],
        device_id=device, device_id_type=MESH,
    )
    copy.start()
    return copy


def plus(*terms):
    total = terms[0].astype(WIDE)
    for term in terms[1:]:
        total = total + term.astype(WIDE)
    return total


HALF_COLS = 128


def net_scratch(nodes, halo, pixels, width, hidden, kept):
    near = nodes + 2 * halo
    return dict(
        owner_hot=pltpu.VMEM((nodes, pixels), LOW),
        node_hot=pltpu.VMEM((nodes, pixels), LOW),
        bias=pltpu.VMEM((near, nodes), WIDE),
        send_hot=pltpu.VMEM((2 * halo, nodes), LOW),
        inv_count=pltpu.VMEM((nodes, 1), WIDE),
        sums=pltpu.VMEM((2 * nodes, 2 * HALF_COLS), LOW),
        wave=pltpu.VMEM((2, 4, width), WIDE),
        d_wave=pltpu.VMEM((2, 4, width), WIDE),
        start=pltpu.VMEM((nodes, width), WIDE),
        unit_one=pltpu.VMEM((2, nodes, width), LOW),
        inv_one=pltpu.VMEM((2, nodes, 1), WIDE),
        normed=pltpu.VMEM((2 * near, width), LOW),
        queries=pltpu.VMEM((2, nodes, width), LOW),
        extended=pltpu.VMEM((2, near, 2 * width), LOW),
        probs=pltpu.VMEM((2, HEADS, near, nodes), LOW),
        mixed=pltpu.VMEM((2 * nodes, width), LOW),
        unit_two=pltpu.VMEM((2, nodes, width), LOW),
        inv_two=pltpu.VMEM((2, nodes, 1), WIDE),
        second=pltpu.VMEM((2 * nodes, width), LOW),
        gated=pltpu.VMEM((2 * nodes, hidden), LOW),
        slope=pltpu.VMEM((2 * nodes, hidden), LOW),
        final=pltpu.VMEM((2 * nodes, width), LOW),
        taken=pltpu.VMEM((2 * nodes, HALF_COLS), LOW),
        d_branch=pltpu.VMEM((2 * nodes, width), LOW),
        d_attn=pltpu.VMEM((2 * nodes, width), LOW),
        d_queries=pltpu.VMEM((2 * nodes, width), LOW),
        d_keyval=pltpu.VMEM((2 * near, 2 * width), LOW),
        d_summed=pltpu.VMEM((2 * nodes, width), LOW),
        d_mixed=pltpu.VMEM((nodes, width), LOW),
        d_scores=pltpu.VMEM((near, nodes), LOW),
        scores=pltpu.VMEM((near, nodes), WIDE),
        outgoing=pltpu.VMEM((4, 2 * halo, width), LOW),
        returned=pltpu.VMEM((2, 2 * halo, width), LOW),
        state=pltpu.VMEM((kept, pixels), WIDE),
        extra=pltpu.VMEM((kept, pixels), WIDE),
        low_state=pltpu.VMEM((HALF_COLS, pixels), LOW),
        g_early=pltpu.VMEM(GRID + (width // 32, 5 * width), LOW),
        g_up=pltpu.VMEM(GRID + (width // 32, hidden), LOW),
        g_down=pltpu.VMEM(GRID + (hidden // 32, width), LOW),
        lost=pltpu.VMEM((8, 128), WIDE),
        board=pltpu.VMEM((12, 8, 128), WIDE),
        w_early=pltpu.VMEM(GRID + (width // 32, 5 * width), LOW),
        w_up=pltpu.VMEM(GRID + (width // 32, hidden), LOW),
        w_down=pltpu.VMEM(GRID + (hidden // 32, width), LOW),
        loads=pltpu.SemaphoreType.DMA((7,)),
        ready=pltpu.SemaphoreType.REGULAR((2,)),
        fold=pltpu.SemaphoreType.DMA((2, 6, 4, 3)),
        small=pltpu.SemaphoreType.DMA((2, 12)),
        links=pltpu.SemaphoreType.DMA((2, 4, 2)),
        spread=pltpu.SemaphoreType.DMA((2, 6, 4, 3)),
    )


def loop(count, body):
    def step(i, carry):
        body(i)
        return carry

    lax.fori_loop(0, count, step, 0)


def block(index, size):
    return pl.ds(pl.multiple_of(index * size, size), size)


def spread_steps(arrays, sems, first, where):
    z, y, x, c, sibling, across_x, across_y, along_z = where
    planes, x_one, y_one, x_two, y_two, core = {}, {}, {}, {}, {}, {}

    def plane_of(d):
        return (z - d + 4) % 4

    def cross(d):
        for i, out in enumerate(arrays):
            h = out.shape[-1] // 2
            here_l, here_r = out.at[plane_of(d), y, x, c, :, :h], out.at[plane_of(d), y, x, c, :, h:]
            x_one[d, i] = send(here_l, here_l, sems, (1, d, first + i), across_x)
            y_one[d, i] = send(here_r, here_r, sems, (2, d, first + i), across_y)

    def begin():
        for i, out in enumerate(arrays):
            mine = out.at[z, y, x, c]
            for d in (1, 3, 2):
                planes[d, i] = send(mine, mine, sems, (0, d, first + i), along_z[d])
        cross(0)

    def arrive(d):
        for i in range(len(arrays)):
            planes[d, i].wait_recv()
        cross(d)

    def turn(d):
        for i, out in enumerate(arrays):
            h = out.shape[-1] // 2
            x_one[d, i].wait_recv()
            both = out.at[plane_of(d), y, :, c, :, :h]
            y_two[d, i] = send(both, both, sems, (3, d, first + i), across_y)
            y_one[d, i].wait_recv()
            both = out.at[plane_of(d), :, x, c, :, h:]
            x_two[d, i] = send(both, both, sems, (4, d, first + i), across_x)

    def share(d):
        for i, out in enumerate(arrays):
            y_two[d, i].wait_recv()
            x_two[d, i].wait_recv()
            plane = out.at[plane_of(d), :, :, c]
            core[d, i] = send(plane, plane, sems, (5, d, first + i), sibling)

    def end():
        for group in (planes, x_one, y_one, x_two, y_two):
            for copy in group.values():
                copy.wait_send()
        for copy in core.values():
            copy.wait()

    do = functools.partial
    return [begin, do(arrive, 1), do(arrive, 3), do(turn, 0), do(arrive, 2), do(turn, 1), do(turn, 3), do(share, 0),
            do(turn, 2), do(share, 1), do(share, 3), do(share, 2), end]


def far_planes(z):
    return [3 * (1 - z // 2), 2 - z // 2, z + 1 - 2 * (z % 2), z]


class Fold:
    def __init__(self, sources, rooms, outs, sems, first, where):
        self.sources, self.rooms, self.outs, self.sems, self.first = sources, rooms, outs, sems, first
        self.z, self.y, self.x, self.c, self.sibling, self.across_x, self.across_y, _ = where
        self.far = far_planes(self.z)
        self.near, self.one, self.two, self.last = {}, {}, {}, []

    def start(self, k):
        p = self.far[k]
        for i, (g, room) in enumerate(zip(self.sources, self.rooms)):
            self.near[k, i] = send(
                g.at[p, :, :, 1 - self.c], room.at[p, :, :, 0], self.sems, (0, k, self.first + i), self.sibling)

    def chip(self, k):
        p = self.far[k]
        for i, (g, room) in enumerate(zip(self.sources, self.rooms)):
            h = g.shape[-1] // 2
            self.near[k, i].wait_recv()
            room[p, :, :, 0] = plus(g[p, :, :, self.c], room[p, :, :, 0]).astype(LOW)
            self.one[k, i, 0] = send(room.at[p, :, 1 - self.x, 0, :, :h], room.at[p, 0, :, 1, :, :h], self.sems,
                                     (1, k, self.first + i), self.across_x)
            self.one[k, i, 1] = send(room.at[p, 1 - self.y, :, 0, :, h:], room.at[p, 0, :, 1, :, h:], self.sems,
                                     (2, k, self.first + i), self.across_y)

    def turn(self, k):
        p = self.far[k]
        for i, room in enumerate(self.rooms):
            h = room.shape[-1] // 2
            self.one[k, i, 0].wait_recv()
            room[p, 0, :, 1, :, :h] = plus(room[p, :, self.x, 0, :, :h], room[p, 0, :, 1, :, :h]).astype(LOW)
            self.two[k, i, 0] = send(room.at[p, 0, 1 - self.y, 1, :, :h], room.at[p, 1, 0, 1, :, :h], self.sems,
                                     (3, k, self.first + i), self.across_y)
            self.one[k, i, 1].wait_recv()
            room[p, 0, :, 1, :, h:] = plus(room[p, self.y, :, 0, :, h:], room[p, 0, :, 1, :, h:]).astype(LOW)
            self.two[k, i, 1] = send(room.at[p, 0, 1 - self.x, 1, :, h:], room.at[p, 1, 0, 1, :, h:], self.sems,
                                     (4, k, self.first + i), self.across_x)

    def leave(self, k):
        p = self.far[k]
        for i, (room, out) in enumerate(zip(self.rooms, self.outs)):
            h = room.shape[-1] // 2
            self.two[k, i, 0].wait_recv()
            self.two[k, i, 1].wait_recv()
            left = plus(room[p, 0, self.y, 1, :, :h], room[p, 1, 0, 1, :, :h])
            right = plus(room[p, 0, self.x, 1, :, h:], room[p, 1, 0, 1, :, h:])
            if k == 3:
                out[:, :h] = left
                out[:, h:] = right
                continue
            room[p, 1, 0, 1, :, :h] = left.astype(LOW)
            room[p, 1, 0, 1, :, h:] = right.astype(LOW)
            copy = pltpu.make_async_remote_copy(
                src_ref=room.at[p, 1, 0, 1], dst_ref=room.at[self.z, 1, 1, 1],
                send_sem=self.sems.at[0, 5, k, self.first + i], recv_sem=self.sems.at[1, 5, self.z, self.first + i],
                device_id={"patch": p * 2 + self.y, "rep": self.x * 2 + self.c}, device_id_type=MESH,
            )
            copy.start()
            self.last.append(copy)

    def end(self):
        for i, (room, out) in enumerate(zip(self.rooms, self.outs)):
            for k in range(3):
                p = self.far[k]
                come = room.at[p, 1, 1, 1]
                pltpu.make_async_remote_copy(
                    src_ref=come, dst_ref=come, send_sem=self.sems.at[0, 5, k, self.first + i],
                    recv_sem=self.sems.at[1, 5, p, self.first + i], device_id=self.sibling, device_id_type=MESH,
                ).wait_recv()
                out[...] = plus(out[...], room[p, 1, 1, 1])

    def drain(self):
        for copy in list(self.near.values()) + list(self.one.values()) + list(self.two.values()) + self.last:
            copy.wait_send()


def net_kernel(names, chan, gathered, numbers, counts, previous, noisy, target, noise, owners, decode_idx, near_idx,
               send_idx, waves, *rest):
    outs = rest[-4 - len(names) : -len(names)]
    weights, scratch = rest[: -4 - len(names)], rest[-len(names) :]
    r = types.SimpleNamespace(**dict(zip(names, scratch)))
    nodes, pixels = near_idx.shape[1], owners.shape[1]
    halo = send_idx.shape[0] // 2
    near = nodes + 2 * halo
    width, hidden = r.start.shape[1], r.gated.shape[1]
    at = [0, 3 * width, 4 * width, 4 * width + hidden, 4 * width + hidden + 256, 4 * width + hidden + 384]
    tile = 1024
    tiles = pixels // tile
    patches = lax.axis_size("patch")
    me = lax.axis_index("patch")
    lower, upper = {"patch": (me + patches - 1) % patches}, {"patch": (me + 1) % patches}
    barrier = pltpu.get_barrier_semaphore()
    others = [lower, upper]
    if not gathered:
        where = places()
        z, y, x, c, sibling, across_x, across_y, along_z = where
        folders = [sibling, across_x, across_y] + along_z[1:]
        plane_peers = [
            {"patch": z * 2 + (y + m // 4) % 2, "rep": ((x + m // 2 % 2) % 2) * 2 + (c + m % 2) % 2} for m in range(1, 8)]
        others += plane_peers + along_z[1:]
    for other in others:
        pl.semaphore_signal(barrier, inc=1, device_id=other, device_id_type=MESH)

    def load(src, dst, slot):
        copy = pltpu.make_async_copy(src, dst, r.loads.at[slot])
        copy.start()
        return copy

    pairs = ((previous, r.low_state), (noisy, r.state), (noise, r.extra))
    loads = [load(src, dst, slot) for slot, (src, dst) in enumerate(pairs)]
    rows_used = r.state.shape[0]
    w_at = [0, width, 3 * width, 4 * width, 4 * width + HALF_COLS, 4 * width + 2 * HALF_COLS, 4 * width + 3 * HALF_COLS]
    w_targets = (r.w_early, r.w_up, r.w_down)
    early_steps, late_steps = [], []
    if gathered:
        pl.semaphore_wait(barrier, len(others))
        for i, (src, dst) in enumerate(zip(weights, w_targets)):
            load(src, dst, 4 + i).wait()
    else:
        project, output, encode_prev, encode_noisy, decode, noise_rows, up, down = weights
        r.w_early[z, y, x, c, :, 4 * width :] = jnp.zeros((width // 32, width), LOW)
        for i, piece in ((0, project), (2, output), (3, encode_prev), (4, encode_noisy), (5, decode), (6, noise_rows)):
            r.w_early[z, y, x, c, :, w_at[i] : w_at[i] + piece.shape[1]] = piece[...].astype(LOW)
        r.w_up[z, y, x, c] = up[...].astype(LOW)
        r.w_down[z, y, x, c] = down[...].astype(LOW)
        early_steps = spread_steps(w_targets[:1], r.spread, 0, where)
        late_steps = spread_steps(w_targets[1:], r.spread, 1, where)
        pl.semaphore_wait(barrier, len(others))

    def advance(steps, count):
        for _ in range(min(count, len(steps))):
            steps.pop(0)()

    def early(first, last):
        return r.w_early[:, :, :, :, :, w_at[first] : (w_at + [5 * width])[last]].reshape(width, -1)

    def all_up():
        return r.w_up[...].reshape(width, hidden)

    advance(early_steps, 1)

    level = [numbers[4 * s] for s in range(2)]
    c_in = [numbers[4 * s + 1] for s in range(2)]
    c_skip = [numbers[4 * s + 2] for s in range(2)]
    c_out = [numbers[4 * s + 3] for s in range(2)]

    def build_hot(t):
        cols = block(t, tile)
        place = lax.broadcasted_iota(jnp.int32, (1, tile), 1) + t * tile
        own = jnp.where(place < counts[1], owners[:, cols], -1)
        three = [decode_idx[i : i + 1, cols] for i in range(3)]

        def rows(b):
            row = lax.broadcasted_iota(jnp.int32, (16, tile), 0) + b * 16
            r.owner_hot[block(b, 16), cols] = (row == own).astype(WIDE).astype(LOW)
            total = sum((row == idx).astype(WIDE) for idx in three)
            r.node_hot[block(b, 16), cols] = total.astype(LOW)

        loop(nodes // 16, rows)


    def build_bias(b):
        rows = block(b, 32)
        place = lax.broadcasted_iota(jnp.int32, (32, nodes), 0) + b * 32
        listed = jnp.zeros((32, nodes), WIDE)
        for j in range(1, NEIGH):
            listed = listed + (near_idx[j : j + 1] == place).astype(WIDE)
        listed = jnp.where((place >= nodes) | (place < counts[0]), listed, 0.0)
        listed = listed + (near_idx[0:1] == place).astype(WIDE)
        r.bias[rows] = jnp.where(listed > 0.0, jnp.log(jnp.maximum(listed, 1.0)), -1e30)

    loop(near // 32, build_bias)
    advance(early_steps, 4)
    advance(late_steps, 1)
    for t in range(tiles):
        build_hot(t)
        advance(early_steps, 2)
    r.send_hot[...] = (
        lax.broadcasted_iota(jnp.int32, (2 * halo, nodes), 1) == send_idx[...]
    ).astype(WIDE).astype(LOW)

    loads[0].wait()
    summed = nt(r.owner_hot[...], r.low_state[...])
    channel = lax.broadcasted_iota(jnp.int32, (nodes, HALF_COLS), 1)
    total = jnp.sum(jnp.where(channel == chan, summed, 0.0), axis=1, keepdims=True)
    r.inv_count[...] = 1.0 / jnp.maximum(total, 1.0)
    summed = jnp.where(channel < chan, summed, 0.0).astype(LOW)
    r.sums[:nodes, :HALF_COLS] = summed
    r.sums[nodes:, :HALF_COLS] = summed
    for copy in loads[1:]:
        copy.wait()
    r.low_state[:rows_used] = (r.state[...] * c_in[0]).astype(LOW)
    r.sums[:nodes, HALF_COLS:] = nt(r.owner_hot[...], r.low_state[...]).astype(LOW)
    advance(early_steps, len(early_steps))
    advance(late_steps, 3)

    noise_block = early(6, 7).astype(WIDE).reshape(32, 16, 128)
    lane = lax.broadcasted_iota(jnp.int32, (1, 128), 1)
    for s in range(2):
        parts = jnp.sum(noise_block * waves[s][None], axis=1)
        both = parts + pltpu.roll(parts, 64, 1)
        for k in range(16):
            piece = jnp.where(lane < 64, both[2 * k : 2 * k + 1], both[2 * k + 1 : 2 * k + 2])
            r.wave[s, k // 4 : k // 4 + 1, (k % 4) * 128 : (k % 4 + 1) * 128] = piece


    def pass_on(number, first, second):
        copies = []
        for i, (dst, device) in enumerate(((first, lower), (second, upper))):
            copy = pltpu.make_async_remote_copy(
                src_ref=r.outgoing.at[number, i * halo : (i + 1) * halo], dst_ref=dst,
                send_sem=r.links.at[0, number, i], recv_sem=r.links.at[1, number, i],
                device_id=device, device_id_type=MESH,
            )
            copy.start()
            copies.append(copy)
        return copies

    def encode(s):
        rows = slice(s * nodes, (s + 1) * nodes)
        if s:
            r.low_state[:rows_used] = (r.state[...] * c_in[s]).astype(LOW)
            r.sums[rows, HALF_COLS:] = nt(r.owner_hot[...], r.low_state[...]).astype(LOW)
        r.start[...] = nt(r.sums[rows], early(3, 5)) * r.inv_count[...]

        def norm(b):
            part = block(b, 64)
            unit, inverse = norm_parts(r.start[part])
            r.unit_one[s, part] = unit.astype(LOW)
            r.inv_one[s, part] = inverse
            scaled = unit * (1.0 + r.wave[s, 0:1]) + r.wave[s, 1:2]
            r.normed[pl.ds(pl.multiple_of(s * nodes + b * 64, 64), 64)] = scaled.astype(LOW)

        loop(nodes // 64, norm)
        normed = r.normed[rows]
        r.outgoing[s] = nn(r.send_hot[...], normed).astype(LOW)
        first = 2 * nodes + 2 * halo * s
        copies = pass_on(s, r.normed.at[first + halo : first + 2 * halo], r.normed.at[first : first + halo])
        r.queries[s] = nn(normed, early(0, 1)).astype(LOW)
        advance(late_steps, 1)
        r.extended[s, :nodes] = nn(normed, early(1, 2)).astype(LOW)
        advance(late_steps, 1)
        return copies

    def attend(s, copies):
        rows = slice(s * nodes, (s + 1) * nodes)
        for copy in copies:
            copy.wait()
        first = 2 * nodes + 2 * halo * s
        r.extended[s, nodes:] = nn(r.normed[first : first + 2 * halo], early(1, 2)).astype(LOW)
        for head in range(HEADS):
            cols = slice(head * HD, (head + 1) * HD)
            r.scores[...] = nt(r.extended[s, :, cols], r.queries[s, :, cols])

            def soft(b):
                part = block(b, 128)
                top = jnp.full((8, 128), -1e30, WIDE)
                for k in range(near // 64):
                    rows = slice(k * 64, (k + 1) * 64)
                    score = r.scores[rows, part] * SCALE + r.bias[rows, part]
                    r.scores[rows, part] = score
                    top = jnp.maximum(top, jnp.max(score.reshape(8, 8, 128), axis=0))
                top = jnp.max(top, axis=0, keepdims=True)
                total = jnp.zeros((8, 128), WIDE)
                for k in range(near // 64):
                    rows = slice(k * 64, (k + 1) * 64)
                    weight = jnp.exp(r.scores[rows, part] - top)
                    r.scores[rows, part] = weight
                    total = total + jnp.sum(weight.reshape(8, 8, 128), axis=0)
                total = 1.0 / jnp.sum(total, axis=0, keepdims=True)
                for k in range(near // 64):
                    rows = slice(k * 64, (k + 1) * 64)
                    r.probs[s, head, rows, part] = (r.scores[rows, part] * total).astype(LOW)

            loop(nodes // 128, soft)
            values = r.extended[s, :, width + head * HD : width + (head + 1) * HD]
            r.mixed[rows, cols] = tn(values, r.probs[s, head]).T.astype(LOW)
            advance(late_steps, 2)
        advance(late_steps, len(late_steps))
        r.start[...] += nn(r.mixed[rows], early(2, 3))

        def norm(b):
            part = block(b, 64)
            unit, inverse = norm_parts(r.start[part])
            r.unit_two[s, part] = unit.astype(LOW)
            r.inv_two[s, part] = inverse
            scaled = unit * (1.0 + r.wave[s, 2:3]) + r.wave[s, 3:4]
            r.second[pl.ds(pl.multiple_of(s * nodes + b * 64, 64), 64)] = scaled.astype(LOW)

        loop(nodes // 64, norm)

        def feed(j):
            cols = block(j, 256)
            upward = nn(r.second[rows], r.w_up[:, :, :, :, :, cols].reshape(width, 256))
            gate = 1.0 / (1.0 + jnp.exp(-upward))
            r.gated[rows, cols] = (upward * gate).astype(LOW)
            r.slope[rows, cols] = (gate * (1.0 + upward * (1.0 - gate))).astype(LOW)

        loop(hidden // 256, feed)
        r.final[rows] = (r.start[...] + nn(r.gated[rows], r.w_down[...].reshape(hidden, width))).astype(LOW)
        out = nn(r.final[rows], early(5, 6)) * (1.0 / 3.0)
        return out.T.astype(LOW)[:rows_used]

    def gradient(s):
        rows = slice(s * nodes, (s + 1) * nodes)
        taken = (nt(r.node_hot[...], r.low_state[...]) * (1.0 / 3.0)).astype(LOW)
        r.taken[rows] = taken
        d_final = nt(taken, early(5, 6))
        r.start[...] = d_final
        r.d_branch[rows] = d_final.astype(LOW)

        def feed(j):
            cols = block(j, 256)
            d_gated = nt(r.d_branch[rows], r.w_down[j // 2, j % 2].reshape(256, width))
            r.slope[rows, cols] = (d_gated * r.slope[rows, cols].astype(WIDE)).astype(LOW)

        loop(hidden // 256, feed)
        r.scores[:nodes, :width] = nt(r.slope[rows], all_up())
        if s == 0:
            announce(0)
        norm_gradient(s, r.unit_two, r.inv_two, 2)
        if s == 0:
            products_late()
        r.d_attn[rows] = r.start[...].astype(LOW)
        r.d_mixed[...] = nt(r.d_attn[rows], early(2, 3)).astype(LOW)
        first = 2 * nodes + 2 * halo * s
        far = slice(first, first + 2 * halo)
        for head in range(HEADS):
            cols = slice(head * HD, (head + 1) * HD)
            after = slice(width + head * HD, width + (head + 1) * HD)
            r.scores[...] = nt(r.extended[s, :, after], r.d_mixed[:, cols])

            def soft(b):
                part = block(b, 128)
                total = jnp.zeros((8, 128), WIDE)
                for k in range(near // 64):
                    rows = slice(k * 64, (k + 1) * 64)
                    slope = r.probs[s, head, rows, part].astype(WIDE) * r.scores[rows, part]
                    total = total + jnp.sum(slope.reshape(8, 8, 128), axis=0)
                total = jnp.sum(total, axis=0, keepdims=True)
                for k in range(near // 64):
                    rows = slice(k * 64, (k + 1) * 64)
                    slope = r.probs[s, head, rows, part].astype(WIDE) * (r.scores[rows, part] - total)
                    r.d_scores[rows, part] = (slope * SCALE).astype(LOW)

            loop(nodes // 128, soft)
            d_values = nn(r.probs[s, head], r.d_mixed[:, cols]).astype(LOW)
            d_keys = nn(r.d_scores[...], r.queries[s, :, cols]).astype(LOW)
            r.d_keyval[rows, after] = d_values[:nodes]
            r.d_keyval[far, after] = d_values[nodes:]
            r.d_keyval[rows, cols] = d_keys[:nodes]
            r.d_keyval[far, cols] = d_keys[nodes:]
            r.d_queries[rows, cols] = tn(r.extended[s, :, cols], r.d_scores[...]).T.astype(LOW)
            if s == 0:
                advance(fold_steps, 2)
        r.outgoing[2 + s] = nt(r.d_keyval[far], early(1, 2)).astype(LOW)
        copies = pass_on(2 + s, r.returned.at[s, halo:], r.returned.at[s, :halo])
        r.scores[:nodes, :width] = nt(r.d_queries[rows], early(0, 1)) + nt(r.d_keyval[rows], early(1, 2))
        return copies

    def norm_gradient(s, units, inverses, which):
        r.d_wave[s, which : which + 2] = jnp.zeros((2, width), WIDE)

        def norm(b):
            part = block(b, 64)
            unit = units[s, part].astype(WIDE)
            d_out = r.scores[part, :width]
            d_scale = jnp.sum(d_out * unit, axis=0, keepdims=True)
            d_shift = jnp.sum(d_out, axis=0, keepdims=True)
            r.d_wave[s, which : which + 1] += d_scale
            r.d_wave[s, which + 1 : which + 2] += d_shift
            d_unit = d_out * (1.0 + r.wave[s, which : which + 1])
            along = jnp.mean(d_unit * unit, axis=-1, keepdims=True)
            d_hidden = d_unit - jnp.mean(d_unit, axis=-1, keepdims=True) - unit * along
            r.start[part] += inverses[s, part] * d_hidden

        loop(nodes // 64, norm)

    def absorb(s, copies):
        rows = slice(s * nodes, (s + 1) * nodes)
        for copy in copies:
            copy.wait()
        r.scores[:nodes, :width] += tn(r.send_hot[...], r.returned[s])
        norm_gradient(s, r.unit_one, r.inv_one, 0)
        r.d_summed[rows] = (r.start[...] * r.inv_count[...]).astype(LOW)

    if not gathered:
        late = Fold((r.g_up, r.g_down), (r.w_up, r.w_down), outs[1:3], r.fold, 1, where)
        soon_fold = Fold((r.g_early,), (r.w_early,), outs[:1], r.fold, 0, where)
    fold_steps = []

    def announce(which):
        if not gathered:
            for other in folders:
                pl.semaphore_signal(r.ready.at[which], inc=1, device_id=other, device_id_type=MESH)

    def products_late():
        planes = range(4) if gathered else far_planes(z)
        for k, p in enumerate(planes):
            r.g_down[p] = tn(r.gated[:, block(p, hidden // 4)], r.d_branch[...]).astype(LOW).reshape(r.g_down.shape[1:])
            r.g_up[p] = tn(r.second[:, block(p, width // 4)], r.slope[...]).astype(LOW).reshape(r.g_up.shape[1:])
            if gathered:
                continue
            if k == 0:
                pl.semaphore_wait(r.ready.at[0], len(folders))
            late.start(k)
            if k > 0:
                late.chip(k - 1)
            if k > 1:
                late.turn(k - 2)
            if k > 2:
                late.leave(k - 3)
        if not gathered:
            do = functools.partial
            fold_steps.extend([
                do(late.chip, 3), do(late.turn, 2), do(late.leave, 1), do(late.turn, 3), do(late.leave, 2),
                do(late.leave, 3)])

    def put_early(i, first, value):
        value = value.astype(LOW)
        r.g_early[2 * i : 2 * i + 2, :, :, :, :, first : first + value.shape[1]] = value.reshape(
            (2, 2, 2, 2, width // 32, value.shape[1]))

    copies = encode(0)
    nodes_out = attend(0, copies)

    def decode_one(t):
        cols = block(t, tile)
        out = nn(nodes_out, r.node_hot[:, cols])
        r.state[:, cols] = c_skip[0] * r.state[:, cols] + c_out[0] * out + level[1] * r.extra[:, cols]

    loop(tiles, decode_one)
    load_target = load(target, r.extra, 3)
    copies = encode(1)
    nodes_out_two = attend(1, copies)
    r.lost[...] = jnp.zeros(r.lost.shape, WIDE)
    load_target.wait()

    def decode_two(t):
        cols = block(t, tile)
        out = nn(nodes_out_two, r.node_hot[:, cols])
        place = lax.broadcasted_iota(jnp.int32, (1, tile), 1) + t * tile
        error = c_skip[1] * r.state[:, cols] + c_out[1] * out - r.extra[:, cols]
        error = jnp.where(place < counts[1], error, 0.0)
        r.lost[...] += jnp.sum(error * error)
        r.extra[:, cols] = 2.0 * error
        r.low_state[:rows_used, cols] = (c_out[1] * 2.0 * error).astype(LOW)

    loop(tiles, decode_two)
    copies = gradient(1)
    absorb(1, copies)
    d_nodes = nn(r.d_summed[nodes:], early(4, 5))
    d_nodes = d_nodes.T.astype(LOW)[:rows_used]

    def into_one(t):
        cols = block(t, tile)
        d_noisy = c_skip[1] * r.extra[:, cols] + c_in[1] * nn(d_nodes, r.owner_hot[:, cols])
        r.low_state[:rows_used, cols] = (c_out[0] * d_noisy).astype(LOW)

    loop(tiles, into_one)
    copies = gradient(0)
    announce(1)
    for i in range(2):
        cols = slice(i * width // 2, (i + 1) * width // 2)
        put_early(i, 0, tn(r.normed[: 2 * nodes, cols], r.d_queries[...]))
        advance(fold_steps, 1)
        put_early(i, width, tn(r.normed[:, cols], r.d_keyval[...]))
        put_early(i, w_at[2], tn(r.mixed[:, cols], r.d_attn[...]))
        put_early(i, w_at[5], tn(r.final[:, cols], r.taken[...]))
        advance(fold_steps, 1)
    absorb(0, copies)
    advance(fold_steps, len(fold_steps))
    for i in range(2):
        put_early(i, w_at[3], tn(r.d_summed[:, i * width // 2 : (i + 1) * width // 2], r.sums[...]))
        total = jnp.zeros((16, 16, 128), WIDE)
        for s in range(2):
            pieces = []
            for k in range(8 * i, 8 * i + 8):
                piece = r.d_wave[s, k // 4 : k // 4 + 1, (k % 4) * 128 : (k % 4 + 1) * 128]
                turned = pltpu.roll(piece, 64, 1)
                pieces.append(jnp.where(lane < 64, piece, turned))
                pieces.append(jnp.where(lane < 64, turned, piece))
            total = total + jnp.concatenate(pieces, axis=0)[:, None, :] * waves[s][None]
        put_early(i, w_at[6], total.reshape(256, 128))
    if gathered:
        for i, src in enumerate((r.g_early, r.g_up, r.g_down)):
            load(src, outs[i], 4 + i).wait()
        outs[3][...] = r.lost[...]
        return

    pl.semaphore_wait(r.ready.at[1], len(folders))
    for k in range(4):
        soon_fold.start(k)
    for k in range(4):
        soon_fold.chip(k)
    late.end()
    squares = jnp.sum(outs[1][...] * outs[1][...]) + jnp.sum(outs[2][...] * outs[2][...])
    for k in range(4):
        soon_fold.turn(k)
    for k in range(4):
        soon_fold.leave(k)
    soon_fold.end()
    squares = squares + jnp.sum(outs[0][...] * outs[0][...])
    row = lax.broadcasted_iota(jnp.int32, (8, 128), 0)
    live = (chan * jnp.minimum(counts[1], pixels)).astype(WIDE)
    mine = y * 4 + x * 2 + c
    r.board[mine] = jnp.where(row == 0, squares, jnp.where(row == 1, r.lost[...], live))
    more = []
    for m, device in enumerate(plane_peers):
        more.append(send(r.board.at[mine], r.board.at[mine], r.small, (m,), device))
    for copy in more:
        copy.wait_recv()
    r.board[8 + z] = sum(r.board[m] for m in range(1, 8)) + r.board[0]
    level_copies = [send(r.board.at[8 + z], r.board.at[8 + z], r.small, (7 + d,), along_z[d]) for d in (1, 2, 3)]
    for copy in level_copies:
        copy.wait_recv()
    outs[3][...] = r.board[8] + r.board[9] + r.board[10] + r.board[11]
    late.drain()
    soon_fold.drain()
    for copy in more + level_copies:
        copy.wait_send()


def run_net(chan, gathered, numbers, counts, previous, noisy, target, noise, owners, decode_idx, near_idx, send_idx,
            waves, width, hidden, weights):
    nodes, pixels = near_idx.shape[1], owners.shape[1]
    scratch = net_scratch(nodes, send_idx.shape[0] // 2, pixels, width, hidden, noisy.shape[0])
    vmem, smem = pl.BlockSpec(memory_space=pltpu.VMEM), pl.BlockSpec(memory_space=pltpu.SMEM)
    hbm = pl.BlockSpec(memory_space=pl.ANY)
    if gathered:
        results = [(GRID + (width // 32, 5 * width), LOW), (GRID + (width // 32, hidden), LOW), (GRID + (hidden // 32, width), LOW)]
    else:
        results = [((width // 32, 5 * width), WIDE), ((width // 32, hidden), WIDE), ((hidden // 32, width), WIDE)]
    return pl.pallas_call(
        functools.partial(net_kernel, tuple(scratch), chan, gathered),
        out_shape=[jax.ShapeDtypeStruct(shape, kind) for shape, kind in results + [((8, 128), WIDE)]],
        in_specs=[smem] * 2 + [hbm] * 4 + [vmem] * 5 + [hbm if gathered else vmem] * len(weights),
        out_specs=[hbm if gathered else vmem] * 3 + [vmem],
        scratch_shapes=list(scratch.values()),
        compiler_params=pltpu.CompilerParams(
            collective_id=3, has_side_effects=True, vmem_limit_bytes=VMEM_LIMIT),
    )(numbers, counts, previous, noisy, target, noise, owners, decode_idx, near_idx, send_idx, waves, *weights)


def fill(array, columns):
    return jnp.pad(array, ((0, 0), (0, columns - array.shape[1])))


def on_device(
    previous_state, target_state, noise_draws, noise_level, pixel_owner, mesh_to_grid, neighbours, halo_send,
    node_count, pixel_count, w_encode, w_project, w_output, w_up, w_down, w_noise, w_decode,
    m_encode, m_project, m_output, m_up, m_down, m_noise, m_decode,
    v_encode, v_project, v_output, v_up, v_down, v_noise, v_decode,
):
    width = w_project.shape[1] // 3
    hidden = w_up.shape[1]
    channels = previous_state.shape[1]
    rows = w_project.shape[0]
    small_slice = lax.axis_size("patch") == 8 and lax.axis_size("rep") == 4
    flipped = w_encode.T
    halves = (flipped[:, :channels], flipped[:, channels:])
    if small_slice:
        weights = (w_project, w_output) + halves + (w_decode, w_noise.reshape(rows, HALF_COLS), w_up, w_down)
    else:
        pieces = [w_project, w_output] + [fill(half, HALF_COLS) for half in halves] + [fill(w_decode, HALF_COLS)]
        early = lax.all_gather(jnp.concatenate(pieces, axis=1).astype(LOW), BOTH, axis=0, tiled=True)
        noise = lax.all_gather(w_noise.astype(LOW), BOTH, axis=1, tiled=True).reshape(FOUR, -1, 64)
        early = jnp.concatenate([early, noise.transpose(1, 0, 2).reshape(width, HALF_COLS)], axis=1)
        all_up = lax.all_gather(w_up.astype(LOW), BOTH, axis=0, tiled=True)
        all_down = lax.all_gather(w_down.astype(LOW), BOTH, axis=0, tiled=True)
        weights = [w.reshape(GRID + (-1, w.shape[1])) for w in (early, all_up, all_down)]
    at = [0, 3 * width, 4 * width] + [4 * width + HALF_COLS * i for i in range(1, 4)]

    levels = noise_level[0]
    pixels = pixel_owner.shape[1]
    padding = ((0, -channels % 16), (0, 0))
    previous = jnp.concatenate([previous_state[0], jnp.ones((1, pixels), WIDE)], axis=0).astype(LOW)
    previous = jnp.pad(previous, ((0, HALF_COLS - channels - 1), (0, 0)))
    target = jnp.pad(target_state[0], padding)
    noisy = jnp.pad(target_state[0] + levels[0] * noise_draws[0, 0], padding)
    noise_two = jnp.pad(noise_draws[0, 1], padding)
    c_in = lax.rsqrt(levels * levels + 1.0)
    numbers = jnp.stack([levels, c_in, 1.0 / (levels * levels + 1.0), levels * c_in], axis=1).reshape(8)
    counts = jnp.concatenate([node_count[0], pixel_count[0]])
    waves = jnp.stack([fourier(levels[i]).reshape(FOUR // 2, 2) for i in range(2)])
    waves = jnp.repeat(waves, 64, axis=2)
    s_early, s_up, s_down, totals = run_net(
        channels, not small_slice, numbers, counts, previous, noisy, target, noise_two, pixel_owner, mesh_to_grid[0],
        neighbours[0].T, halo_send.reshape(-1, 1), waves, width, hidden, weights,
    )
    if small_slice:
        totals = totals[:3, 0]
        s_noise = s_early[:, at[5] :].reshape(FOUR, -1)
    else:
        g_early = s_early.reshape(width, -1)
        g_noise = g_early[:, at[5] :].reshape(-1, FOUR, 64).transpose(1, 0, 2).reshape(FOUR, -1)
        parts = (g_early[:, : at[5]], s_up.reshape(width, -1), s_down.reshape(hidden, -1))
        s_early, s_up, s_down = (
            lax.psum_scatter(g.astype(WIDE), BOTH, scatter_dimension=0, tiled=True) for g in parts)
        s_noise = lax.psum_scatter(g_noise.astype(WIDE), BOTH, scatter_dimension=1, tiled=True)
        squares = sum(jnp.sum(shard * shard) for shard in (s_early, s_up, s_down, s_noise))
        count_local = (channels * jnp.minimum(pixel_count[0, 0], pixels)).astype(WIDE)
        totals = lax.psum((squares, totals[0, 0], count_local), BOTH)
    shards = (
        jnp.concatenate([s_early[:, at[2] : at[2] + channels], s_early[:, at[3] : at[3] + channels]], axis=1).T,
        s_early[:, : at[1]],
        s_early[:, at[1] : at[2]],
        s_up,
        s_down,
        s_noise,
        s_early[:, at[4] : at[4] + channels],
    )
    grad_norm = jnp.sqrt(totals[0])
    factor = THRESHOLD / jnp.maximum(grad_norm, THRESHOLD)
    masters = (w_encode, w_project, w_output, w_up, w_down, w_noise, w_decode)
    moments = (m_encode, m_project, m_output, m_up, m_down, m_noise, m_decode)
    seconds = (v_encode, v_project, v_output, v_up, v_down, v_noise, v_decode)
    new_weights, new_moments, new_seconds = ([], [], [])
    for w, m, v, g in zip(masters, moments, seconds, shards):
        clipped = g * factor
        moment = BETA_ONE * m + (1.0 - BETA_ONE) * clipped
        variance = BETA_TWO * v + (1.0 - BETA_TWO) * clipped * clipped
        stepped = (
            moment
            / (1.0 - BETA_ONE**STEP)
            / (jnp.sqrt(variance / (1.0 - BETA_TWO**STEP)) + EPSILON)
        )
        new_weights.append(w - LEARN_RATE * (stepped + DECAY_RATE * w))
        new_moments.append(moment)
        new_seconds.append(variance)
    return (
        tuple(new_weights)
        + tuple(new_moments)
        + tuple(new_seconds)
        + (totals[1], totals[2], grad_norm)
    )


def solution(mesh):
    in_specs = (
        P("rep", None, "patch"),
        P("rep", None, "patch"),
        P("rep", None, None, "patch"),
        P("rep", None),
        P("rep", "patch"),
        P("rep", None, "patch"),
        P("rep", "patch", None),
        P("rep", "patch"),
        P("rep", "patch"),
        P("rep", "patch"),
        P(None, ("patch", "rep")),
        P(("patch", "rep"), None),
        P(("patch", "rep"), None),
        P(("patch", "rep"), None),
        P(("patch", "rep"), None),
        P(None, ("patch", "rep")),
        P(("patch", "rep"), None),
        P(None, ("patch", "rep")),
        P(("patch", "rep"), None),
        P(("patch", "rep"), None),
        P(("patch", "rep"), None),
        P(("patch", "rep"), None),
        P(None, ("patch", "rep")),
        P(("patch", "rep"), None),
        P(None, ("patch", "rep")),
        P(("patch", "rep"), None),
        P(("patch", "rep"), None),
        P(("patch", "rep"), None),
        P(("patch", "rep"), None),
        P(None, ("patch", "rep")),
        P(("patch", "rep"), None),
    )
    out_specs = (
        P(None, ("patch", "rep")),
        P(("patch", "rep"), None),
        P(("patch", "rep"), None),
        P(("patch", "rep"), None),
        P(("patch", "rep"), None),
        P(None, ("patch", "rep")),
        P(("patch", "rep"), None),
        P(None, ("patch", "rep")),
        P(("patch", "rep"), None),
        P(("patch", "rep"), None),
        P(("patch", "rep"), None),
        P(("patch", "rep"), None),
        P(None, ("patch", "rep")),
        P(("patch", "rep"), None),
        P(None, ("patch", "rep")),
        P(("patch", "rep"), None),
        P(("patch", "rep"), None),
        P(("patch", "rep"), None),
        P(("patch", "rep"), None),
        P(None, ("patch", "rep")),
        P(("patch", "rep"), None),
        P(),
        P(),
        P(),
    )
    return jax.shard_map(
        on_device, mesh=mesh, in_specs=in_specs, out_specs=out_specs, check_vma=False
    )
```

```python
import functools
import types

import jax
import jax.numpy as jnp
from jax import lax
from jax.experimental import pallas as pl
from jax.experimental.pallas import tpu as pltpu
from jax.sharding import PartitionSpec as P

HEADS = 4
HD = 128
FOUR = 32
NEIGH = 16
STEP = 5


LEARN_RATE = 0.03
BETA_ONE = 0.9
BETA_TWO = 0.95
EPSILON = 1e-08
DECAY_RATE = 0.1
THRESHOLD = 1.0

BOTH = ("patch", "rep")
LOW = jnp.bfloat16
WIDE = jnp.float32
SCALE = HD ** (-0.5)
VMEM_LIMIT = 64 * 2**20


def nn(a, b):
    return lax.dot_general(a, b, (((1,), (0,)), ((), ())), preferred_element_type=WIDE)


def nt(a, b):
    return lax.dot_general(a, b, (((1,), (1,)), ((), ())), preferred_element_type=WIDE)


def tn(a, b):
    return lax.dot_general(a, b, (((0,), (0,)), ((), ())), preferred_element_type=WIDE)


def norm_parts(hidden):
    centre = hidden - jnp.mean(hidden, axis=-1, keepdims=True)
    spread = jnp.mean(centre * centre, axis=-1, keepdims=True)
    inverse = lax.rsqrt(spread + 1e-05)
    return centre * inverse, inverse


MESH = pl.DeviceIdType.MESH
GRID = (4, 2, 2, 2)


def places():
    patch, rep = lax.axis_index("patch"), lax.axis_index("rep")
    z, y, x, c = patch // 2, patch % 2, rep // 2, rep % 2
    sibling = {"patch": patch, "rep": x * 2 + (1 - c)}
    across_x = {"patch": patch, "rep": (1 - x) * 2 + c}
    across_y = {"patch": z * 2 + (1 - y), "rep": rep}
    along_z = [{"patch": ((z + d) % 4) * 2 + y, "rep": rep} for d in range(4)]
    return z, y, x, c, sibling, across_x, across_y, along_z


def send(src, dst, sems, index, device):
    copy = pltpu.make_async_remote_copy(
        src_ref=src, dst_ref=dst, send_sem=sems.at[(0,) + index], recv_sem=sems.at[(1,) + index],
        device_id=device, device_id_type=MESH,
    )
    copy.start()
    return copy


def plus(*terms):
    total = terms[0].astype(WIDE)
    for term in terms[1:]:
        total = total + term.astype(WIDE)
    return total


HALF_COLS = 128


def net_scratch(nodes, halo, pixels, width, hidden, kept):
    near = nodes + 2 * halo
    return dict(
        owner_hot=pltpu.VMEM((nodes, pixels), LOW),
        node_hot=pltpu.VMEM((nodes, pixels), LOW),
        bias=pltpu.VMEM((near, nodes), WIDE),
        send_hot=pltpu.VMEM((nodes, 2 * halo), LOW),
        inv_count=pltpu.VMEM((nodes, 1), WIDE),
        sums=pltpu.VMEM((2 * nodes, 2 * HALF_COLS), LOW),
        wave=pltpu.VMEM((2, 4, width), WIDE),
        d_wave=pltpu.VMEM((2, 4, width), WIDE),
        start=pltpu.VMEM((nodes, width), WIDE),
        unit_one=pltpu.VMEM((2, nodes, width), LOW),
        inv_one=pltpu.VMEM((2, nodes, 1), WIDE),
        normed=pltpu.VMEM((2 * near, width), LOW),
        queries=pltpu.VMEM((2, nodes, width), LOW),
        extended=pltpu.VMEM((2, near, 2 * width), LOW),
        probs=pltpu.VMEM((2, HEADS, near, nodes), LOW),
        mixed=pltpu.VMEM((2 * nodes, width), LOW),
        unit_two=pltpu.VMEM((2, nodes, width), LOW),
        inv_two=pltpu.VMEM((2, nodes, 1), WIDE),
        second=pltpu.VMEM((2 * nodes, width), LOW),
        gated=pltpu.VMEM((2 * nodes, hidden), LOW),
        slope=pltpu.VMEM((2 * nodes, hidden), LOW),
        final=pltpu.VMEM((2 * nodes, width), LOW),
        taken=pltpu.VMEM((2 * nodes, HALF_COLS), LOW),
        d_branch=pltpu.VMEM((2 * nodes, width), LOW),
        d_attn=pltpu.VMEM((2 * nodes, width), LOW),
        d_queries=pltpu.VMEM((2 * nodes, width), LOW),
        d_keyval=pltpu.VMEM((2 * near, 2 * width), LOW),
        d_summed=pltpu.VMEM((2 * nodes, width), LOW),
        d_mixed=pltpu.VMEM((nodes, width), LOW),
        d_scores=pltpu.VMEM((near, nodes), LOW),
        scores=pltpu.VMEM((near, nodes), WIDE),
        outgoing=pltpu.VMEM((4, 2 * halo, width), LOW),
        returned=pltpu.VMEM((2, 2 * halo, width), LOW),
        state=pltpu.VMEM((kept, pixels), WIDE),
        extra=pltpu.VMEM((kept, pixels), WIDE),
        low_state=pltpu.VMEM((kept, pixels), LOW),
        g_early=pltpu.VMEM(GRID + (width // 32, 5 * width), LOW),
        g_up=pltpu.VMEM(GRID + (width // 32, hidden), LOW),
        g_down=pltpu.VMEM(GRID + (hidden // 32, width), LOW),
        lost=pltpu.VMEM((8, 128), WIDE),
        noise_rows=pltpu.VMEM((FOUR // 2, 128), WIDE),
        waves=pltpu.VMEM((2, FOUR // 2, 128), WIDE),
        board=pltpu.VMEM((12, 8, 128), WIDE),
        w_early=pltpu.VMEM(GRID + (width // 32, 5 * width), LOW),
        w_up=pltpu.VMEM(GRID + (width // 32, hidden), LOW),
        w_down=pltpu.VMEM(GRID + (hidden // 32, width), LOW),
        loads=pltpu.SemaphoreType.DMA((7,)),
        ready=pltpu.SemaphoreType.REGULAR((2,)),
        fold=pltpu.SemaphoreType.DMA((2, 6, 4, 3)),
        small=pltpu.SemaphoreType.DMA((2, 12)),
        links=pltpu.SemaphoreType.DMA((2, 4, 2)),
        spread=pltpu.SemaphoreType.DMA((2, 6, 4, 3)),
    )


def loop(count, body):
    def step(i, carry):
        body(i)
        return carry

    lax.fori_loop(0, count, step, 0)


def block(index, size):
    return pl.ds(pl.multiple_of(index * size, size), size)


def spread_steps(arrays, sems, first, where):
    z, y, x, c, sibling, across_x, across_y, along_z = where
    planes, x_one, y_one, x_two, y_two, core = {}, {}, {}, {}, {}, {}

    def plane_of(d):
        return (z - d + 4) % 4

    def cross(d):
        for i, out in enumerate(arrays):
            h = out.shape[-1] // 2
            here_l, here_r = out.at[plane_of(d), y, x, c, :, :h], out.at[plane_of(d), y, x, c, :, h:]
            x_one[d, i] = send(here_l, here_l, sems, (1, d, first + i), across_x)
            y_one[d, i] = send(here_r, here_r, sems, (2, d, first + i), across_y)

    def begin():
        for i, out in enumerate(arrays):
            mine = out.at[z, y, x, c]
            for d in (1, 3, 2):
                planes[d, i] = send(mine, mine, sems, (0, d, first + i), along_z[d])
        cross(0)

    def arrive(d):
        for i in range(len(arrays)):
            planes[d, i].wait_recv()
        cross(d)

    def turn(d):
        for i, out in enumerate(arrays):
            h = out.shape[-1] // 2
            x_one[d, i].wait_recv()
            both = out.at[plane_of(d), y, :, c, :, :h]
            y_two[d, i] = send(both, both, sems, (3, d, first + i), across_y)
            y_one[d, i].wait_recv()
            both = out.at[plane_of(d), :, x, c, :, h:]
            x_two[d, i] = send(both, both, sems, (4, d, first + i), across_x)

    def share(d):
        for i, out in enumerate(arrays):
            y_two[d, i].wait_recv()
            x_two[d, i].wait_recv()
            plane = out.at[plane_of(d), :, :, c]
            core[d, i] = send(plane, plane, sems, (5, d, first + i), sibling)

    def end():
        for group in (planes, x_one, y_one, x_two, y_two):
            for copy in group.values():
                copy.wait_send()
        for copy in core.values():
            copy.wait()

    do = functools.partial
    return [begin, do(arrive, 1), do(arrive, 3), do(turn, 0), do(arrive, 2), do(turn, 1), do(turn, 3), do(share, 0),
            do(turn, 2), do(share, 1), do(share, 3), do(share, 2), end]


def far_planes(z):
    return [3 * (1 - z // 2), 2 - z // 2, z + 1 - 2 * (z % 2), z]


class Fold:
    def __init__(self, sources, rooms, outs, sems, first, where):
        self.sources, self.rooms, self.outs, self.sems, self.first = sources, rooms, outs, sems, first
        self.z, self.y, self.x, self.c, self.sibling, self.across_x, self.across_y, _ = where
        self.far = far_planes(self.z)
        self.near, self.one, self.two, self.last = {}, {}, {}, []

    def start(self, k):
        p = self.far[k]
        for i, (g, room) in enumerate(zip(self.sources, self.rooms)):
            self.near[k, i] = send(
                g.at[p, :, :, 1 - self.c], room.at[p, :, :, 0], self.sems, (0, k, self.first + i), self.sibling)

    def chip(self, k):
        p = self.far[k]
        for i, (g, room) in enumerate(zip(self.sources, self.rooms)):
            h = g.shape[-1] // 2
            self.near[k, i].wait_recv()
            room[p, :, :, 0] = plus(g[p, :, :, self.c], room[p, :, :, 0]).astype(LOW)
            self.one[k, i, 0] = send(room.at[p, :, 1 - self.x, 0, :, :h], room.at[p, 0, :, 1, :, :h], self.sems,
                                     (1, k, self.first + i), self.across_x)
            self.one[k, i, 1] = send(room.at[p, 1 - self.y, :, 0, :, h:], room.at[p, 0, :, 1, :, h:], self.sems,
                                     (2, k, self.first + i), self.across_y)

    def turn(self, k):
        p = self.far[k]
        for i, room in enumerate(self.rooms):
            h = room.shape[-1] // 2
            self.one[k, i, 0].wait_recv()
            room[p, 0, :, 1, :, :h] = plus(room[p, :, self.x, 0, :, :h], room[p, 0, :, 1, :, :h]).astype(LOW)
            self.two[k, i, 0] = send(room.at[p, 0, 1 - self.y, 1, :, :h], room.at[p, 1, 0, 1, :, :h], self.sems,
                                     (3, k, self.first + i), self.across_y)
            self.one[k, i, 1].wait_recv()
            room[p, 0, :, 1, :, h:] = plus(room[p, self.y, :, 0, :, h:], room[p, 0, :, 1, :, h:]).astype(LOW)
            self.two[k, i, 1] = send(room.at[p, 0, 1 - self.x, 1, :, h:], room.at[p, 1, 0, 1, :, h:], self.sems,
                                     (4, k, self.first + i), self.across_x)

    def leave(self, k):
        p = self.far[k]
        for i, (room, out) in enumerate(zip(self.rooms, self.outs)):
            h = room.shape[-1] // 2
            self.two[k, i, 0].wait_recv()
            self.two[k, i, 1].wait_recv()
            left = plus(room[p, 0, self.y, 1, :, :h], room[p, 1, 0, 1, :, :h])
            right = plus(room[p, 0, self.x, 1, :, h:], room[p, 1, 0, 1, :, h:])
            if k == 3:
                out[:, :h] = left
                out[:, h:] = right
                continue
            room[p, 1, 0, 1, :, :h] = left.astype(LOW)
            room[p, 1, 0, 1, :, h:] = right.astype(LOW)
            copy = pltpu.make_async_remote_copy(
                src_ref=room.at[p, 1, 0, 1], dst_ref=room.at[self.z, 1, 1, 1],
                send_sem=self.sems.at[0, 5, k, self.first + i], recv_sem=self.sems.at[1, 5, self.z, self.first + i],
                device_id={"patch": p * 2 + self.y, "rep": self.x * 2 + self.c}, device_id_type=MESH,
            )
            copy.start()
            self.last.append(copy)

    def end(self):
        for i, (room, out) in enumerate(zip(self.rooms, self.outs)):
            for k in range(3):
                p = self.far[k]
                come = room.at[p, 1, 1, 1]
                pltpu.make_async_remote_copy(
                    src_ref=come, dst_ref=come, send_sem=self.sems.at[0, 5, k, self.first + i],
                    recv_sem=self.sems.at[1, 5, p, self.first + i], device_id=self.sibling, device_id_type=MESH,
                ).wait_recv()
                out[...] = plus(out[...], room[p, 1, 1, 1])

    def drain(self):
        for copy in list(self.near.values()) + list(self.one.values()) + list(self.two.values()) + self.last:
            copy.wait_send()


def net_kernel(names, gathered, levels, node_count, pixel_count, previous, noisy, target, noise, owners, decode_idx,
               near_idx, send_idx, *rest):
    outs = rest[-4 - len(names) : -len(names)]
    weights, scratch = rest[: -4 - len(names)], rest[-len(names) :]
    r = types.SimpleNamespace(**dict(zip(names, scratch)))
    nodes, pixels = near_idx.shape[1], owners.shape[1]
    waves = r.waves
    halo, chan = send_idx.shape[1] // 2, previous.shape[0]
    near = nodes + 2 * halo
    width, hidden = r.start.shape[1], r.gated.shape[1]
    at = [0, 3 * width, 4 * width, 4 * width + hidden, 4 * width + hidden + 256, 4 * width + hidden + 384]
    tile = 1024
    tiles = pixels // tile
    patches = lax.axis_size("patch")
    me = lax.axis_index("patch")
    lower, upper = {"patch": (me + patches - 1) % patches}, {"patch": (me + 1) % patches}
    barrier = pltpu.get_barrier_semaphore()
    others = [lower, upper]
    if not gathered:
        where = places()
        z, y, x, c, sibling, across_x, across_y, along_z = where
        folders = [sibling, across_x, across_y] + along_z[1:]
        plane_peers = [
            {"patch": z * 2 + (y + m // 4) % 2, "rep": ((x + m // 2 % 2) % 2) * 2 + (c + m % 2) % 2} for m in range(1, 8)]
        others += plane_peers + along_z[1:]
    for other in others:
        pl.semaphore_signal(barrier, inc=1, device_id=other, device_id_type=MESH)

    def load(src, dst, slot):
        copy = pltpu.make_async_copy(src, dst, r.loads.at[slot])
        copy.start()
        return copy

    loads = [load(previous, r.extra, 0), load(noisy, r.state, 1)]
    w_at = [0, width, 3 * width, 4 * width, 4 * width + HALF_COLS, 4 * width + 2 * HALF_COLS, 4 * width + 3 * HALF_COLS]
    w_targets = (r.w_early, r.w_up, r.w_down)
    early_steps, late_steps = [], []
    if gathered:
        pl.semaphore_wait(barrier, len(others))
        for i, (src, dst) in enumerate(zip(weights, w_targets)):
            load(src, dst, 4 + i).wait()
    else:
        project, output, encode_prev, encode_noisy, decode, noise_rows, up, down = weights
        for i in range(FOUR // 2):
            r.noise_rows[i : i + 1, :64] = noise_rows[2 * i : 2 * i + 1]
            r.noise_rows[i : i + 1, 64:] = noise_rows[2 * i + 1 : 2 * i + 2]
        noise_rows = r.noise_rows
        r.w_early[z, y, x, c, :, 4 * width :] = jnp.zeros((width // 32, width), LOW)
        for i, piece in ((0, project), (2, output), (3, encode_prev), (4, encode_noisy), (5, decode), (6, noise_rows)):
            r.w_early[z, y, x, c, :, w_at[i] : w_at[i] + piece.shape[1]] = piece[...].astype(LOW)
        r.w_up[z, y, x, c] = up[...].astype(LOW)
        r.w_down[z, y, x, c] = down[...].astype(LOW)
        early_steps = spread_steps(w_targets[:1], r.spread, 0, where)
        late_steps = spread_steps(w_targets[1:], r.spread, 1, where)
        pl.semaphore_wait(barrier, len(others))

    def encode_state(s):
        r.low_state[...] = (r.state[...] * c_in[s]).astype(LOW)
        r.sums[s * nodes : (s + 1) * nodes, HALF_COLS : HALF_COLS + chan] = nt(
            r.owner_hot[...], r.low_state[...]).astype(LOW)

    def advance(steps, count):
        for _ in range(min(count, len(steps))):
            steps.pop(0)()

    def early(first, last):
        return r.w_early[:, :, :, :, :, w_at[first] : (w_at + [5 * width])[last]].reshape(width, -1)

    def all_up():
        return r.w_up[...].reshape(width, hidden)

    advance(early_steps, 1)

    level = [levels[0, s] for s in range(2)]
    c_in, c_skip, c_out = [], [], []
    for s in range(2):
        whole = jnp.full((8, 128), level[s], WIDE)
        scaled = lax.rsqrt(whole * whole + 1.0)
        c_in.append(scaled[:1, :1])
        c_skip.append((1.0 / (whole * whole + 1.0))[:1, :1])
        c_out.append((whole * scaled)[:1, :1])
        shape = (FOUR // 2, 128)
        feature = 2 * lax.broadcasted_iota(jnp.int32, shape, 0) + lax.broadcasted_iota(jnp.int32, shape, 1) // 64
        frequency = 0.25 * ((feature % (FOUR // 2)).astype(WIDE) + 1.0)
        angle = jnp.log(jnp.full(shape, level[s], WIDE)) * frequency
        waves[s] = jnp.where(feature < FOUR // 2, jnp.sin(angle), jnp.cos(angle))

    def build_hot(t):
        cols = block(t, tile)
        place = lax.broadcasted_iota(jnp.int32, (1, tile), 1) + t * tile
        own = jnp.where(place < pixel_count[0], owners[:, cols], -1)
        three = [decode_idx[i : i + 1, cols] for i in range(3)]

        def rows(b):
            row = lax.broadcasted_iota(jnp.int32, (16, tile), 0) + b * 16
            r.owner_hot[block(b, 16), cols] = (row == own).astype(WIDE).astype(LOW)
            total = sum((row == idx).astype(WIDE) for idx in three)
            r.node_hot[block(b, 16), cols] = total.astype(LOW)

        loop(nodes // 16, rows)


    def build_bias(b):
        rows = block(b, 32)
        place = lax.broadcasted_iota(jnp.int32, (32, nodes), 0) + b * 32
        listed = jnp.zeros((32, nodes), WIDE)
        for j in range(1, NEIGH):
            listed = listed + (near_idx[j : j + 1] == place).astype(WIDE)
        listed = jnp.where((place >= nodes) | (place < node_count[0]), listed, 0.0)
        listed = listed + (near_idx[0:1] == place).astype(WIDE)
        r.bias[rows] = jnp.where(listed > 0.0, jnp.log(jnp.maximum(listed, 1.0)), -1e30)

    loop(near // 32, build_bias)
    advance(early_steps, 4)
    advance(late_steps, 1)
    for t in range(tiles):
        build_hot(t)
        advance(early_steps, 2)
    r.send_hot[...] = (
        lax.broadcasted_iota(jnp.int32, (nodes, 2 * halo), 0) == send_idx[...]
    ).astype(WIDE).astype(LOW)

    loads[0].wait()
    total = nt(r.owner_hot[...], jnp.ones((8, pixels), LOW))[:, :1]
    r.inv_count[...] = 1.0 / jnp.maximum(total, 1.0)
    r.sums[...] = jnp.zeros(r.sums.shape, LOW)
    r.taken[...] = jnp.zeros(r.taken.shape, LOW)
    r.low_state[...] = r.extra[...].astype(LOW)
    load_noise = load(noise, r.extra, 2)
    summed = nt(r.owner_hot[...], r.low_state[...]).astype(LOW)
    r.sums[:nodes, :chan] = summed
    r.sums[nodes:, :chan] = summed
    loads[1].wait()
    encode_state(0)
    advance(early_steps, len(early_steps))
    advance(late_steps, 3)

    noise_block = early(6, 7).astype(WIDE).reshape(32, 16, 128)
    lane = lax.broadcasted_iota(jnp.int32, (1, 128), 1)
    for s in range(2):
        parts = jnp.sum(noise_block * waves[s][None], axis=1)
        both = parts + pltpu.roll(parts, 64, 1)
        for k in range(16):
            piece = jnp.where(lane < 64, both[2 * k : 2 * k + 1], both[2 * k + 1 : 2 * k + 2])
            r.wave[s, k // 4 : k // 4 + 1, (k % 4) * 128 : (k % 4 + 1) * 128] = piece


    def pass_on(number, first, second):
        copies = []
        for i, (dst, device) in enumerate(((first, lower), (second, upper))):
            copy = pltpu.make_async_remote_copy(
                src_ref=r.outgoing.at[number, i * halo : (i + 1) * halo], dst_ref=dst,
                send_sem=r.links.at[0, number, i], recv_sem=r.links.at[1, number, i],
                device_id=device, device_id_type=MESH,
            )
            copy.start()
            copies.append(copy)
        return copies

    def encode(s):
        rows = slice(s * nodes, (s + 1) * nodes)
        if s:
            encode_state(s)
        r.start[...] = nt(r.sums[rows], early(3, 5)) * r.inv_count[...]

        def norm(b):
            part = block(b, 64)
            unit, inverse = norm_parts(r.start[part])
            r.unit_one[s, part] = unit.astype(LOW)
            r.inv_one[s, part] = inverse
            scaled = unit * (1.0 + r.wave[s, 0:1]) + r.wave[s, 1:2]
            r.normed[pl.ds(pl.multiple_of(s * nodes + b * 64, 64), 64)] = scaled.astype(LOW)

        loop(nodes // 64, norm)
        normed = r.normed[rows]
        r.outgoing[s] = tn(r.send_hot[...], normed).astype(LOW)
        first = 2 * nodes + 2 * halo * s
        copies = pass_on(s, r.normed.at[first + halo : first + 2 * halo], r.normed.at[first : first + halo])
        r.queries[s] = nn(normed, early(0, 1)).astype(LOW)
        advance(late_steps, 1)
        r.extended[s, :nodes] = nn(normed, early(1, 2)).astype(LOW)
        advance(late_steps, 1)
        return copies

    def attend(s, copies):
        rows = slice(s * nodes, (s + 1) * nodes)
        for copy in copies:
            copy.wait()
        first = 2 * nodes + 2 * halo * s
        r.extended[s, nodes:] = nn(r.normed[first : first + 2 * halo], early(1, 2)).astype(LOW)
        for head in range(HEADS):
            cols = slice(head * HD, (head + 1) * HD)
            r.scores[...] = nt(r.extended[s, :, cols], r.queries[s, :, cols])

            def soft(b):
                part = block(b, 128)
                top = jnp.full((8, 128), -1e30, WIDE)
                for k in range(near // 64):
                    rows = slice(k * 64, (k + 1) * 64)
                    score = r.scores[rows, part] * SCALE + r.bias[rows, part]
                    r.scores[rows, part] = score
                    top = jnp.maximum(top, jnp.max(score.reshape(8, 8, 128), axis=0))
                top = jnp.max(top, axis=0, keepdims=True)
                total = jnp.zeros((8, 128), WIDE)
                for k in range(near // 64):
                    rows = slice(k * 64, (k + 1) * 64)
                    weight = jnp.exp(r.scores[rows, part] - top)
                    r.scores[rows, part] = weight
                    total = total + jnp.sum(weight.reshape(8, 8, 128), axis=0)
                total = 1.0 / jnp.sum(total, axis=0, keepdims=True)
                for k in range(near // 64):
                    rows = slice(k * 64, (k + 1) * 64)
                    r.probs[s, head, rows, part] = (r.scores[rows, part] * total).astype(LOW)

            loop(nodes // 128, soft)
            values = r.extended[s, :, width + head * HD : width + (head + 1) * HD]
            r.mixed[rows, cols] = tn(values, r.probs[s, head]).T.astype(LOW)
            advance(late_steps, 2)
        advance(late_steps, len(late_steps))
        r.start[...] += nn(r.mixed[rows], early(2, 3))

        def norm(b):
            part = block(b, 64)
            unit, inverse = norm_parts(r.start[part])
            r.unit_two[s, part] = unit.astype(LOW)
            r.inv_two[s, part] = inverse
            scaled = unit * (1.0 + r.wave[s, 2:3]) + r.wave[s, 3:4]
            r.second[pl.ds(pl.multiple_of(s * nodes + b * 64, 64), 64)] = scaled.astype(LOW)

        loop(nodes // 64, norm)

        def feed(j):
            cols = block(j, 256)
            upward = nn(r.second[rows], r.w_up[:, :, :, :, :, cols].reshape(width, 256))
            gate = 1.0 / (1.0 + jnp.exp(-upward))
            r.gated[rows, cols] = (upward * gate).astype(LOW)
            r.slope[rows, cols] = (gate * (1.0 + upward * (1.0 - gate))).astype(LOW)

        loop(hidden // 256, feed)
        r.final[rows] = (r.start[...] + nn(r.gated[rows], r.w_down[...].reshape(hidden, width))).astype(LOW)
        out = nn(r.final[rows], early(5, 6)) * (1.0 / 3.0)
        return out.T[:chan].astype(LOW)

    def gradient(s):
        rows = slice(s * nodes, (s + 1) * nodes)
        r.taken[rows, :chan] = (nt(r.node_hot[...], r.low_state[...]) * (1.0 / 3.0)).astype(LOW)
        d_final = nt(r.taken[rows], early(5, 6))
        r.start[...] = d_final
        r.d_branch[rows] = d_final.astype(LOW)

        def feed(j):
            cols = block(j, 256)
            d_gated = nt(r.d_branch[rows], r.w_down[j // 2, j % 2].reshape(256, width))
            r.slope[rows, cols] = (d_gated * r.slope[rows, cols].astype(WIDE)).astype(LOW)

        loop(hidden // 256, feed)
        r.scores[:nodes, :width] = nt(r.slope[rows], all_up())
        if s == 0:
            announce(0)
        norm_gradient(s, r.unit_two, r.inv_two, 2)
        if s == 0:
            products_late()
        r.d_attn[rows] = r.start[...].astype(LOW)
        r.d_mixed[...] = nt(r.d_attn[rows], early(2, 3)).astype(LOW)
        first = 2 * nodes + 2 * halo * s
        far = slice(first, first + 2 * halo)
        for head in range(HEADS):
            cols = slice(head * HD, (head + 1) * HD)
            after = slice(width + head * HD, width + (head + 1) * HD)
            r.scores[...] = nt(r.extended[s, :, after], r.d_mixed[:, cols])

            def soft(b):
                part = block(b, 128)
                total = jnp.zeros((8, 128), WIDE)
                for k in range(near // 64):
                    rows = slice(k * 64, (k + 1) * 64)
                    slope = r.probs[s, head, rows, part].astype(WIDE) * r.scores[rows, part]
                    total = total + jnp.sum(slope.reshape(8, 8, 128), axis=0)
                total = jnp.sum(total, axis=0, keepdims=True)
                for k in range(near // 64):
                    rows = slice(k * 64, (k + 1) * 64)
                    slope = r.probs[s, head, rows, part].astype(WIDE) * (r.scores[rows, part] - total)
                    r.d_scores[rows, part] = (slope * SCALE).astype(LOW)

            loop(nodes // 128, soft)
            d_values = nn(r.probs[s, head], r.d_mixed[:, cols]).astype(LOW)
            d_keys = nn(r.d_scores[...], r.queries[s, :, cols]).astype(LOW)
            r.d_keyval[rows, after] = d_values[:nodes]
            r.d_keyval[far, after] = d_values[nodes:]
            r.d_keyval[rows, cols] = d_keys[:nodes]
            r.d_keyval[far, cols] = d_keys[nodes:]
            r.d_queries[rows, cols] = tn(r.extended[s, :, cols], r.d_scores[...]).T.astype(LOW)
            if s == 0:
                advance(fold_steps, 2)
        r.outgoing[2 + s] = nt(r.d_keyval[far], early(1, 2)).astype(LOW)
        copies = pass_on(2 + s, r.returned.at[s, halo:], r.returned.at[s, :halo])
        r.scores[:nodes, :width] = nt(r.d_queries[rows], early(0, 1)) + nt(r.d_keyval[rows], early(1, 2))
        return copies

    def norm_gradient(s, units, inverses, which):
        r.d_wave[s, which : which + 2] = jnp.zeros((2, width), WIDE)

        def norm(b):
            part = block(b, 64)
            unit = units[s, part].astype(WIDE)
            d_out = r.scores[part, :width]
            d_scale = jnp.sum(d_out * unit, axis=0, keepdims=True)
            d_shift = jnp.sum(d_out, axis=0, keepdims=True)
            r.d_wave[s, which : which + 1] += d_scale
            r.d_wave[s, which + 1 : which + 2] += d_shift
            d_unit = d_out * (1.0 + r.wave[s, which : which + 1])
            along = jnp.mean(d_unit * unit, axis=-1, keepdims=True)
            d_hidden = d_unit - jnp.mean(d_unit, axis=-1, keepdims=True) - unit * along
            r.start[part] += inverses[s, part] * d_hidden

        loop(nodes // 64, norm)

    def absorb(s, copies):
        rows = slice(s * nodes, (s + 1) * nodes)
        for copy in copies:
            copy.wait()
        r.scores[:nodes, :width] += nn(r.send_hot[...], r.returned[s])
        norm_gradient(s, r.unit_one, r.inv_one, 0)
        r.d_summed[rows] = (r.start[...] * r.inv_count[...]).astype(LOW)

    if not gathered:
        late = Fold((r.g_up, r.g_down), (r.w_up, r.w_down), outs[1:3], r.fold, 1, where)
        soon_fold = Fold((r.g_early,), (r.w_early,), outs[:1], r.fold, 0, where)
    fold_steps = []

    def announce(which):
        if not gathered:
            for other in folders:
                pl.semaphore_signal(r.ready.at[which], inc=1, device_id=other, device_id_type=MESH)

    def products_late():
        planes = range(4) if gathered else far_planes(z)
        for k, p in enumerate(planes):
            r.g_down[p] = tn(r.gated[:, block(p, hidden // 4)], r.d_branch[...]).astype(LOW).reshape(r.g_down.shape[1:])
            r.g_up[p] = tn(r.second[:, block(p, width // 4)], r.slope[...]).astype(LOW).reshape(r.g_up.shape[1:])
            if gathered:
                continue
            if k == 0:
                pl.semaphore_wait(r.ready.at[0], len(folders))
            late.start(k)
            if k > 0:
                late.chip(k - 1)
            if k > 1:
                late.turn(k - 2)
            if k > 2:
                late.leave(k - 3)
        if not gathered:
            do = functools.partial
            fold_steps.extend([
                do(late.chip, 3), do(late.turn, 2), do(late.leave, 1), do(late.turn, 3), do(late.leave, 2),
                do(late.leave, 3)])

    def put_early(i, first, value):
        value = value.astype(LOW)
        r.g_early[2 * i : 2 * i + 2, :, :, :, :, first : first + value.shape[1]] = value.reshape(
            (2, 2, 2, 2, width // 32, value.shape[1]))

    copies = encode(0)
    nodes_out = attend(0, copies)

    load_noise.wait()

    def decode_one(t):
        cols = block(t, tile)
        out = nn(nodes_out, r.node_hot[:, cols])
        r.state[:, cols] = c_skip[0] * r.state[:, cols] + c_out[0] * out + level[1] * r.extra[:, cols]

    loop(tiles, decode_one)
    load_target = load(target, r.extra, 3)
    copies = encode(1)
    nodes_out_two = attend(1, copies)
    r.lost[...] = jnp.zeros(r.lost.shape, WIDE)
    load_target.wait()

    def decode_two(t):
        cols = block(t, tile)
        out = nn(nodes_out_two, r.node_hot[:, cols])
        place = lax.broadcasted_iota(jnp.int32, (1, tile), 1) + t * tile
        error = c_skip[1] * r.state[:, cols] + c_out[1] * out - r.extra[:, cols]
        error = jnp.where(place < pixel_count[0], error, 0.0)
        r.lost[...] += jnp.sum(error * error)
        r.extra[:, cols] = 2.0 * error
        r.low_state[:, cols] = (c_out[1] * 2.0 * error).astype(LOW)

    loop(tiles, decode_two)
    copies = gradient(1)
    absorb(1, copies)
    d_nodes = nn(r.d_summed[nodes:], early(4, 5))
    d_nodes = d_nodes.T[:chan].astype(LOW)

    def into_one(t):
        cols = block(t, tile)
        d_noisy = c_skip[1] * r.extra[:, cols] + c_in[1] * nn(d_nodes, r.owner_hot[:, cols])
        r.low_state[:, cols] = (c_out[0] * d_noisy).astype(LOW)

    loop(tiles, into_one)
    copies = gradient(0)
    announce(1)
    for i in range(2):
        cols = slice(i * width // 2, (i + 1) * width // 2)
        put_early(i, 0, tn(r.normed[: 2 * nodes, cols], r.d_queries[...]))
        advance(fold_steps, 1)
        put_early(i, width, tn(r.normed[:, cols], r.d_keyval[...]))
        put_early(i, w_at[2], tn(r.mixed[:, cols], r.d_attn[...]))
        put_early(i, w_at[5], tn(r.final[:, cols], r.taken[...]))
        advance(fold_steps, 1)
    absorb(0, copies)
    advance(fold_steps, len(fold_steps))
    for i in range(2):
        put_early(i, w_at[3], tn(r.d_summed[:, i * width // 2 : (i + 1) * width // 2], r.sums[...]))
        total = jnp.zeros((16, 16, 128), WIDE)
        for s in range(2):
            pieces = []
            for k in range(8 * i, 8 * i + 8):
                piece = r.d_wave[s, k // 4 : k // 4 + 1, (k % 4) * 128 : (k % 4 + 1) * 128]
                turned = pltpu.roll(piece, 64, 1)
                pieces.append(jnp.where(lane < 64, piece, turned))
                pieces.append(jnp.where(lane < 64, turned, piece))
            total = total + jnp.concatenate(pieces, axis=0)[:, None, :] * waves[s][None]
        put_early(i, w_at[6], total.reshape(256, 128))
    if gathered:
        for i, src in enumerate((r.g_early, r.g_up, r.g_down)):
            load(src, outs[i], 4 + i).wait()
        outs[3][...] = r.lost[...]
        return

    pl.semaphore_wait(r.ready.at[1], len(folders))
    for k in range(4):
        soon_fold.start(k)
    for k in range(4):
        soon_fold.chip(k)
    late.end()
    squares = jnp.sum(outs[1][...] * outs[1][...]) + jnp.sum(outs[2][...] * outs[2][...])
    for k in range(4):
        soon_fold.turn(k)
    for k in range(4):
        soon_fold.leave(k)
    soon_fold.end()
    squares = squares + jnp.sum(outs[0][...] * outs[0][...])
    row = lax.broadcasted_iota(jnp.int32, (8, 128), 0)
    live = (chan * jnp.minimum(pixel_count[0], pixels)).astype(WIDE)
    mine = y * 4 + x * 2 + c
    r.board[mine] = jnp.where(row == 0, squares, jnp.where(row == 1, r.lost[...], live))
    more = []
    for m, device in enumerate(plane_peers):
        more.append(send(r.board.at[mine], r.board.at[mine], r.small, (m,), device))
    for copy in more:
        copy.wait_recv()
    r.board[8 + z] = sum(r.board[m] for m in range(1, 8)) + r.board[0]
    level_copies = [send(r.board.at[8 + z], r.board.at[8 + z], r.small, (7 + d,), along_z[d]) for d in (1, 2, 3)]
    for copy in level_copies:
        copy.wait_recv()
    outs[3][...] = r.board[8] + r.board[9] + r.board[10] + r.board[11]
    late.drain()
    soon_fold.drain()
    for copy in more + level_copies:
        copy.wait_send()


def run_net(gathered, levels, node_count, pixel_count, previous, noisy, target, noise, owners, decode_idx, near_idx, send_idx,
            width, hidden, weights):
    nodes, pixels = near_idx.shape[1], owners.shape[1]
    scratch = net_scratch(nodes, send_idx.shape[1] // 2, pixels, width, hidden, noisy.shape[0])
    vmem, smem = pl.BlockSpec(memory_space=pltpu.VMEM), pl.BlockSpec(memory_space=pltpu.SMEM)
    hbm = pl.BlockSpec(memory_space=pl.ANY)
    if gathered:
        results = [(GRID + (width // 32, 5 * width), LOW), (GRID + (width // 32, hidden), LOW), (GRID + (hidden // 32, width), LOW)]
    else:
        results = [((width // 32, 5 * width), WIDE), ((width // 32, hidden), WIDE), ((hidden // 32, width), WIDE)]
    return pl.pallas_call(
        functools.partial(net_kernel, tuple(scratch), gathered),
        out_shape=[jax.ShapeDtypeStruct(shape, kind) for shape, kind in results + [((8, 128), WIDE)]],
        in_specs=[smem] * 3 + [hbm] * 4 + [vmem] * 4 + [hbm if gathered else vmem] * len(weights),
        out_specs=[hbm if gathered else vmem] * 3 + [vmem],
        scratch_shapes=list(scratch.values()),
        compiler_params=pltpu.CompilerParams(
            collective_id=3, has_side_effects=True, vmem_limit_bytes=VMEM_LIMIT),
    )(levels, node_count, pixel_count, previous, noisy, target, noise, owners, decode_idx, near_idx, send_idx, *weights)


def adam_kernel(packed, totals, *refs):
    g_early, g_up, g_down = refs[:3]
    given, made, (loss, count, norm, turned) = refs[-46:-25], refs[-25:-4], refs[-4:]
    loss[...] = totals[1:2, 0:1]
    count[...] = totals[2:3, 0:1]
    norm[...] = jnp.sqrt(totals[0:1, 0:1])
    factor = THRESHOLD / jnp.maximum(jnp.sqrt(totals[0:1, 0:1]), THRESHOLD)
    width = refs[-46 + 6].shape[1]
    at = [0, 3 * width, 4 * width] + [4 * width + HALF_COLS * i for i in range(1, 4)]
    chan = given[0].shape[1] // 2

    def update(i, at_in, g):
        w, m, v = (given[3 * i + j][at_in] for j in range(3))
        clipped = g * factor
        moment = BETA_ONE * m + (1.0 - BETA_ONE) * clipped
        variance = BETA_TWO * v + (1.0 - BETA_TWO) * clipped * clipped
        stepped = (
            moment
            / (1.0 - BETA_ONE**STEP)
            / (jnp.sqrt(variance / (1.0 - BETA_TWO**STEP)) + EPSILON)
        )
        made[3 * i][at_in] = w - LEARN_RATE * (stepped + DECAY_RATE * w)
        made[3 * i + 1][at_in] = moment
        made[3 * i + 2][at_in] = variance

    whole = (slice(None), slice(None))
    both = jnp.concatenate([g_early[:, at[2] : at[2] + chan], g_early[:, at[3] : at[3] + chan]], axis=1)
    update(0, whole, both)
    update(1, whole, g_early[:, : at[1]])
    update(2, whole, g_early[:, at[1] : at[2]])
    update(3, whole, g_up[...])
    update(4, whole, g_down[...])
    for i in range(FOUR // 2 if packed else 0):
        turned[2 * i : 2 * i + 1] = g_early[i : i + 1, at[5] : at[5] + 64]
        turned[2 * i + 1 : 2 * i + 2] = g_early[i : i + 1, at[5] + 64 :]
    update(5, whole, turned[...] if packed else refs[3][...])
    update(6, whole, g_early[:, at[4] : at[4] + chan])


def run_adam(totals, grads, given):
    return pl.pallas_call(
        functools.partial(adam_kernel, len(grads) == 3),
        out_shape=[jax.ShapeDtypeStruct(shape, WIDE) for shape in [a.shape for a in given] + [(1, 1)] * 3],
        in_specs=[pl.BlockSpec(memory_space=pltpu.VMEM)] * (1 + len(grads) + len(given)),
        out_specs=[pl.BlockSpec(memory_space=pltpu.VMEM)] * (len(given) + 3),
        scratch_shapes=[pltpu.VMEM((FOUR, 64), WIDE)],
        compiler_params=pltpu.CompilerParams(vmem_limit_bytes=VMEM_LIMIT),
    )(totals, *grads, *given)


def fill(array, columns):
    return jnp.pad(array, ((0, 0), (0, columns - array.shape[1])))


def on_device(
    previous_state, target_state, noise_draws, noise_level, pixel_owner, mesh_to_grid, neighbours, halo_send,
    node_count, pixel_count, w_encode, w_project, w_output, w_up, w_down, w_noise, w_decode,
    m_encode, m_project, m_output, m_up, m_down, m_noise, m_decode,
    v_encode, v_project, v_output, v_up, v_down, v_noise, v_decode,
):
    width = w_project.shape[1] // 3
    hidden = w_up.shape[1]
    channels = previous_state.shape[1]
    rows = w_project.shape[0]
    small_slice = lax.axis_size("patch") == 8 and lax.axis_size("rep") == 4
    flipped = w_encode.T
    halves = (flipped[:, :channels], flipped[:, channels:])
    if small_slice:
        weights = (w_project, w_output) + halves + (w_decode, w_noise, w_up, w_down)
    else:
        pieces = [w_project, w_output] + [fill(half, HALF_COLS) for half in halves] + [fill(w_decode, HALF_COLS)]
        early = lax.all_gather(jnp.concatenate(pieces, axis=1).astype(LOW), BOTH, axis=0, tiled=True)
        noise = lax.all_gather(w_noise.astype(LOW), BOTH, axis=1, tiled=True).reshape(FOUR, -1, 64)
        early = jnp.concatenate([early, noise.transpose(1, 0, 2).reshape(width, HALF_COLS)], axis=1)
        all_up = lax.all_gather(w_up.astype(LOW), BOTH, axis=0, tiled=True)
        all_down = lax.all_gather(w_down.astype(LOW), BOTH, axis=0, tiled=True)
        weights = [w.reshape(GRID + (-1, w.shape[1])) for w in (early, all_up, all_down)]
    at = [0, 3 * width, 4 * width] + [4 * width + HALF_COLS * i for i in range(1, 4)]

    pixels = pixel_owner.shape[1]
    noisy = target_state[0] + noise_level[0, 0] * noise_draws[0, 0]
    s_early, s_up, s_down, totals = run_net(
        not small_slice, noise_level, node_count[0], pixel_count[0], previous_state[0], noisy, target_state[0], noise_draws[0, 1],
        pixel_owner, mesh_to_grid[0], neighbours[0].T, halo_send, width, hidden, weights,
    )
    masters = (w_encode, w_project, w_output, w_up, w_down, w_noise, w_decode)
    moments = (m_encode, m_project, m_output, m_up, m_down, m_noise, m_decode)
    seconds = (v_encode, v_project, v_output, v_up, v_down, v_noise, v_decode)
    grads = (s_early, s_up, s_down)
    if not small_slice:
        g_early = s_early.reshape(width, -1)
        g_noise = g_early[:, at[5] :].reshape(-1, FOUR, 64).transpose(1, 0, 2).reshape(FOUR, -1)
        parts = (g_early[:, : at[5]], s_up.reshape(width, -1), s_down.reshape(hidden, -1))
        s_early, s_up, s_down = (
            lax.psum_scatter(g.astype(WIDE), BOTH, scatter_dimension=0, tiled=True) for g in parts)
        s_noise = lax.psum_scatter(g_noise.astype(WIDE), BOTH, scatter_dimension=1, tiled=True)
        squares = sum(jnp.sum(shard * shard) for shard in (s_early, s_up, s_down, s_noise))
        count_local = (channels * jnp.minimum(pixel_count[0, 0], pixels)).astype(WIDE)
        sums = lax.psum((squares, totals[0, 0], count_local), BOTH)
        totals = jnp.broadcast_to(jnp.stack(sums + sums[:1] * 5)[:, None], (8, 128))
        grads = (s_early, s_up, s_down, s_noise)
    given = [a for group in zip(masters, moments, seconds) for a in group]
    given[:3] = [a.T for a in given[:3]]
    *made, loss, count, norm = run_adam(totals, grads, given)
    made[:3] = [a.T for a in made[:3]]
    return tuple(made[0::3]) + tuple(made[1::3]) + tuple(made[2::3]) + tuple(a.reshape(()) for a in (loss, count, norm))


def solution(mesh):
    in_specs = (
        P("rep", None, "patch"),
        P("rep", None, "patch"),
        P("rep", None, None, "patch"),
        P("rep", None),
        P("rep", "patch"),
        P("rep", None, "patch"),
        P("rep", "patch", None),
        P("rep", "patch"),
        P("rep", "patch"),
        P("rep", "patch"),
        P(None, ("patch", "rep")),
        P(("patch", "rep"), None),
        P(("patch", "rep"), None),
        P(("patch", "rep"), None),
        P(("patch", "rep"), None),
        P(None, ("patch", "rep")),
        P(("patch", "rep"), None),
        P(None, ("patch", "rep")),
        P(("patch", "rep"), None),
        P(("patch", "rep"), None),
        P(("patch", "rep"), None),
        P(("patch", "rep"), None),
        P(None, ("patch", "rep")),
        P(("patch", "rep"), None),
        P(None, ("patch", "rep")),
        P(("patch", "rep"), None),
        P(("patch", "rep"), None),
        P(("patch", "rep"), None),
        P(("patch", "rep"), None),
        P(None, ("patch", "rep")),
        P(("patch", "rep"), None),
    )
    out_specs = (
        P(None, ("patch", "rep")),
        P(("patch", "rep"), None),
        P(("patch", "rep"), None),
        P(("patch", "rep"), None),
        P(("patch", "rep"), None),
        P(None, ("patch", "rep")),
        P(("patch", "rep"), None),
        P(None, ("patch", "rep")),
        P(("patch", "rep"), None),
        P(("patch", "rep"), None),
        P(("patch", "rep"), None),
        P(("patch", "rep"), None),
        P(None, ("patch", "rep")),
        P(("patch", "rep"), None),
        P(None, ("patch", "rep")),
        P(("patch", "rep"), None),
        P(("patch", "rep"), None),
        P(("patch", "rep"), None),
        P(("patch", "rep"), None),
        P(None, ("patch", "rep")),
        P(("patch", "rep"), None),
        P(),
        P(),
        P(),
    )
    return jax.shard_map(
        on_device, mesh=mesh, in_specs=in_specs, out_specs=out_specs, check_vma=False
    )
```

```python
import functools
import types

import jax
import jax.numpy as jnp
from jax import lax
from jax.experimental import pallas as pl
from jax.experimental.pallas import tpu as pltpu
from jax.sharding import PartitionSpec as P

HEADS = 4
HD = 128
FOUR = 32
NEIGH = 16
STEP = 5


LEARN_RATE = 0.03
BETA_ONE = 0.9
BETA_TWO = 0.95
EPSILON = 1e-08
DECAY_RATE = 0.1
THRESHOLD = 1.0

BOTH = ("patch", "rep")
LOW = jnp.bfloat16
WIDE = jnp.float32
SCALE = HD ** (-0.5)
VMEM_LIMIT = 64 * 2**20


def nn(a, b):
    return lax.dot_general(a, b, (((1,), (0,)), ((), ())), preferred_element_type=WIDE)


def nt(a, b):
    return lax.dot_general(a, b, (((1,), (1,)), ((), ())), preferred_element_type=WIDE)


def tn(a, b):
    return lax.dot_general(a, b, (((0,), (0,)), ((), ())), preferred_element_type=WIDE)


def norm_parts(hidden):
    centre = hidden - jnp.mean(hidden, axis=-1, keepdims=True)
    spread = jnp.mean(centre * centre, axis=-1, keepdims=True)
    inverse = lax.rsqrt(spread + 1e-05)
    return centre * inverse, inverse


MESH = pl.DeviceIdType.MESH
GRID = (4, 2, 2, 2)


def places():
    patch, rep = lax.axis_index("patch"), lax.axis_index("rep")
    z, y, x, c = patch // 2, patch % 2, rep // 2, rep % 2
    sibling = {"patch": patch, "rep": x * 2 + (1 - c)}
    across_x = {"patch": patch, "rep": (1 - x) * 2 + c}
    across_y = {"patch": z * 2 + (1 - y), "rep": rep}
    along_z = [{"patch": ((z + d) % 4) * 2 + y, "rep": rep} for d in range(4)]
    return z, y, x, c, sibling, across_x, across_y, along_z


def send(src, dst, sems, index, device):
    copy = pltpu.make_async_remote_copy(
        src_ref=src, dst_ref=dst, send_sem=sems.at[(0,) + index], recv_sem=sems.at[(1,) + index],
        device_id=device, device_id_type=MESH,
    )
    copy.start()
    return copy


def plus(*terms):
    total = terms[0].astype(WIDE)
    for term in terms[1:]:
        total = total + term.astype(WIDE)
    return total


HALF_COLS = 128


def net_scratch(nodes, halo, pixels, width, hidden, kept):
    near = nodes + 2 * halo
    return dict(
        owner_hot=pltpu.VMEM((nodes, pixels), LOW),
        node_hot=pltpu.VMEM((nodes, pixels), LOW),
        bias=pltpu.VMEM((near, nodes), WIDE),
        send_hot=pltpu.VMEM((nodes, 2 * halo), LOW),
        inv_count=pltpu.VMEM((nodes, 1), WIDE),
        sums=pltpu.VMEM((2 * nodes, 2 * HALF_COLS), LOW),
        wave=pltpu.VMEM((2, 4, width), WIDE),
        d_wave=pltpu.VMEM((2, 4, width), WIDE),
        start=pltpu.VMEM((nodes, width), WIDE),
        unit_one=pltpu.VMEM((2, nodes, width), LOW),
        inv_one=pltpu.VMEM((2, nodes, 1), WIDE),
        normed=pltpu.VMEM((2 * near, width), LOW),
        queries=pltpu.VMEM((2, nodes, width), LOW),
        extended=pltpu.VMEM((2, near, 2 * width), LOW),
        probs=pltpu.VMEM((2, HEADS, near, nodes), LOW),
        mixed=pltpu.VMEM((2 * nodes, width), LOW),
        unit_two=pltpu.VMEM((2, nodes, width), LOW),
        inv_two=pltpu.VMEM((2, nodes, 1), WIDE),
        second=pltpu.VMEM((2 * nodes, width), LOW),
        gated=pltpu.VMEM((2 * nodes, hidden), LOW),
        slope=pltpu.VMEM((2 * nodes, hidden), LOW),
        final=pltpu.VMEM((2 * nodes, width), LOW),
        taken=pltpu.VMEM((2 * nodes, HALF_COLS), LOW),
        d_branch=pltpu.VMEM((2 * nodes, width), LOW),
        d_attn=pltpu.VMEM((2 * nodes, width), LOW),
        d_queries=pltpu.VMEM((2 * nodes, width), LOW),
        d_keyval=pltpu.VMEM((2 * near, 2 * width), LOW),
        d_summed=pltpu.VMEM((2 * nodes, width), LOW),
        d_mixed=pltpu.VMEM((nodes, width), LOW),
        d_scores=pltpu.VMEM((near, nodes), LOW),
        scores=pltpu.VMEM((near, nodes), WIDE),
        outgoing=pltpu.VMEM((4, 2 * halo, width), LOW),
        returned=pltpu.VMEM((2, 2 * halo, width), LOW),
        state=pltpu.VMEM((kept, pixels), WIDE),
        extra=pltpu.VMEM((kept, pixels), WIDE),
        low_state=pltpu.VMEM((kept, pixels), LOW),
        g_early=pltpu.VMEM(GRID + (width // 32, 5 * width), LOW),
        g_up=pltpu.VMEM(GRID + (width // 32, hidden), LOW),
        g_down=pltpu.VMEM(GRID + (hidden // 32, width), LOW),
        lost=pltpu.VMEM((8, 128), WIDE),
        noise_rows=pltpu.VMEM((FOUR // 2, 128), WIDE),
        waves=pltpu.VMEM((2, FOUR // 2, 128), WIDE),
        board=pltpu.VMEM((12, 8, 128), WIDE),
        w_early=pltpu.VMEM(GRID + (width // 32, 5 * width), LOW),
        w_up=pltpu.VMEM(GRID + (width // 32, hidden), LOW),
        w_down=pltpu.VMEM(GRID + (hidden // 32, width), LOW),
        loads=pltpu.SemaphoreType.DMA((7,)),
        ready=pltpu.SemaphoreType.REGULAR((2,)),
        fold=pltpu.SemaphoreType.DMA((2, 6, 4, 4)),
        small=pltpu.SemaphoreType.DMA((2, 12)),
        links=pltpu.SemaphoreType.DMA((2, 4, 2)),
        spread=pltpu.SemaphoreType.DMA((2, 6, 4, 3)),
    )


def loop(count, body):
    def step(i, carry):
        body(i)
        return carry

    lax.fori_loop(0, count, step, 0)


def block(index, size):
    return pl.ds(pl.multiple_of(index * size, size), size)


def spread_steps(arrays, sems, first, where):
    z, y, x, c, sibling, across_x, across_y, along_z = where
    planes, x_one, y_one, x_two, y_two, core = {}, {}, {}, {}, {}, {}

    def plane_of(d):
        return (z - d + 4) % 4

    def cross(d):
        for i, out in enumerate(arrays):
            h = out.shape[-1] // 2
            here_l, here_r = out.at[plane_of(d), y, x, c, :, :h], out.at[plane_of(d), y, x, c, :, h:]
            x_one[d, i] = send(here_l, here_l, sems, (1, d, first + i), across_x)
            y_one[d, i] = send(here_r, here_r, sems, (2, d, first + i), across_y)

    def begin():
        for i, out in enumerate(arrays):
            mine = out.at[z, y, x, c]
            for d in (1, 3, 2):
                planes[d, i] = send(mine, mine, sems, (0, d, first + i), along_z[d])
        cross(0)

    def arrive(d):
        for i in range(len(arrays)):
            planes[d, i].wait_recv()
        cross(d)

    def turn(d):
        for i, out in enumerate(arrays):
            h = out.shape[-1] // 2
            x_one[d, i].wait_recv()
            both = out.at[plane_of(d), y, :, c, :, :h]
            y_two[d, i] = send(both, both, sems, (3, d, first + i), across_y)
            y_one[d, i].wait_recv()
            both = out.at[plane_of(d), :, x, c, :, h:]
            x_two[d, i] = send(both, both, sems, (4, d, first + i), across_x)

    def share(d):
        for i, out in enumerate(arrays):
            y_two[d, i].wait_recv()
            x_two[d, i].wait_recv()
            plane = out.at[plane_of(d), :, :, c]
            core[d, i] = send(plane, plane, sems, (5, d, first + i), sibling)

    def end():
        for group in (planes, x_one, y_one, x_two, y_two):
            for copy in group.values():
                copy.wait_send()
        for copy in core.values():
            copy.wait()

    do = functools.partial
    return [begin, do(arrive, 1), do(arrive, 3), do(turn, 0), do(arrive, 2), do(turn, 1), do(turn, 3), do(share, 0),
            do(turn, 2), do(share, 1), do(share, 3), do(share, 2), end]


def far_planes(z):
    return [3 * (1 - z // 2), 2 - z // 2, z + 1 - 2 * (z % 2), z]


class Fold:
    def __init__(self, sources, rooms, outs, spans, sems, first, where):
        self.sources, self.rooms, self.outs, self.sems, self.first = sources, rooms, outs, sems, first
        self.z, self.y, self.x, self.c, self.sibling, self.across_x, self.across_y, _ = where
        self.far = far_planes(self.z)
        self.spans = [(i, slice(a, b), slice(a, (a + b) // 2), slice((a + b) // 2, b)) for i, (a, b) in enumerate(spans)]
        self.near, self.one, self.two, self.last = {}, {}, {}, []

    def start(self, k):
        p = self.far[k]
        for g, room, (i, cols, lower, upper) in zip(self.sources, self.rooms, self.spans):
            self.near[k, i] = send(
                g.at[p, :, :, 1 - self.c, :, cols], room.at[p, :, :, 0, :, cols], self.sems, (0, k, self.first + i), self.sibling)

    def chip(self, k):
        p = self.far[k]
        for g, room, (i, cols, lower, upper) in zip(self.sources, self.rooms, self.spans):
            self.near[k, i].wait_recv()
            room[p, :, :, 0, :, cols] = plus(g[p, :, :, self.c, :, cols], room[p, :, :, 0, :, cols]).astype(LOW)
            self.one[k, i, 0] = send(room.at[p, :, 1 - self.x, 0, :, lower], room.at[p, 0, :, 1, :, lower], self.sems,
                                     (1, k, self.first + i), self.across_x)
            self.one[k, i, 1] = send(room.at[p, 1 - self.y, :, 0, :, upper], room.at[p, 0, :, 1, :, upper], self.sems,
                                     (2, k, self.first + i), self.across_y)

    def turn(self, k):
        p = self.far[k]
        for room, (i, cols, lower, upper) in zip(self.rooms, self.spans):
            self.one[k, i, 0].wait_recv()
            room[p, 0, :, 1, :, lower] = plus(room[p, :, self.x, 0, :, lower], room[p, 0, :, 1, :, lower]).astype(LOW)
            self.two[k, i, 0] = send(room.at[p, 0, 1 - self.y, 1, :, lower], room.at[p, 1, 0, 1, :, lower], self.sems,
                                     (3, k, self.first + i), self.across_y)
            self.one[k, i, 1].wait_recv()
            room[p, 0, :, 1, :, upper] = plus(room[p, self.y, :, 0, :, upper], room[p, 0, :, 1, :, upper]).astype(LOW)
            self.two[k, i, 1] = send(room.at[p, 0, 1 - self.x, 1, :, upper], room.at[p, 1, 0, 1, :, upper], self.sems,
                                     (4, k, self.first + i), self.across_x)

    def leave(self, k):
        p = self.far[k]
        for room, out, (i, cols, lower, upper) in zip(self.rooms, self.outs, self.spans):
            self.two[k, i, 0].wait_recv()
            self.two[k, i, 1].wait_recv()
            left = plus(room[p, 0, self.y, 1, :, lower], room[p, 1, 0, 1, :, lower])
            right = plus(room[p, 0, self.x, 1, :, upper], room[p, 1, 0, 1, :, upper])
            if k == 3:
                out[:, lower] = left
                out[:, upper] = right
                continue
            room[p, 1, 0, 1, :, lower] = left.astype(LOW)
            room[p, 1, 0, 1, :, upper] = right.astype(LOW)
            copy = pltpu.make_async_remote_copy(
                src_ref=room.at[p, 1, 0, 1, :, cols], dst_ref=room.at[self.z, 1, 1, 1, :, cols],
                send_sem=self.sems.at[0, 5, k, self.first + i], recv_sem=self.sems.at[1, 5, self.z, self.first + i],
                device_id={"patch": p * 2 + self.y, "rep": self.x * 2 + self.c}, device_id_type=MESH,
            )
            copy.start()
            self.last.append(copy)

    def end(self):
        for room, out, (i, cols, lower, upper) in zip(self.rooms, self.outs, self.spans):
            for k in range(3):
                p = self.far[k]
                come = room.at[p, 1, 1, 1, :, cols]
                pltpu.make_async_remote_copy(
                    src_ref=come, dst_ref=come, send_sem=self.sems.at[0, 5, k, self.first + i],
                    recv_sem=self.sems.at[1, 5, p, self.first + i], device_id=self.sibling, device_id_type=MESH,
                ).wait_recv()
                out[:, cols] = plus(out[:, cols], room[p, 1, 1, 1, :, cols])

    def drain(self):
        for copy in list(self.near.values()) + list(self.one.values()) + list(self.two.values()) + self.last:
            copy.wait_send()


def net_kernel(names, gathered, levels, node_count, pixel_count, previous, noisy, target, noise, owners, decode_idx,
               near_idx, send_idx, *rest):
    outs = rest[-4 - len(names) : -len(names)]
    weights, scratch = rest[: -4 - len(names)], rest[-len(names) :]
    r = types.SimpleNamespace(**dict(zip(names, scratch)))
    nodes, pixels = near_idx.shape[1], owners.shape[1]
    waves = r.waves
    halo, chan = send_idx.shape[1] // 2, previous.shape[0]
    near = nodes + 2 * halo
    width, hidden = r.start.shape[1], r.gated.shape[1]
    at = [0, 3 * width, 4 * width, 4 * width + hidden, 4 * width + hidden + 256, 4 * width + hidden + 384]
    tile = 1536
    tiles = pixels // tile
    patches = lax.axis_size("patch")
    me = lax.axis_index("patch")
    lower, upper = {"patch": (me + patches - 1) % patches}, {"patch": (me + 1) % patches}
    barrier = pltpu.get_barrier_semaphore()
    others = [lower, upper]
    if not gathered:
        where = places()
        z, y, x, c, sibling, across_x, across_y, along_z = where
        folders = [sibling, across_x, across_y] + along_z[1:]
        plane_peers = [
            {"patch": z * 2 + (y + m // 4) % 2, "rep": ((x + m // 2 % 2) % 2) * 2 + (c + m % 2) % 2} for m in range(1, 8)]
        others += plane_peers + along_z[1:]
    for other in others:
        pl.semaphore_signal(barrier, inc=1, device_id=other, device_id_type=MESH)

    def load(src, dst, slot):
        copy = pltpu.make_async_copy(src, dst, r.loads.at[slot])
        copy.start()
        return copy

    loads = [load(previous, r.extra, 0), load(noisy, r.state, 1)]
    w_at = [0, width, 3 * width, 4 * width, 4 * width + HALF_COLS, 4 * width + 2 * HALF_COLS, 4 * width + 3 * HALF_COLS]
    w_targets = (r.w_early, r.w_up, r.w_down)
    early_steps, late_steps = [], []
    if gathered:
        pl.semaphore_wait(barrier, len(others))
        for i, (src, dst) in enumerate(zip(weights, w_targets)):
            load(src, dst, 4 + i).wait()
    else:
        project, output, encode_prev, encode_noisy, decode, noise_rows, up, down = weights
        for i in range(FOUR // 2):
            r.noise_rows[i : i + 1, :64] = noise_rows[2 * i : 2 * i + 1]
            r.noise_rows[i : i + 1, 64:] = noise_rows[2 * i + 1 : 2 * i + 2]
        noise_rows = r.noise_rows
        r.w_early[z, y, x, c, :, 4 * width :] = jnp.zeros((width // 32, width), LOW)
        for i, piece in ((0, project), (2, output), (3, encode_prev), (4, encode_noisy), (5, decode), (6, noise_rows)):
            r.w_early[z, y, x, c, :, w_at[i] : w_at[i] + piece.shape[1]] = piece[...].astype(LOW)
        r.w_up[z, y, x, c] = up[...].astype(LOW)
        r.w_down[z, y, x, c] = down[...].astype(LOW)
        early_steps = spread_steps(w_targets[:1], r.spread, 0, where)
        late_steps = spread_steps(w_targets[1:], r.spread, 1, where)
        pl.semaphore_wait(barrier, len(others))

    def encode_state(s):
        r.low_state[...] = (r.state[...] * c_in[s]).astype(LOW)
        r.sums[s * nodes : (s + 1) * nodes, HALF_COLS : HALF_COLS + chan] = nt(
            r.owner_hot[...], r.low_state[...]).astype(LOW)

    def advance(steps, count):
        for _ in range(min(count, len(steps))):
            steps.pop(0)()

    def early(first, last):
        return r.w_early[:, :, :, :, :, w_at[first] : (w_at + [5 * width])[last]].reshape(width, -1)

    def all_up():
        return r.w_up[...].reshape(width, hidden)

    advance(early_steps, 1)

    level = [levels[0, s] for s in range(2)]
    c_in, c_skip, c_out = [], [], []
    for s in range(2):
        whole = jnp.full((8, 128), level[s], WIDE)
        scaled = lax.rsqrt(whole * whole + 1.0)
        c_in.append(scaled[:1, :1])
        c_skip.append((1.0 / (whole * whole + 1.0))[:1, :1])
        c_out.append((whole * scaled)[:1, :1])
        shape = (FOUR // 2, 128)
        feature = 2 * lax.broadcasted_iota(jnp.int32, shape, 0) + lax.broadcasted_iota(jnp.int32, shape, 1) // 64
        frequency = 0.25 * ((feature % (FOUR // 2)).astype(WIDE) + 1.0)
        angle = jnp.log(jnp.full(shape, level[s], WIDE)) * frequency
        waves[s] = jnp.where(feature < FOUR // 2, jnp.sin(angle), jnp.cos(angle))

    def build_hot(t):
        cols = block(t, tile)
        place = lax.broadcasted_iota(jnp.int32, (1, tile), 1) + t * tile
        own = jnp.where(place < pixel_count[0], owners[:, cols], -1)
        three = [decode_idx[i : i + 1, cols] for i in range(3)]

        def rows(b):
            row = lax.broadcasted_iota(jnp.int32, (16, tile), 0) + b * 16
            r.owner_hot[block(b, 16), cols] = (row == own).astype(WIDE).astype(LOW)
            total = sum((row == idx).astype(WIDE) for idx in three)
            r.node_hot[block(b, 16), cols] = total.astype(LOW)

        loop(nodes // 16, rows)


    def build_bias(b):
        rows = block(b, 32)
        place = lax.broadcasted_iota(jnp.int32, (32, nodes), 0) + b * 32
        listed = jnp.zeros((32, nodes), WIDE)
        for j in range(1, NEIGH):
            listed = listed + (near_idx[j : j + 1] == place).astype(WIDE)
        listed = jnp.where((place >= nodes) | (place < node_count[0]), listed, 0.0)
        listed = listed + (near_idx[0:1] == place).astype(WIDE)
        r.bias[rows] = jnp.where(listed > 0.0, jnp.log(jnp.maximum(listed, 1.0)), -1e30)

    loop(near // 32, build_bias)
    advance(early_steps, 4)
    advance(late_steps, 1)
    for t in range(tiles):
        build_hot(t)
        advance(early_steps, 2)
    r.send_hot[...] = (
        lax.broadcasted_iota(jnp.int32, (nodes, 2 * halo), 0) == send_idx[...]
    ).astype(WIDE).astype(LOW)

    loads[0].wait()
    total = nt(r.owner_hot[...], jnp.ones((8, pixels), LOW))[:, :1]
    r.inv_count[...] = 1.0 / jnp.maximum(total, 1.0)
    r.sums[...] = jnp.zeros(r.sums.shape, LOW)
    r.taken[...] = jnp.zeros(r.taken.shape, LOW)
    r.low_state[...] = r.extra[...].astype(LOW)
    load_noise = load(noise, r.extra, 2)
    summed = nt(r.owner_hot[...], r.low_state[...]).astype(LOW)
    r.sums[:nodes, :chan] = summed
    r.sums[nodes:, :chan] = summed
    loads[1].wait()
    encode_state(0)
    advance(early_steps, len(early_steps))
    advance(late_steps, 3)

    noise_block = early(6, 7).astype(WIDE).reshape(32, 16, 128)
    lane = lax.broadcasted_iota(jnp.int32, (1, 128), 1)
    for s in range(2):
        parts = jnp.sum(noise_block * waves[s][None], axis=1)
        both = parts + pltpu.roll(parts, 64, 1)
        for k in range(16):
            piece = jnp.where(lane < 64, both[2 * k : 2 * k + 1], both[2 * k + 1 : 2 * k + 2])
            r.wave[s, k // 4 : k // 4 + 1, (k % 4) * 128 : (k % 4 + 1) * 128] = piece


    def pass_on(number, first, second):
        copies = []
        for i, (dst, device) in enumerate(((first, lower), (second, upper))):
            copy = pltpu.make_async_remote_copy(
                src_ref=r.outgoing.at[number, i * halo : (i + 1) * halo], dst_ref=dst,
                send_sem=r.links.at[0, number, i], recv_sem=r.links.at[1, number, i],
                device_id=device, device_id_type=MESH,
            )
            copy.start()
            copies.append(copy)
        return copies

    def encode(s):
        rows = slice(s * nodes, (s + 1) * nodes)
        if s:
            encode_state(s)
        r.start[...] = nt(r.sums[rows], early(3, 5)) * r.inv_count[...]

        def norm(b):
            part = block(b, 256)
            unit, inverse = norm_parts(r.start[part])
            r.unit_one[s, part] = unit.astype(LOW)
            r.inv_one[s, part] = inverse
            scaled = unit * (1.0 + r.wave[s, 0:1]) + r.wave[s, 1:2]
            r.normed[pl.ds(pl.multiple_of(s * nodes + b * 256, 256), 256)] = scaled.astype(LOW)

        loop(nodes // 256, norm)
        normed = r.normed[rows]
        r.outgoing[s] = tn(r.send_hot[...], normed).astype(LOW)
        first = 2 * nodes + 2 * halo * s
        copies = pass_on(s, r.normed.at[first + halo : first + 2 * halo], r.normed.at[first : first + halo])
        r.queries[s] = nn(normed, early(0, 1)).astype(LOW)
        advance(late_steps, 1)
        r.extended[s, :nodes] = nn(normed, early(1, 2)).astype(LOW)
        advance(late_steps, 1)
        return copies

    def attend(s, copies):
        rows = slice(s * nodes, (s + 1) * nodes)
        for copy in copies:
            copy.wait()
        first = 2 * nodes + 2 * halo * s
        r.extended[s, nodes:] = nn(r.normed[first : first + 2 * halo], early(1, 2)).astype(LOW)
        for head in range(HEADS):
            cols = slice(head * HD, (head + 1) * HD)
            r.scores[...] = nt(r.extended[s, :, cols], r.queries[s, :, cols])

            def soft(b):
                part = block(b, 128)
                top = jnp.full((8, 128), -1e30, WIDE)
                for k in range(near // 64):
                    rows = slice(k * 64, (k + 1) * 64)
                    score = r.scores[rows, part] * SCALE + r.bias[rows, part]
                    r.scores[rows, part] = score
                    top = jnp.maximum(top, jnp.max(score.reshape(8, 8, 128), axis=0))
                top = jnp.max(top, axis=0, keepdims=True)
                total = jnp.zeros((8, 128), WIDE)
                for k in range(near // 64):
                    rows = slice(k * 64, (k + 1) * 64)
                    weight = jnp.exp(r.scores[rows, part] - top)
                    r.scores[rows, part] = weight
                    total = total + jnp.sum(weight.reshape(8, 8, 128), axis=0)
                total = 1.0 / jnp.sum(total, axis=0, keepdims=True)
                for k in range(near // 64):
                    rows = slice(k * 64, (k + 1) * 64)
                    r.probs[s, head, rows, part] = (r.scores[rows, part] * total).astype(LOW)

            loop(nodes // 128, soft)
            values = r.extended[s, :, width + head * HD : width + (head + 1) * HD]
            r.mixed[rows, cols] = tn(values, r.probs[s, head]).T.astype(LOW)
            advance(late_steps, 2)
        advance(late_steps, len(late_steps))
        r.start[...] += nn(r.mixed[rows], early(2, 3))

        def norm(b):
            part = block(b, 256)
            unit, inverse = norm_parts(r.start[part])
            r.unit_two[s, part] = unit.astype(LOW)
            r.inv_two[s, part] = inverse
            scaled = unit * (1.0 + r.wave[s, 2:3]) + r.wave[s, 3:4]
            r.second[pl.ds(pl.multiple_of(s * nodes + b * 256, 256), 256)] = scaled.astype(LOW)

        loop(nodes // 256, norm)

        def feed(j):
            cols = block(j, 256)
            upward = nn(r.second[rows], r.w_up[:, :, :, :, :, cols].reshape(width, 256))
            gate = 1.0 / (1.0 + jnp.exp(-upward))
            r.gated[rows, cols] = (upward * gate).astype(LOW)
            r.slope[rows, cols] = (gate * (1.0 + upward * (1.0 - gate))).astype(LOW)

        loop(hidden // 256, feed)
        r.final[rows] = (r.start[...] + nn(r.gated[rows], r.w_down[...].reshape(hidden, width))).astype(LOW)
        out = nn(r.final[rows], early(5, 6)) * (1.0 / 3.0)
        return out.T[:chan].astype(LOW)

    def gradient(s):
        rows = slice(s * nodes, (s + 1) * nodes)
        r.taken[rows, :chan] = (nt(r.node_hot[...], r.low_state[...]) * (1.0 / 3.0)).astype(LOW)
        d_final = nt(r.taken[rows], early(5, 6))
        r.start[...] = d_final
        r.d_branch[rows] = d_final.astype(LOW)

        def feed(j):
            cols = block(j, 256)
            d_gated = nt(r.d_branch[rows], r.w_down[j // 2, j % 2].reshape(256, width))
            r.slope[rows, cols] = (d_gated * r.slope[rows, cols].astype(WIDE)).astype(LOW)

        loop(hidden // 256, feed)
        r.scores[:nodes, :width] = nt(r.slope[rows], all_up())
        if s == 0:
            announce(0)
        norm_gradient(s, r.unit_two, r.inv_two, 2)
        if s == 0:
            products_late()
        r.d_attn[rows] = r.start[...].astype(LOW)
        r.d_mixed[...] = nt(r.d_attn[rows], early(2, 3)).astype(LOW)
        first = 2 * nodes + 2 * halo * s
        far = slice(first, first + 2 * halo)
        for head in range(HEADS):
            cols = slice(head * HD, (head + 1) * HD)
            after = slice(width + head * HD, width + (head + 1) * HD)
            r.scores[...] = nt(r.extended[s, :, after], r.d_mixed[:, cols])

            def soft(b):
                part = block(b, 128)
                total = jnp.zeros((8, 128), WIDE)
                for k in range(near // 64):
                    rows = slice(k * 64, (k + 1) * 64)
                    slope = r.probs[s, head, rows, part].astype(WIDE) * r.scores[rows, part]
                    total = total + jnp.sum(slope.reshape(8, 8, 128), axis=0)
                total = jnp.sum(total, axis=0, keepdims=True)
                for k in range(near // 64):
                    rows = slice(k * 64, (k + 1) * 64)
                    slope = r.probs[s, head, rows, part].astype(WIDE) * (r.scores[rows, part] - total)
                    r.d_scores[rows, part] = (slope * SCALE).astype(LOW)

            loop(nodes // 128, soft)
            d_values = nn(r.probs[s, head], r.d_mixed[:, cols]).astype(LOW)
            d_keys = nn(r.d_scores[...], r.queries[s, :, cols]).astype(LOW)
            r.d_keyval[rows, after] = d_values[:nodes]
            r.d_keyval[far, after] = d_values[nodes:]
            r.d_keyval[rows, cols] = d_keys[:nodes]
            r.d_keyval[far, cols] = d_keys[nodes:]
            r.d_queries[rows, cols] = tn(r.extended[s, :, cols], r.d_scores[...]).T.astype(LOW)
            if s == 0:
                advance(fold_steps, 2)
        r.outgoing[2 + s] = nt(r.d_keyval[far], early(1, 2)).astype(LOW)
        copies = pass_on(2 + s, r.returned.at[s, halo:], r.returned.at[s, :halo])
        r.scores[:nodes, :width] = nt(r.d_queries[rows], early(0, 1)) + nt(r.d_keyval[rows], early(1, 2))
        return copies

    def norm_gradient(s, units, inverses, which):
        r.d_wave[s, which : which + 2] = jnp.zeros((2, width), WIDE)

        def norm(b):
            part = block(b, 256)
            unit = units[s, part].astype(WIDE)
            d_out = r.scores[part, :width]
            d_scale = jnp.sum(d_out * unit, axis=0, keepdims=True)
            d_shift = jnp.sum(d_out, axis=0, keepdims=True)
            r.d_wave[s, which : which + 1] += d_scale
            r.d_wave[s, which + 1 : which + 2] += d_shift
            d_unit = d_out * (1.0 + r.wave[s, which : which + 1])
            along = jnp.mean(d_unit * unit, axis=-1, keepdims=True)
            d_hidden = d_unit - jnp.mean(d_unit, axis=-1, keepdims=True) - unit * along
            r.start[part] += inverses[s, part] * d_hidden

        loop(nodes // 256, norm)

    def absorb(s, copies):
        rows = slice(s * nodes, (s + 1) * nodes)
        for copy in copies:
            copy.wait()
        r.scores[:nodes, :width] += nn(r.send_hot[...], r.returned[s])
        norm_gradient(s, r.unit_one, r.inv_one, 0)
        r.d_summed[rows] = (r.start[...] * r.inv_count[...]).astype(LOW)

    if not gathered:
        late = Fold((r.g_up, r.g_down), (r.w_up, r.w_down), outs[1:3], ((0, hidden), (0, width)), r.fold, 1, where)
        cut = 4 * width
        soon_fold = Fold((r.g_early,), (r.w_early,), outs[:1], ((0, cut),), r.fold, 0, where)
        tail_fold = Fold((r.g_early,), (r.w_early,), outs[:1], ((cut, cut + width),), r.fold, 3, where)
    fold_steps = []

    def announce(which):
        if not gathered:
            for other in folders:
                pl.semaphore_signal(r.ready.at[which], inc=1, device_id=other, device_id_type=MESH)

    def products_late():
        planes = range(4) if gathered else far_planes(z)
        for k, p in enumerate(planes):
            r.g_down[p] = tn(r.gated[:, block(p, hidden // 4)], r.d_branch[...]).astype(LOW).reshape(r.g_down.shape[1:])
            r.g_up[p] = tn(r.second[:, block(p, width // 4)], r.slope[...]).astype(LOW).reshape(r.g_up.shape[1:])
            if gathered:
                continue
            if k == 0:
                pl.semaphore_wait(r.ready.at[0], len(folders))
            late.start(k)
            if k > 0:
                late.chip(k - 1)
            if k > 1:
                late.turn(k - 2)
            if k > 2:
                late.leave(k - 3)
        if not gathered:
            do = functools.partial
            fold_steps.extend([
                do(late.chip, 3), do(late.turn, 2), do(late.leave, 1), do(late.turn, 3), do(late.leave, 2),
                do(late.leave, 3)])

    def put_early(i, first, value):
        value = value.astype(LOW)
        r.g_early[2 * i : 2 * i + 2, :, :, :, :, first : first + value.shape[1]] = value.reshape(
            (2, 2, 2, 2, width // 32, value.shape[1]))

    copies = encode(0)
    nodes_out = attend(0, copies)

    load_noise.wait()

    def decode_one(t):
        cols = block(t, tile)
        out = nn(nodes_out, r.node_hot[:, cols])
        r.state[:, cols] = c_skip[0] * r.state[:, cols] + c_out[0] * out + level[1] * r.extra[:, cols]

    loop(tiles, decode_one)
    load_target = load(target, r.extra, 3)
    copies = encode(1)
    nodes_out_two = attend(1, copies)
    r.lost[...] = jnp.zeros(r.lost.shape, WIDE)
    load_target.wait()

    def decode_two(t):
        cols = block(t, tile)
        out = nn(nodes_out_two, r.node_hot[:, cols])
        place = lax.broadcasted_iota(jnp.int32, (1, tile), 1) + t * tile
        error = c_skip[1] * r.state[:, cols] + c_out[1] * out - r.extra[:, cols]
        error = jnp.where(place < pixel_count[0], error, 0.0)
        r.lost[...] += jnp.sum(error * error)
        r.extra[:, cols] = 2.0 * error
        r.low_state[:, cols] = (c_out[1] * 2.0 * error).astype(LOW)

    loop(tiles, decode_two)
    copies = gradient(1)
    absorb(1, copies)
    d_nodes = nn(r.d_summed[nodes:], early(4, 5))
    d_nodes = d_nodes.T[:chan].astype(LOW)

    def into_one(t):
        cols = block(t, tile)
        d_noisy = c_skip[1] * r.extra[:, cols] + c_in[1] * nn(d_nodes, r.owner_hot[:, cols])
        r.low_state[:, cols] = (c_out[0] * d_noisy).astype(LOW)

    loop(tiles, into_one)
    copies = gradient(0)
    announce(1)
    for i in range(2):
        cols = slice(i * width // 2, (i + 1) * width // 2)
        put_early(i, 0, tn(r.normed[: 2 * nodes, cols], r.d_queries[...]))
        advance(fold_steps, 1)
        put_early(i, width, tn(r.normed[:, cols], r.d_keyval[...]))
        put_early(i, w_at[2], tn(r.mixed[:, cols], r.d_attn[...]))
        put_early(i, w_at[5], tn(r.final[:, cols], r.taken[...]))
        advance(fold_steps, 1)
    advance(fold_steps, len(fold_steps))
    if not gathered:
        pl.semaphore_wait(r.ready.at[1], len(folders))
        for k in range(4):
            soon_fold.start(k)
        for k in range(4):
            soon_fold.chip(k)
    absorb(0, copies)
    if not gathered:
        soon_fold.turn(0)
    for i in range(2):
        put_early(i, w_at[3], tn(r.d_summed[:, i * width // 2 : (i + 1) * width // 2], r.sums[...]))
        total = jnp.zeros((16, 16, 128), WIDE)
        for s in range(2):
            pieces = []
            for k in range(8 * i, 8 * i + 8):
                piece = r.d_wave[s, k // 4 : k // 4 + 1, (k % 4) * 128 : (k % 4 + 1) * 128]
                turned = pltpu.roll(piece, 64, 1)
                pieces.append(jnp.where(lane < 64, piece, turned))
                pieces.append(jnp.where(lane < 64, turned, piece))
            total = total + jnp.concatenate(pieces, axis=0)[:, None, :] * waves[s][None]
        put_early(i, w_at[6], total.reshape(256, 128))
    if gathered:
        for i, src in enumerate((r.g_early, r.g_up, r.g_down)):
            load(src, outs[i], 4 + i).wait()
        outs[3][...] = r.lost[...]
        return

    for k in range(4):
        tail_fold.start(k)
    soon_fold.turn(1)
    for k in range(4):
        tail_fold.chip(k)
    soon_fold.leave(0)
    soon_fold.turn(2)
    soon_fold.leave(1)
    soon_fold.turn(3)
    for k in range(4):
        tail_fold.turn(k)
    soon_fold.leave(2)
    late.end()
    squares = jnp.sum(outs[1][...] * outs[1][...]) + jnp.sum(outs[2][...] * outs[2][...])
    soon_fold.leave(3)
    for k in range(4):
        tail_fold.leave(k)
    soon_fold.end()
    tail_fold.end()
    squares = squares + jnp.sum(outs[0][...] * outs[0][...])
    row = lax.broadcasted_iota(jnp.int32, (8, 128), 0)
    live = (chan * jnp.minimum(pixel_count[0], pixels)).astype(WIDE)
    mine = y * 4 + x * 2 + c
    r.board[mine] = jnp.where(row == 0, squares, jnp.where(row == 1, r.lost[...], live))
    more = []
    for m, device in enumerate(plane_peers):
        more.append(send(r.board.at[mine], r.board.at[mine], r.small, (m,), device))
    for copy in more:
        copy.wait_recv()
    r.board[8 + z] = sum(r.board[m] for m in range(1, 8)) + r.board[0]
    level_copies = [send(r.board.at[8 + z], r.board.at[8 + z], r.small, (7 + d,), along_z[d]) for d in (1, 2, 3)]
    for copy in level_copies:
        copy.wait_recv()
    outs[3][...] = r.board[8] + r.board[9] + r.board[10] + r.board[11]
    late.drain()
    soon_fold.drain()
    tail_fold.drain()
    for copy in more + level_copies:
        copy.wait_send()


def run_net(gathered, levels, node_count, pixel_count, previous, noisy, target, noise, owners, decode_idx, near_idx, send_idx,
            width, hidden, weights):
    nodes, pixels = near_idx.shape[1], owners.shape[1]
    scratch = net_scratch(nodes, send_idx.shape[1] // 2, pixels, width, hidden, noisy.shape[0])
    vmem, smem = pl.BlockSpec(memory_space=pltpu.VMEM), pl.BlockSpec(memory_space=pltpu.SMEM)
    hbm = pl.BlockSpec(memory_space=pl.ANY)
    if gathered:
        results = [(GRID + (width // 32, 5 * width), LOW), (GRID + (width // 32, hidden), LOW), (GRID + (hidden // 32, width), LOW)]
    else:
        results = [((width // 32, 5 * width), WIDE), ((width // 32, hidden), WIDE), ((hidden // 32, width), WIDE)]
    return pl.pallas_call(
        functools.partial(net_kernel, tuple(scratch), gathered),
        out_shape=[jax.ShapeDtypeStruct(shape, kind) for shape, kind in results + [((8, 128), WIDE)]],
        in_specs=[smem] * 3 + [hbm] * 4 + [vmem] * 4 + [hbm if gathered else vmem] * len(weights),
        out_specs=[hbm if gathered else vmem] * 3 + [vmem],
        scratch_shapes=list(scratch.values()),
        compiler_params=pltpu.CompilerParams(
            collective_id=3, has_side_effects=True, vmem_limit_bytes=VMEM_LIMIT),
    )(levels, node_count, pixel_count, previous, noisy, target, noise, owners, decode_idx, near_idx, send_idx, *weights)


def adam_kernel(packed, totals, *refs):
    g_early, g_up, g_down = refs[:3]
    given, made, (loss, count, norm, turned) = refs[-46:-25], refs[-25:-4], refs[-4:]
    loss[...] = totals[1:2, 0:1]
    count[...] = totals[2:3, 0:1]
    norm[...] = jnp.sqrt(totals[0:1, 0:1])
    factor = THRESHOLD / jnp.maximum(jnp.sqrt(totals[0:1, 0:1]), THRESHOLD)
    width = refs[-46 + 6].shape[1]
    at = [0, 3 * width, 4 * width] + [4 * width + HALF_COLS * i for i in range(1, 4)]
    chan = given[0].shape[1] // 2

    def update(i, at_in, g):
        w, m, v = (given[3 * i + j][at_in] for j in range(3))
        clipped = g * factor
        moment = BETA_ONE * m + (1.0 - BETA_ONE) * clipped
        variance = BETA_TWO * v + (1.0 - BETA_TWO) * clipped * clipped
        stepped = (
            moment
            / (1.0 - BETA_ONE**STEP)
            / (jnp.sqrt(variance / (1.0 - BETA_TWO**STEP)) + EPSILON)
        )
        made[3 * i][at_in] = w - LEARN_RATE * (stepped + DECAY_RATE * w)
        made[3 * i + 1][at_in] = moment
        made[3 * i + 2][at_in] = variance

    whole = (slice(None), slice(None))
    both = jnp.concatenate([g_early[:, at[2] : at[2] + chan], g_early[:, at[3] : at[3] + chan]], axis=1)
    update(0, whole, both)
    update(1, whole, g_early[:, : at[1]])
    update(2, whole, g_early[:, at[1] : at[2]])
    update(3, whole, g_up[...])
    update(4, whole, g_down[...])
    for i in range(FOUR // 2 if packed else 0):
        turned[2 * i : 2 * i + 1] = g_early[i : i + 1, at[5] : at[5] + 64]
        turned[2 * i + 1 : 2 * i + 2] = g_early[i : i + 1, at[5] + 64 :]
    update(5, whole, turned[...] if packed else refs[3][...])
    update(6, whole, g_early[:, at[4] : at[4] + chan])


def run_adam(totals, grads, given):
    return pl.pallas_call(
        functools.partial(adam_kernel, len(grads) == 3),
        out_shape=[jax.ShapeDtypeStruct(shape, WIDE) for shape in [a.shape for a in given] + [(1, 1)] * 3],
        in_specs=[pl.BlockSpec(memory_space=pltpu.VMEM)] * (1 + len(grads) + len(given)),
        out_specs=[pl.BlockSpec(memory_space=pltpu.VMEM)] * (len(given) + 3),
        scratch_shapes=[pltpu.VMEM((FOUR, 64), WIDE)],
        compiler_params=pltpu.CompilerParams(vmem_limit_bytes=VMEM_LIMIT),
    )(totals, *grads, *given)


def fill(array, columns):
    return jnp.pad(array, ((0, 0), (0, columns - array.shape[1])))


def on_device(
    previous_state, target_state, noise_draws, noise_level, pixel_owner, mesh_to_grid, neighbours, halo_send,
    node_count, pixel_count, w_encode, w_project, w_output, w_up, w_down, w_noise, w_decode,
    m_encode, m_project, m_output, m_up, m_down, m_noise, m_decode,
    v_encode, v_project, v_output, v_up, v_down, v_noise, v_decode,
):
    width = w_project.shape[1] // 3
    hidden = w_up.shape[1]
    channels = previous_state.shape[1]
    rows = w_project.shape[0]
    small_slice = lax.axis_size("patch") == 8 and lax.axis_size("rep") == 4
    flipped = w_encode.T
    halves = (flipped[:, :channels], flipped[:, channels:])
    if small_slice:
        weights = (w_project, w_output) + halves + (w_decode, w_noise, w_up, w_down)
    else:
        pieces = [w_project, w_output] + [fill(half, HALF_COLS) for half in halves] + [fill(w_decode, HALF_COLS)]
        early = lax.all_gather(jnp.concatenate(pieces, axis=1).astype(LOW), BOTH, axis=0, tiled=True)
        noise = lax.all_gather(w_noise.astype(LOW), BOTH, axis=1, tiled=True).reshape(FOUR, -1, 64)
        early = jnp.concatenate([early, noise.transpose(1, 0, 2).reshape(width, HALF_COLS)], axis=1)
        all_up = lax.all_gather(w_up.astype(LOW), BOTH, axis=0, tiled=True)
        all_down = lax.all_gather(w_down.astype(LOW), BOTH, axis=0, tiled=True)
        weights = [w.reshape(GRID + (-1, w.shape[1])) for w in (early, all_up, all_down)]
    at = [0, 3 * width, 4 * width] + [4 * width + HALF_COLS * i for i in range(1, 4)]

    pixels = pixel_owner.shape[1]
    noisy = target_state[0] + noise_level[0, 0] * noise_draws[0, 0]
    s_early, s_up, s_down, totals = run_net(
        not small_slice, noise_level, node_count[0], pixel_count[0], previous_state[0], noisy, target_state[0], noise_draws[0, 1],
        pixel_owner, mesh_to_grid[0], neighbours[0].T, halo_send, width, hidden, weights,
    )
    masters = (w_encode, w_project, w_output, w_up, w_down, w_noise, w_decode)
    moments = (m_encode, m_project, m_output, m_up, m_down, m_noise, m_decode)
    seconds = (v_encode, v_project, v_output, v_up, v_down, v_noise, v_decode)
    grads = (s_early, s_up, s_down)
    if not small_slice:
        g_early = s_early.reshape(width, -1)
        g_noise = g_early[:, at[5] :].reshape(-1, FOUR, 64).transpose(1, 0, 2).reshape(FOUR, -1)
        parts = (g_early[:, : at[5]], s_up.reshape(width, -1), s_down.reshape(hidden, -1))
        s_early, s_up, s_down = (
            lax.psum_scatter(g.astype(WIDE), BOTH, scatter_dimension=0, tiled=True) for g in parts)
        s_noise = lax.psum_scatter(g_noise.astype(WIDE), BOTH, scatter_dimension=1, tiled=True)
        squares = sum(jnp.sum(shard * shard) for shard in (s_early, s_up, s_down, s_noise))
        count_local = (channels * jnp.minimum(pixel_count[0, 0], pixels)).astype(WIDE)
        sums = lax.psum((squares, totals[0, 0], count_local), BOTH)
        totals = jnp.broadcast_to(jnp.stack(sums + sums[:1] * 5)[:, None], (8, 128))
        grads = (s_early, s_up, s_down, s_noise)
    given = [a for group in zip(masters, moments, seconds) for a in group]
    given[:3] = [a.T for a in given[:3]]
    *made, loss, count, norm = run_adam(totals, grads, given)
    made[:3] = [a.T for a in made[:3]]
    return tuple(made[0::3]) + tuple(made[1::3]) + tuple(made[2::3]) + tuple(a.reshape(()) for a in (loss, count, norm))


def solution(mesh):
    in_specs = (
        P("rep", None, "patch"),
        P("rep", None, "patch"),
        P("rep", None, None, "patch"),
        P("rep", None),
        P("rep", "patch"),
        P("rep", None, "patch"),
        P("rep", "patch", None),
        P("rep", "patch"),
        P("rep", "patch"),
        P("rep", "patch"),
        P(None, ("patch", "rep")),
        P(("patch", "rep"), None),
        P(("patch", "rep"), None),
        P(("patch", "rep"), None),
        P(("patch", "rep"), None),
        P(None, ("patch", "rep")),
        P(("patch", "rep"), None),
        P(None, ("patch", "rep")),
        P(("patch", "rep"), None),
        P(("patch", "rep"), None),
        P(("patch", "rep"), None),
        P(("patch", "rep"), None),
        P(None, ("patch", "rep")),
        P(("patch", "rep"), None),
        P(None, ("patch", "rep")),
        P(("patch", "rep"), None),
        P(("patch", "rep"), None),
        P(("patch", "rep"), None),
        P(("patch", "rep"), None),
        P(None, ("patch", "rep")),
        P(("patch", "rep"), None),
    )
    out_specs = (
        P(None, ("patch", "rep")),
        P(("patch", "rep"), None),
        P(("patch", "rep"), None),
        P(("patch", "rep"), None),
        P(("patch", "rep"), None),
        P(None, ("patch", "rep")),
        P(("patch", "rep"), None),
        P(None, ("patch", "rep")),
        P(("patch", "rep"), None),
        P(("patch", "rep"), None),
        P(("patch", "rep"), None),
        P(("patch", "rep"), None),
        P(None, ("patch", "rep")),
        P(("patch", "rep"), None),
        P(None, ("patch", "rep")),
        P(("patch", "rep"), None),
        P(("patch", "rep"), None),
        P(("patch", "rep"), None),
        P(("patch", "rep"), None),
        P(None, ("patch", "rep")),
        P(("patch", "rep"), None),
        P(),
        P(),
        P(),
    )
    return jax.shard_map(
        on_device, mesh=mesh, in_specs=in_specs, out_specs=out_specs, check_vma=False
    )
```
